32 devices in a mesh: dp: 16 (over z, y, x), tp: 2 (over core).
Axes of the slice: x: 2, y: 2, z: 4, core: 2. Of those that a mesh axis runs over, the one named last changes fastest.
Arguments:
- tokens: bfloat16 [25216, 1024], P(('dp', 'tp')), may hold values from -6 to 6
- masked: int32 [25216], P(('dp', 'tp')), may hold values from 0 to 1, as said below
- cotangent: bfloat16 [25216, 1024], P(('dp', 'tp')), may hold values from -6 to 6
- mask_token: float32 [1024], replicated, may hold values from -6 to 6
- gain_one: float32 [1024], replicated, may hold values from 0.5 to 1.5
- shift_one: float32 [1024], replicated, may hold values from -2 to 2
- w_query: bfloat16 [1024, 1024], P(None, 'tp'), may hold values from -0.1875 to 0.1875
- w_key: bfloat16 [1024, 1024], P(None, 'tp'), may hold values from -0.1875 to 0.1875
- w_value: bfloat16 [1024, 1024], P(None, 'tp'), may hold values from -0.1875 to 0.1875
- b_query: float32 [1024], P('tp'), may hold values from -3 to 3
- b_value: float32 [1024], P('tp'), may hold values from -3 to 3
- w_out: bfloat16 [1024, 1024], P('tp'), may hold values from -1 to 1
- b_out: float32 [1024], replicated, may hold values from -3 to 3
- scale_one: float32 [1024], replicated, may hold values from 0.5 to 1.5
- gain_two: float32 [1024], replicated, may hold values from 0.5 to 1.5
- shift_two: float32 [1024], replicated, may hold values from -2 to 2
- w_up: bfloat16 [1024, 4096], P(None, 'tp'), may hold values from -0.1875 to 0.1875
- b_up: float32 [4096], P('tp'), may hold values from -3 to 3
- w_down: bfloat16 [4096, 1024], P('tp'), may hold values from -0.125 to 0.125
- b_down: float32 [1024], replicated, may hold values from -3 to 3
- scale_two: float32 [1024], replicated, may hold values from 0.5 to 1.5
Outputs:
- block_out: bfloat16 [25216, 1024], P(('dp', 'tp'))
- grad_tokens: float32 [25216, 1024], P(('dp', 'tp'))
- grad_mask_token: float32 [1024], replicated
- grad_gain_one: float32 [1024], replicated
- grad_shift_one: float32 [1024], replicated
- grad_w_query: float32 [1024, 1024], P('dp', 'tp')
- grad_w_key: float32 [1024, 1024], P('dp', 'tp')
- grad_w_value: float32 [1024, 1024], P('dp', 'tp')
- grad_b_query: float32 [1024], P('tp')
- grad_b_value: float32 [1024], P('tp')
- grad_w_out: float32 [1024, 1024], P('tp', 'dp')
- grad_b_out: float32 [1024], replicated
- grad_scale_one: float32 [1024], replicated
- grad_gain_two: float32 [1024], replicated
- grad_shift_two: float32 [1024], replicated
- grad_w_up: float32 [1024, 4096], P('dp', 'tp')
- grad_b_up: float32 [4096], P('tp')
- grad_w_down: float32 [4096, 1024], P('tp', 'dp')
- grad_b_down: float32 [1024], replicated
- grad_scale_two: float32 [1024], replicated
The draws below stay inside these ranges and needn't reach their ends.
Inputs may be any that keep to these rules, and one draw needn't show every extreme that they name: `masked`: in each image of 197 rows the first (class) row is 0; of the other rows, between two fifths (rounded up) and four fifths (rounded down) are 1, a number that varies from image to image.
All inputs are finite; a program needn't handle non-finite values.
Results may differ from the reference program's by a relative error of at most 0.023.
Values may be sent and summed in bfloat16 or wider, within the bound.
No kernel may reach another device: no remote copies, remote signals or barrier semaphores. Data moves between devices by JAX's collectives and lax.ppermute only.
A program may use at most 256 MiB of HBM per device.

```python
import math
import jax
import jax.numpy as jnp
from jax import lax

D = 1024
HEADS = 16
FF = 4096
SEQ = 197
IMG_DEV = 8
HD = 64
IMAGES = 128
ROWS = 25216


def draw_masked(key, part):
    patches = SEQ - 1
    least = (2 * patches + 4) // 5
    most = 4 * patches // 5
    count_key, order_key = jax.random.split(jax.random.fold_in(key, 11))
    counts = jax.random.randint(count_key, (IMAGES, 1), least, most + 1)
    ranking = jax.vmap(lambda one_key: jax.random.permutation(one_key, patches))(jax.random.split(order_key, IMAGES))
    picked = (ranking < counts).astype(jnp.int32)
    leading = jnp.zeros((IMAGES, 1), jnp.int32)
    return jnp.concatenate([leading, picked], axis=1).reshape(IMAGES * SEQ)


def steps_of(key, shape, cuts, smallest, top_value):
    gain, own = 1.0, jax.random.fold_in(key, 6)
    for position, blocks in cuts:
        draws = jnp.exp(jax.random.uniform(jax.random.fold_in(own, position), (blocks,), jnp.float32, smallest / len(cuts), top_value / len(cuts)))
        gain = gain * jnp.repeat(draws, shape[position] // blocks).reshape([-1 if axis == position else 1 for axis in range(len(shape))])
    return gain


def scatter_about(own_key, dims, scale, bound, shards=(), kind=jnp.bfloat16):
    values = scale * jax.random.normal(own_key, dims, jnp.float32)
    if shards:
        values = values * steps_of(own_key, dims, shards, -0.22, 0.18)
    return jnp.clip(values, -bound, bound).astype(kind)


def setup_inputs(seed: int = 0) -> dict:
    streams_of = jax.random.split(jax.random.key(seed), 22)
    tokens = scatter_about(streams_of[0], (ROWS, D), 1.0, 6.0, ((0, 32),))
    masked = draw_masked(jax.random.fold_in(streams_of[21], 71), 0)
    cotangent = scatter_about(streams_of[2], (ROWS, D), 1.0, 6.0, ((0, 32),))
    mask_token = scatter_about(streams_of[3], (D,), 1.0, 6.0, (), jnp.float32)
    gain_one = jnp.clip(1.0 + 0.1 * jax.random.normal(streams_of[4], (D,), jnp.float32), 0.5, 1.5)
    shift_one = scatter_about(streams_of[5], (D,), 0.3, 2.0, (), jnp.float32)
    w_query = scatter_about(streams_of[6], (D, D), D ** -0.5, 0.1875, ((1, 2),))
    w_key = scatter_about(streams_of[7], (D, D), D ** -0.5, 0.1875, ((1, 2),))
    w_value = scatter_about(streams_of[8], (D, D), D ** -0.5, 0.1875, ((1, 2),))
    b_query = scatter_about(streams_of[9], (D,), 0.5, 3.0, ((0, 2),), jnp.float32)
    b_value = scatter_about(streams_of[10], (D,), 0.5, 3.0, ((0, 2),), jnp.float32)
    w_out = scatter_about(streams_of[11], (D, D), (D // 32) ** -0.5, 1.0, ((0, 2),))
    b_out = scatter_about(streams_of[12], (D,), 0.5, 3.0, (), jnp.float32)
    scale_one = jnp.clip(1.0 + 0.1 * jax.random.normal(streams_of[13], (D,), jnp.float32), 0.5, 1.5)
    gain_two = jnp.clip(1.0 + 0.1 * jax.random.normal(streams_of[14], (D,), jnp.float32), 0.5, 1.5)
    shift_two = scatter_about(streams_of[15], (D,), 0.3, 2.0, (), jnp.float32)
    w_up = scatter_about(streams_of[16], (D, FF), D ** -0.5, 0.1875, ((1, 2),))
    b_up = scatter_about(streams_of[17], (FF,), 0.5, 3.0, ((0, 2),), jnp.float32)
    w_down = scatter_about(streams_of[18], (FF, D), (FF // 2) ** -0.5, 0.125, ((0, 2),))
    b_down = scatter_about(streams_of[19], (D,), 0.5, 3.0, (), jnp.float32)
    scale_two = jnp.clip(1.0 + 0.1 * jax.random.normal(streams_of[20], (D,), jnp.float32), 0.5, 1.5)
    return dict(tokens=tokens, masked=masked, cotangent=cotangent, mask_token=mask_token, gain_one=gain_one, shift_one=shift_one, w_query=w_query, w_key=w_key, w_value=w_value, b_query=b_query, b_value=b_value, w_out=w_out, b_out=b_out, scale_one=scale_one, gain_two=gain_two, shift_two=shift_two, w_up=w_up, b_up=b_up, w_down=w_down, b_down=b_down, scale_two=scale_two)


@jax.custom_vjp
def low(v):
    return lax.optimization_barrier(v.astype(jnp.bfloat16)).astype(jnp.float32)

@jax.custom_vjp
def low_back(v):
    return v

def low_keep(v):
    return (low(v), None)

def low_pass(kept, grad):
    return (grad,)

def back_keep(v):
    return (v, None)

def back_low(kept, grad):
    return (low(grad),)
low.defvjp(low_keep, low_pass)
low_back.defvjp(back_keep, back_low)
EPSILON = 1e-06
HIGHER = lax.Precision.HIGHEST

def matmul(left, right):
    return jnp.dot(left, right, precision=HIGHER)

def layer_norm(rows_in, gain_vec, shift_vec):
    center = rows_in - lax.optimization_barrier(jnp.mean(rows_in, axis=-1, keepdims=True))
    spread = lax.optimization_barrier(jnp.mean(center * center, axis=-1, keepdims=True))
    return center * lax.rsqrt(spread + EPSILON) * gain_vec + shift_vec

def forward(tokens, chosen, params):
    mask_token, gain_one, shift_one, w_query, w_key, w_value, b_query, b_value, w_out, b_out, scale_one, gain_two, shift_two, w_up, b_up, w_down, b_down, scale_two = params
    initial = jnp.where(chosen, mask_token[None, :], tokens)
    normed = low(layer_norm(initial, gain_one, shift_one))
    queries = low(low_back(matmul(normed, w_query) + b_query))
    key_rows = low(low_back(matmul(normed, w_key)))
    values = low(low_back(matmul(normed, w_value) + b_value))
    row_count = tokens.shape[0]
    head_shape = (row_count // SEQ, SEQ, HEADS, HD)
    factor = 1.0 / math.sqrt(HD)
    scores = low_back(jnp.einsum('iqhd,ikhd->ihqk', queries.reshape(head_shape), key_rows.reshape(head_shape), precision=HIGHER) * factor)
    probs_low = low(jax.nn.softmax(scores, axis=-1))
    context = jnp.einsum('ihqk,ikhd->iqhd', probs_low, values.reshape(head_shape), precision=HIGHER)
    context = low(low_back(context.reshape(row_count, HEADS * HD)))
    branch = low_back(matmul(context, w_out) + b_out)
    middle = initial + scale_one * branch
    normed_two = low(layer_norm(middle, gain_two, shift_two))
    pre_act = low_back(matmul(normed_two, w_up) + b_up)
    hidden = low(jax.nn.gelu(pre_act, approximate=False))
    output = low_back(matmul(hidden, w_down) + b_down)
    return middle + scale_two * output

def reference(tokens, masked, cotangent, mask_token, gain_one, shift_one, w_query, w_key, w_value, b_query, b_value, w_out, b_out, scale_one, gain_two, shift_two, w_up, b_up, w_down, b_down, scale_two):
    params = tuple((p.astype(jnp.float32) for p in (mask_token, gain_one, shift_one, w_query, w_key, w_value, b_query, b_value, w_out, b_out, scale_one, gain_two, shift_two, w_up, b_up, w_down, b_down, scale_two)))
    group_rows = IMG_DEV * SEQ
    groups = tokens.shape[0] // group_rows
    width = tokens.shape[1]
    token_groups = tokens.astype(jnp.float32).reshape(groups, group_rows, width)
    mask_groups = masked.reshape(groups, group_rows)
    cot_groups = cotangent.astype(jnp.float32).reshape(groups, group_rows, width)

    def one_group(running, item):
        group_tokens, group_mask, group_cot = item
        chosen = (group_mask > 0)[:, None]
        result, pull = jax.vjp(lambda rows_in, weights: forward(rows_in, chosen, weights), group_tokens, params)
        weighting = group_cot * group_mask[:, None].astype(jnp.float32)
        grad_rows, grad_params = pull(weighting)
        running = jax.tree.map(jnp.add, running, grad_params)
        return (running, (result.astype(jnp.bfloat16), grad_rows))
    zeros = jax.tree.map(jnp.zeros_like, params)
    totals, (outputs, grad_rows) = lax.scan(one_group, zeros, (token_groups, mask_groups, cot_groups))
    block_out = outputs.reshape(groups * group_rows, width)
    grad_tokens = grad_rows.reshape(groups * group_rows, width)
    return (block_out, grad_tokens, totals[0], totals[1], totals[2], totals[3], totals[4], totals[5], totals[6], totals[7], totals[8], totals[9], totals[10], totals[11], totals[12], totals[13], totals[14], totals[15], totals[16], totals[17])
```

```python
import functools
import math

import jax
import jax.numpy as jnp
from jax import lax
from jax.experimental import pallas as pl
from jax.experimental.pallas import tpu as pltpu
from jax.sharding import PartitionSpec as P

SEQ = 197
HD = 64
PAIR = 2 * HD
EPSILON = 1e-06
BF16 = jnp.bfloat16
F32 = jnp.float32
MIB = 2**20
LOWEST = -1e30

def layer_norm(rows_in, gain_vec, shift_vec):
    center = rows_in - jnp.mean(rows_in, axis=-1, keepdims=True)
    spread = jnp.mean(center * center, axis=-1, keepdims=True)
    return center * lax.rsqrt(spread + EPSILON) * gain_vec + shift_vec


def norm_backward(rows_in, gain_vec, shift_vec, grad_rows):
    unused, pull = jax.vjp(layer_norm, rows_in, gain_vec, shift_vec)
    return pull(grad_rows)


def gelu_exact(values):
    return jax.nn.gelu(values, approximate=False)


def product(left, right):
    return jnp.dot(left, right, preferred_element_type=jnp.float32)


def times_transposed(left, right):
    return lax.dot_general(
        left, right, (((1,), (1,)), ((), ())), preferred_element_type=jnp.float32
    )


def transposed_times(left, right):
    return lax.dot_general(
        left, right, (((0,), (0,)), ((), ())), preferred_element_type=jnp.float32
    )


def attend_forward(queries, key_rows, values, factor):
    scores = (
        jnp.einsum("iqhd,ikhd->ihqk", queries, key_rows, preferred_element_type=jnp.float32)
        * factor
    )
    row_max = jnp.max(scores, axis=-1, keepdims=True)
    raised = jnp.exp(scores - row_max)
    sum_exp = jnp.sum(raised, axis=-1, keepdims=True)
    probs_low = (raised / sum_exp).astype(jnp.bfloat16)
    context = jnp.einsum("ihqk,ikhd->iqhd", probs_low, values, preferred_element_type=jnp.float32)
    return (context, row_max + jnp.log(sum_exp))


def attend_backward(queries, key_rows, values, log_total, grad_context, factor):
    scores = (
        jnp.einsum("iqhd,ikhd->ihqk", queries, key_rows, preferred_element_type=jnp.float32)
        * factor
    )
    probs = jnp.exp(scores - log_total)
    grad_probs = jnp.einsum(
        "iqhd,ikhd->ihqk", grad_context, values, preferred_element_type=jnp.float32
    )
    inner = jnp.sum(grad_probs * probs, axis=-1, keepdims=True)
    grad_scores = (probs * (grad_probs - inner)).astype(jnp.bfloat16)
    grad_queries = (
        jnp.einsum("ihqk,ikhd->iqhd", grad_scores, key_rows, preferred_element_type=jnp.float32)
        * factor
    )
    grad_keys = (
        jnp.einsum("ihqk,iqhd->ikhd", grad_scores, queries, preferred_element_type=jnp.float32)
        * factor
    )
    grad_values = jnp.einsum(
        "ihqk,iqhd->ikhd",
        probs.astype(jnp.bfloat16),
        grad_context,
        preferred_element_type=jnp.float32,
    )
    return (grad_queries, grad_keys, grad_values)


def gathered_body(
    tokens,
    masked,
    cotangent,
    mask_token,
    gain_one,
    shift_one,
    w_query,
    w_key,
    w_value,
    b_query,
    b_value,
    w_out,
    b_out,
    scale_one,
    gain_two,
    shift_two,
    w_up,
    b_up,
    w_down,
    b_down,
    scale_two,
):
    local_cols = w_query.shape[1]
    local_heads = local_cols // HD
    factor = 1.0 / math.sqrt(HD)
    chosen = (masked > 0)[:, None]
    initial = jnp.where(chosen, mask_token[None, :], tokens.astype(jnp.float32))
    normed = layer_norm(initial, gain_one, shift_one).astype(jnp.bfloat16)
    w_joined = jnp.concatenate([w_query, w_key, w_value], axis=1)
    b_joined = jnp.concatenate([b_query, jnp.zeros_like(b_query), b_value])
    gathered = lax.all_gather(normed, "tp", axis=0, tiled=True)
    joined = (product(gathered, w_joined) + b_joined).astype(jnp.bfloat16)
    group_rows = gathered.shape[0]
    head_shape = (group_rows // SEQ, SEQ, local_heads, HD)
    queries = joined[:, :local_cols].reshape(head_shape)
    key_rows = joined[:, local_cols : 2 * local_cols].reshape(head_shape)
    values = joined[:, 2 * local_cols :].reshape(head_shape)
    context, log_total = attend_forward(queries, key_rows, values, factor)
    context = context.reshape(group_rows, local_cols).astype(jnp.bfloat16)
    branch = (
        lax.psum_scatter(
            product(context, w_out).astype(jnp.bfloat16), "tp", scatter_dimension=0, tiled=True
        ).astype(jnp.float32)
        + b_out
    )
    middle = initial + scale_one * branch
    normed_two = layer_norm(middle, gain_two, shift_two).astype(jnp.bfloat16)
    gathered_two = lax.all_gather(normed_two, "tp", axis=0, tiled=True)
    pre_act = product(gathered_two, w_up) + b_up
    hidden = gelu_exact(pre_act).astype(jnp.bfloat16)
    output = (
        lax.psum_scatter(
            product(hidden, w_down).astype(jnp.bfloat16), "tp", scatter_dimension=0, tiled=True
        ).astype(jnp.float32)
        + b_down
    )
    block_out = (middle + scale_two * output).astype(jnp.bfloat16)
    grad_block = cotangent.astype(jnp.float32) * chosen.astype(jnp.float32)
    grad_output = (scale_two * grad_block).astype(jnp.bfloat16)
    grad_scale_two = jnp.sum(grad_block * output, axis=0)
    grad_b_down = jnp.sum(grad_output.astype(jnp.float32), axis=0)
    portion = lax.all_gather(grad_output, "tp", axis=0, tiled=True)
    grad_hidden = times_transposed(portion, w_down)
    grad_w_down = transposed_times(hidden, portion)
    grad_hidden, grad_w_down = (grad_hidden, grad_w_down)
    unused, gelu_pull = jax.vjp(gelu_exact, pre_act)
    grad_pre = gelu_pull(grad_hidden)[0].astype(jnp.bfloat16)
    grad_b_up = jnp.sum(grad_pre.astype(jnp.float32), axis=0)
    grad_normed_two = lax.psum_scatter(
        times_transposed(grad_pre, w_up).astype(jnp.bfloat16), "tp", scatter_dimension=0, tiled=True
    ).astype(jnp.float32)
    grad_w_up = transposed_times(lax.all_gather(normed_two, "tp", axis=0, tiled=True), grad_pre)
    grad_middle_norm, grad_gain_two, grad_shift_two = norm_backward(
        middle, gain_two, shift_two, grad_normed_two
    )
    grad_middle = grad_block + grad_middle_norm
    grad_branch = (scale_one * grad_middle).astype(jnp.bfloat16)
    grad_scale_one = jnp.sum(grad_middle * branch, axis=0)
    grad_b_out = jnp.sum(grad_branch.astype(jnp.float32), axis=0)
    portion = lax.all_gather(grad_branch, "tp", axis=0, tiled=True)
    grad_context = times_transposed(portion, w_out)
    grad_w_out = transposed_times(context, portion)
    grad_context, grad_w_out = (grad_context, grad_w_out)
    grad_context = grad_context.astype(jnp.bfloat16).reshape(head_shape)
    grad_queries, grad_keys, grad_values = attend_backward(
        queries, key_rows, values, log_total, grad_context, factor
    )
    grad_joined = jnp.concatenate(
        [
            grad_queries.reshape(group_rows, local_cols),
            grad_keys.reshape(group_rows, local_cols),
            grad_values.reshape(group_rows, local_cols),
        ],
        axis=1,
    ).astype(jnp.bfloat16)
    grad_b_query = jnp.sum(grad_joined[:, :local_cols].astype(jnp.float32), axis=0)
    grad_b_value = jnp.sum(grad_joined[:, 2 * local_cols :].astype(jnp.float32), axis=0)
    grad_normed = lax.psum_scatter(
        times_transposed(grad_joined, w_joined).astype(jnp.bfloat16),
        "tp",
        scatter_dimension=0,
        tiled=True,
    ).astype(jnp.float32)
    grad_w_joined = transposed_times(lax.all_gather(normed, "tp", axis=0, tiled=True), grad_joined)
    grad_initial_norm, grad_gain_one, grad_shift_one = norm_backward(
        initial, gain_one, shift_one, grad_normed
    )
    grad_initial = grad_middle + grad_initial_norm
    grad_tokens = jnp.where(chosen, 0.0, grad_initial)
    grad_mask_token = jnp.sum(jnp.where(chosen, grad_initial, 0.0), axis=0)
    (
        grad_mask_token,
        grad_gain_one,
        grad_shift_one,
        grad_b_out,
        grad_scale_one,
        grad_gain_two,
        grad_shift_two,
        grad_b_down,
        grad_scale_two,
    ) = lax.psum(
        (
            grad_mask_token,
            grad_gain_one,
            grad_shift_one,
            grad_b_out,
            grad_scale_one,
            grad_gain_two,
            grad_shift_two,
            grad_b_down,
            grad_scale_two,
        ),
        ("dp", "tp"),
    )
    grad_b_query, grad_b_value, grad_b_up = lax.psum((grad_b_query, grad_b_value, grad_b_up), "dp")
    grad_w_joined, grad_w_out, grad_w_up, grad_w_down = (
        lax.psum_scatter(
            grad_w_joined.astype(jnp.bfloat16), "dp", scatter_dimension=0, tiled=True
        ).astype(jnp.float32),
        lax.psum_scatter(
            grad_w_out.astype(jnp.bfloat16), "dp", scatter_dimension=1, tiled=True
        ).astype(jnp.float32),
        lax.psum_scatter(
            grad_w_up.astype(jnp.bfloat16), "dp", scatter_dimension=0, tiled=True
        ).astype(jnp.float32),
        lax.psum_scatter(
            grad_w_down.astype(jnp.bfloat16), "dp", scatter_dimension=1, tiled=True
        ).astype(jnp.float32),
    )
    grad_w_query = grad_w_joined[:, :local_cols]
    grad_w_key = grad_w_joined[:, local_cols : 2 * local_cols]
    grad_w_value = grad_w_joined[:, 2 * local_cols :]
    return (
        block_out,
        grad_tokens,
        grad_mask_token,
        grad_gain_one,
        grad_shift_one,
        grad_w_query,
        grad_w_key,
        grad_w_value,
        grad_b_query,
        grad_b_value,
        grad_w_out,
        grad_b_out,
        grad_scale_one,
        grad_gain_two,
        grad_shift_two,
        grad_w_up,
        grad_b_up,
        grad_w_down,
        grad_b_down,
        grad_scale_two,
    )


def nn(left, right):
    return lax.dot_general(left, right, (((1,), (0,)), ((), ())), preferred_element_type=F32)


def nt(left, right):
    return lax.dot_general(left, right, (((1,), (1,)), ((), ())), preferred_element_type=F32)


def tn(left, right):
    return lax.dot_general(left, right, (((0,), (0,)), ((), ())), preferred_element_type=F32)


def padded(rows):
    return -(-rows // 32) * 32


def windows(rows):
    found = []
    for image in range(rows // SEQ):
        first = image * SEQ
        start = first // 16 * 16
        found.append((start, -(-(first - start + SEQ) // 16) * 16, first - start))
    return found


def row_blocks(total, size=160):
    return [slice(s, min(s + size, total)) for s in range(0, total, size)]


def inside(shape, axis, offset):
    at = lax.broadcasted_iota(jnp.int32, shape, axis)
    return (at >= offset) & (at < offset + SEQ)


def col_sum(values):
    return jnp.sum(values, axis=0, keepdims=True)


def row_mean(values):
    return jnp.mean(values, axis=-1, keepdims=True)


def moments(rows_in):
    center = rows_in - row_mean(rows_in)
    return center, lax.rsqrt(row_mean(center * center) + EPSILON)


def norm_pull(rows_in, gain, grad):
    center, inv = moments(rows_in)
    hat = center * inv
    scaled = grad * gain
    back = (scaled - row_mean(scaled) - hat * row_mean(scaled * hat)) * inv
    return back, col_sum(grad * hat), col_sum(grad)


def gelu_parts(v):
    size = jnp.abs(v)
    t = 1.0 / (1.0 + (0.3275911 * 0.7071067811865476) * size)
    e = jnp.exp(-0.5 * v * v)
    tail = (
        t
        * (
            0.5 * 0.254829592
            + t
            * (
                0.5 * -0.284496736
                + t * (0.5 * 1.421413741 + t * (0.5 * -1.453152027 + t * (0.5 * 1.061405429)))
            )
        )
        * e
    )
    return jnp.where(v < 0, tail, 1.0 - tail), v * e * 0.3989422804014327


def attend(rows, q_ref, k_ref, v_ref, ctx_ref):
    ctx_ref[padded(rows) - 32 :, :] = jnp.zeros((32, ctx_ref.shape[1]), BF16)

    def one_pair(pair, carry):
        lanes = pl.ds(pl.multiple_of(pair * PAIR, PAIR), PAIR)
        for start, size, offset in windows(rows):
            win = slice(start, start + size)
            q, k, v = q_ref[win, lanes], k_ref[win, lanes], v_ref[win, lanes]
            low_half = lax.broadcasted_iota(jnp.int32, (size, PAIR), 1) < HD
            here = inside((size, size), 1, offset)
            total = None
            for mine in (low_half, ~low_half):
                zero = jnp.zeros_like(k)
                scores = jnp.where(here, nt(q, jnp.where(mine, k, zero)), LOWEST)
                raised = jnp.exp(scores - jnp.max(scores, axis=-1, keepdims=True))
                share = 1.0 / jnp.sum(raised, axis=-1, keepdims=True)
                part = nn((raised * share).astype(BF16), jnp.where(mine, v, zero))
                total = part if total is None else total + part
            keep = inside((size, PAIR), 0, offset)
            ctx_ref[win, lanes] = jnp.where(keep, total.astype(BF16), ctx_ref[win, lanes])
        return carry

    lax.fori_loop(0, q_ref.shape[1] // PAIR, one_pair, 0)


def project(normed_ref, wq_ref, wk_ref, wv_ref, bq_ref, bv_ref, q_ref, k_ref, v_ref):
    normed = normed_ref[...]
    q_ref[...] = (nn(normed, wq_ref[...]) + bq_ref[...]).astype(BF16) * BF16(1.0 / math.sqrt(HD))
    k_ref[...] = nn(normed, wk_ref[...]).astype(BF16)
    v_ref[...] = (nn(normed, wv_ref[...]) + bv_ref[...]).astype(BF16)


def first_kernel(
    rows, tok_ref, mask_ref, mt_ref, gain_ref, shift_ref, wq_ref, wk_ref, wv_ref, bq_ref, bv_ref,
    normed_ref, q_ref, k_ref, v_ref, ctx_ref,
):
    for block in row_blocks(rows):
        initial = jnp.where(mask_ref[block] > 0, mt_ref[...], tok_ref[block].astype(F32))
        center, inv = moments(initial)
        normed_ref[block] = (center * inv * gain_ref[...] + shift_ref[...]).astype(BF16)
    over = padded(rows) - rows
    normed_ref[rows:] = jnp.zeros((over, normed_ref.shape[1]), BF16)
    project(normed_ref, wq_ref, wk_ref, wv_ref, bq_ref, bv_ref, q_ref, k_ref, v_ref)
    attend(rows, q_ref, k_ref, v_ref, ctx_ref)


def second_kernel(
    rows, normed_ref, wq_ref, wk_ref, wv_ref, bq_ref, bv_ref, ctx_ref, wo_ref, wo2_ref, bo_ref,
    s1_ref, gain_ref, shift_ref, tok_ref, mask_ref, mt_ref, cot_ref, s2_ref,
    q_ref, k_ref, v_ref, ctx2_ref, middle_ref, normed2_ref, go_ref, sums_ref,
):
    project(normed_ref, wq_ref, wk_ref, wv_ref, bq_ref, bv_ref, q_ref, k_ref, v_ref)
    attend(rows, q_ref, k_ref, v_ref, ctx2_ref)
    over = padded(rows) - rows
    width = middle_ref.shape[1]
    total = jnp.zeros((1, width), F32)
    for block in row_blocks(rows):
        branch = nn(ctx_ref[block], wo_ref[...]) + nn(ctx2_ref[block], wo2_ref[...]) + bo_ref[...]
        masked = mask_ref[block] > 0
        initial = jnp.where(masked, mt_ref[...], tok_ref[block].astype(F32))
        middle = initial + s1_ref[...] * branch
        middle_ref[block] = middle
        center, inv = moments(middle)
        normed2_ref[block] = (center * inv * gain_ref[...] + shift_ref[...]).astype(BF16)
        grad_out = (jnp.where(masked, cot_ref[block].astype(F32), 0.0) * s2_ref[...]).astype(BF16)
        go_ref[block] = grad_out
        total += col_sum(grad_out.astype(F32))
    sums_ref[...] = total
    normed2_ref[rows:] = jnp.zeros((over, width), BF16)
    go_ref[rows:] = jnp.zeros((over, width), BF16)


def feed_kernel(
    me_ref, n2_ref, go_ref, wu_ref, wd_ref, bu_ref, hidden_ref, gp_ref, gwd_ref, gwu_ref, gb_ref
):
    pre = nn(n2_ref[...], wu_ref[...]) + bu_ref[...]
    grad_hidden = nt(go_ref[...], wd_ref[...])
    cdf, slope = gelu_parts(pre)
    hidden = (pre * cdf).astype(BF16)
    grad_pre = (grad_hidden * (cdf + slope)).astype(BF16)
    hidden_ref[...] = hidden
    gp_ref[...] = grad_pre
    gb_ref[...] = col_sum(grad_pre.astype(F32))
    store_blocks(me_ref[0], tn(go_ref[...], hidden), gwd_ref, 0)
    store_blocks(me_ref[0], tn(n2_ref[...], grad_pre), gwu_ref, 0)


def store_blocks(me, product_rows, out_ref, at):
    parts, size, _ = out_ref.shape
    cols = product_rows.shape[1]
    for b in range(parts):
        out_ref[b ^ me, :, at : at + cols] = product_rows[b * size : (b + 1) * size].astype(BF16)


def middle_kernel(
    rows, count, *refs
):
    gps, wus = refs[:count], refs[count : 2 * count]
    (middle_ref, tok_ref, mask_ref, mt_ref, cot_ref, gain_ref, s1_ref) = refs[2 * count : 2 * count + 7]
    gm_ref, gbr_ref, sums_ref, acc_ref = refs[2 * count + 7 :]
    step = pl.program_id(0)
    part = None
    for gp_ref, wu_ref in zip(gps, wus):
        one = nt(gp_ref[...], wu_ref[...])
        part = one if part is None else part + one

    @pl.when(step == 0)
    def first():
        acc_ref[...] = part

    @pl.when(step > 0)
    def later():
        acc_ref[...] += part

    @pl.when(step == pl.num_programs(0) - 1)
    def last():
        width = gm_ref.shape[1]
        sums = [jnp.zeros((1, width), F32)] * 4
        for block in row_blocks(rows):
            masked = mask_ref[block] > 0
            middle = middle_ref[block]
            back, grad_gain, grad_shift = norm_pull(middle, gain_ref[...], acc_ref[block])
            grad_middle = jnp.where(masked, cot_ref[block].astype(F32), 0.0) + back
            gm_ref[block] = grad_middle
            grad_branch = (s1_ref[...] * grad_middle).astype(BF16)
            gbr_ref[block] = grad_branch
            initial = jnp.where(masked, mt_ref[...], tok_ref[block].astype(F32))
            new = (
                grad_gain,
                grad_shift,
                col_sum(grad_middle * (middle - initial)) / s1_ref[...],
                col_sum(grad_branch.astype(F32)),
            )
            sums = [a + b for a, b in zip(sums, new)]
        for i, one in enumerate(sums):
            sums_ref[i : i + 1] = one
        over = padded(rows) - rows
        gbr_ref[rows:] = jnp.zeros((over, width), BF16)


def back_kernel(
    rows, me_ref, gbr_ref, wo_ref, ctx_ref, q_ref, k_ref, v_ref, n1_ref,
    dq_ref, dk_ref, dv_ref, grads_ref, sums_ref, gc_ref,
):
    me = me_ref[0]
    cols = q_ref.shape[1]
    gc_ref[...] = nt(gbr_ref[...], wo_ref[...]).astype(BF16)
    factor = 1.0 / math.sqrt(HD)
    for ref in (dq_ref, dk_ref, dv_ref):
        ref[padded(rows) - 32 :, :] = jnp.zeros((32, cols), BF16)

    def one_pair(pair, carry):
        lanes = pl.ds(pl.multiple_of(pair * PAIR, PAIR), PAIR)
        for start, size, offset in windows(rows):
            win = slice(start, start + size)
            q, k, v = q_ref[win, lanes], k_ref[win, lanes], v_ref[win, lanes]
            keep = inside((size, PAIR), 0, offset)
            gc = jnp.where(keep, gc_ref[win, lanes], jnp.zeros((size, PAIR), BF16))
            low_half = lax.broadcasted_iota(jnp.int32, (size, PAIR), 1) < HD
            here = inside((size, size), 0, offset)
            got = []
            for mine in (low_half, ~low_half):
                zero = jnp.zeros_like(k)
                k_one = jnp.where(mine, k, zero)
                scores = jnp.where(here, nt(k_one, q), LOWEST)
                raised = jnp.exp(scores - jnp.max(scores, axis=0, keepdims=True))
                probs = raised * (1.0 / jnp.sum(raised, axis=0, keepdims=True))
                grad_probs = nt(jnp.where(mine, v, zero), gc)
                inner = jnp.sum(grad_probs * probs, axis=0, keepdims=True)
                grad_scores = (probs * (grad_probs - inner)).astype(BF16)
                got.append((tn(grad_scores, k_one), nn(grad_scores, q), nn(probs.astype(BF16), gc)))
            low, high = got
            for ref, new in (
                (dq_ref, (low[0] + high[0]) * factor),
                (dk_ref, jnp.where(low_half, low[1], high[1])),
                (dv_ref, jnp.where(low_half, low[2], high[2])),
            ):
                ref[win, lanes] = jnp.where(keep, new.astype(BF16), ref[win, lanes])
        return carry

    lax.fori_loop(0, cols // PAIR, one_pair, 0)
    for i, ref in enumerate((dq_ref, dk_ref, dv_ref)):
        store_blocks(me, tn(n1_ref[...], ref[...]), grads_ref, i * cols)
        if i != 1:
            sums_ref[i // 2 : i // 2 + 1] = col_sum(ref[...].astype(F32))
    store_blocks(me, tn(gbr_ref[...], ctx_ref[...]), grads_ref, 3 * cols)


def input_kernel(
    rows, *refs
):
    grads, weights = refs[:6], refs[6:12]
    tok_ref, mask_ref, mt_ref, gain_ref, gm_ref, out_ref, sums_ref = refs[12:]
    width = out_ref.shape[1]
    sums = [jnp.zeros((1, width), F32)] * 3
    for block in row_blocks(rows):
        grad_normed = None
        for grad_ref, w_ref in zip(grads, weights):
            one = nt(grad_ref[block], w_ref[...])
            grad_normed = one if grad_normed is None else grad_normed + one
        masked = mask_ref[block] > 0
        initial = jnp.where(masked, mt_ref[...], tok_ref[block].astype(F32))
        back, grad_gain, grad_shift = norm_pull(initial, gain_ref[...], grad_normed)
        grad_initial = gm_ref[block] + back
        out_ref[block] = jnp.where(masked, 0.0, grad_initial)
        new = (col_sum(jnp.where(masked, grad_initial, 0.0)), grad_gain, grad_shift)
        sums = [a + b for a, b in zip(sums, new)]
    for i, one in enumerate(sums):
        sums_ref[i : i + 1] = one


def output_kernel(
    rows, count, *refs
):
    hiddens, wds = refs[:count], refs[count : 2 * count]
    middle_ref, mask_ref, cot_ref, bd_ref, s2_ref = refs[2 * count : 2 * count + 5]
    out_ref, sums_ref, acc_ref = refs[2 * count + 5 :]
    step = pl.program_id(0)
    part = None
    for hidden_ref, wd_ref in zip(hiddens, wds):
        one = nn(hidden_ref[...], wd_ref[...])
        part = one if part is None else part + one

    @pl.when(step == 0)
    def first():
        acc_ref[...] = part

    @pl.when(step > 0)
    def later():
        acc_ref[...] += part

    @pl.when(step == pl.num_programs(0) - 1)
    def last():
        total = jnp.zeros((1, out_ref.shape[1]), F32)
        for block in row_blocks(rows):
            output = acc_ref[block] + bd_ref[...]
            out_ref[block] = (middle_ref[block] + s2_ref[...] * output).astype(BF16)
            grad_block = jnp.where(mask_ref[block] > 0, cot_ref[block].astype(F32), 0.0)
            total += col_sum(grad_block * output)
        sums_ref[...] = total


def shape_of(shape, dtype=BF16):
    return jax.ShapeDtypeStruct(shape, dtype)


def cost(flops, *arrays):
    moved = sum(a.size * a.dtype.itemsize for a in arrays)
    return pl.CostEstimate(flops=flops, bytes_accessed=moved, transcendentals=0)


def whole_call(kernel, outs, args, flops, scratch=(), name=None, scalars=0):
    vmem = pl.BlockSpec(memory_space=pltpu.VMEM)
    smem = pl.BlockSpec(memory_space=pltpu.SMEM)
    return pl.pallas_call(
        kernel,
        in_specs=[smem] * scalars + [vmem] * (len(args) - scalars),
        out_specs=[vmem] * len(outs),
        out_shape=outs,
        scratch_shapes=list(scratch),
        compiler_params=pltpu.CompilerParams(vmem_limit_bytes=56 * MIB),
        cost_estimate=cost(flops, *args, *outs),
        name=name,
    )(*args)


def feed(me, n2, go, w_up, w_down, b_up, first, count, chunk, n):
    tall, width = n2.shape
    cols = count * chunk
    outs = [
        shape_of((tall, cols)),
        shape_of((tall, cols)),
        shape_of((n, width // n, cols)),
        shape_of((n, width // n, cols)),
        shape_of((1, cols), F32),
    ]

    def all_of(array):
        return pl.BlockSpec(array.shape, lambda c, me: (0, 0))

    def along(size, base):
        return pl.BlockSpec((size, chunk), lambda c, me: (0, c + base))

    blocks = pl.BlockSpec((n, width // n, chunk), lambda c, me: (0, 0, c))
    return pl.pallas_call(
        feed_kernel,
        grid_spec=pltpu.PrefetchScalarGridSpec(
            num_scalar_prefetch=1,
            grid=(count,),
            in_specs=[
                all_of(n2),
                all_of(go),
                along(width, first),
                pl.BlockSpec((chunk, width), lambda c, me: (c + first, 0)),
                along(1, first),
            ],
            out_specs=[along(tall, 0), along(tall, 0), blocks, blocks, along(1, 0)],
        ),
        out_shape=outs,
        compiler_params=pltpu.CompilerParams(vmem_limit_bytes=56 * MIB),
        cost_estimate=cost(8 * tall * width * cols, n2, go, *outs),
        name="feed",
    )(me, n2, go, w_up, w_down, b_up)


def summed(kernel, lefts, rights, picks, rights_axis, others, outs, steps, chunk, name):
    tall = lefts[0].shape[0]
    width = rights[0].shape[1 - rights_axis]
    specs = [pl.BlockSpec((tall, chunk), lambda c: (0, c)) for _ in lefts]
    for base in picks:
        if rights_axis:
            specs.append(pl.BlockSpec((width, chunk), lambda c, base=base: (0, c + base)))
        else:
            specs.append(pl.BlockSpec((chunk, width), lambda c, base=base: (c + base, 0)))
    specs += [pl.BlockSpec(a.shape, lambda c: (0, 0)) for a in others]
    return pl.pallas_call(
        kernel,
        grid=(steps,),
        in_specs=specs,
        out_specs=[pl.BlockSpec(o.shape, lambda c: (0, 0)) for o in outs],
        out_shape=outs,
        scratch_shapes=[pltpu.VMEM((tall, width), F32)],
        compiler_params=pltpu.CompilerParams(vmem_limit_bytes=56 * MIB),
        cost_estimate=cost(2 * tall * width * chunk * steps * len(lefts), *lefts, *others, *outs),
        name=name,
    )(*lefts, *rights, *others)


def pairs(n, bit):
    return [(i, i ^ (1 << bit)) for i in range(n)]


class Scatter:
    def __init__(self, sources, order):
        self.n, self.rows, self.cols = sources[0].shape
        self.order = order
        self.left = list(range(self.n.bit_length() - 1))[::-1]
        dims = (2,) * len(self.left) + (self.rows, self.cols)
        self.sources = [s.reshape(dims) for s in sources]

    def total(self, bit, side):
        at = self.left.index(bit)
        parts = [lax.index_in_dim(s, side, at, keepdims=False) for s in self.sources]
        return parts

    def hop(self, j):
        bit = self.order[j]
        send = functools.reduce(jnp.add, [p.astype(F32) for p in self.total(bit, 1)]).astype(BF16)
        got = lax.ppermute(send, "dp", pairs(self.n, bit))
        self.sources = self.total(bit, 0) + [got]
        self.left.remove(bit)

    def result(self):
        return functools.reduce(jnp.add, [s.astype(F32) for s in self.sources])


def swap(array):
    return lax.ppermute(array, "tp", [(0, 1), (1, 0)])


def local_body(
    tokens, masked, cotangent, mask_token, gain_one, shift_one, w_query, w_key, w_value, b_query,
    b_value, w_out, b_out, scale_one, gain_two, shift_two, w_up, b_up, w_down, b_down, scale_two,
):
    rows, width = tokens.shape
    tall = padded(rows)
    half = w_query.shape[1]
    units = w_up.shape[1]
    n = lax.axis_size("dp")
    bits = n.bit_length() - 1
    me = lax.axis_index("dp").astype(jnp.int32).reshape(1)
    biases = jnp.concatenate([b_query, b_value, b_up]).reshape(-1, 128)

    wq2, wk2, wv2 = swap(w_query), swap(w_key), swap(w_value)
    biases2 = swap(biases).reshape(-1)
    wo2 = swap(w_out)
    wu2, wd2 = swap(w_up), swap(w_down)
    row = lambda v: v.reshape(1, -1)
    bq2, bv2, bu2 = row(biases2[:half]), row(biases2[half : 2 * half]), row(biases2[2 * half :])
    bq, bv, bu = row(b_query), row(b_value), row(b_up)
    mt, g1, s1, bo, sc1 = row(mask_token), row(gain_one), row(shift_one), row(b_out), row(scale_one)
    g2, s2, bd, sc2 = row(gain_two), row(shift_two), row(b_down), row(scale_two)
    mask = masked.reshape(rows, 1)

    narrow = shape_of((tall, half))
    wide = shape_of((tall, width))
    attend_flops = 2 * 2 * 256 * SEQ * rows * half // HD
    normed, q, k, v, ctx = whole_call(
        functools.partial(first_kernel, rows),
        [wide, narrow, narrow, narrow, narrow],
        (tokens, mask, mt, g1, s1, w_query, w_key, w_value, bq, bv),
        6 * rows * width * half + attend_flops,
        name="first",
    )
    q2, k2, v2, ctx2, middle, normed2, go, sum_go = whole_call(
        functools.partial(second_kernel, rows),
        [narrow, narrow, narrow, narrow, shape_of((rows, width), F32), wide, wide, shape_of((1, width), F32)],
        (normed, wq2, wk2, wv2, bq2, bv2, ctx, w_out, wo2, bo, sc1, g2, s2, tokens, mask, mt, cotangent, sc2),
        10 * rows * width * half + attend_flops,
        name="second",
    )

    chunk = min(512, units)
    steps = units // chunk
    cuts = 2 if steps % 2 == 0 else 1
    per = steps // cuts
    hiddens, gps, firsts, grads, sums_up, sums_up2 = [], [], [], [], [], []
    for cut in range(cuts):
        his = feed(me, normed2, go, wu2, wd2, bu2, cut * per, per, chunk, n)
        theirs = (swap(his[2]), swap(his[3]))
        own = feed(me, normed2, go, w_up, w_down, bu, cut * per, per, chunk, n)
        grads.append(((own[2], theirs[0]), (own[3], theirs[1])))
        hiddens += [his[0], own[0]]
        gps += [his[1], own[1]]
        sums_up2.append(his[4])
        sums_up.append(own[4])
        firsts += [cut * per] * 2
    ups, downs = [wu2, w_up] * cuts, [wd2, w_down] * cuts

    gm, gbr, sums_two = summed(
        functools.partial(middle_kernel, rows, len(gps)),
        gps, ups, firsts, 1,
        (middle, tokens, mask, mt, cotangent, g2, sc1),
        [shape_of((rows, width), F32), wide, shape_of((4, width), F32)],
        per, chunk, "middle",
    )

    def back(wo, ctx, q, k, v):
        return pl_back(rows, me, gbr, wo, ctx, q, k, v, normed, n, attend_flops)

    dq2, dk2, dv2, gw2, sums_b2 = back(wo2, ctx2, q2, k2, v2)
    gw2 = swap(gw2)
    dq, dk, dv, gw, sums_b = back(w_out, ctx, q, k, v)

    grad_tokens, sums_one = whole_call(
        functools.partial(input_kernel, rows),
        [shape_of((rows, width), F32), shape_of((3, width), F32)],
        (dq, dk, dv, dq2, dk2, dv2, w_query, w_key, w_value, wq2, wk2, wv2, tokens, mask, mt, g1, gm),
        12 * rows * width * half,
        name="input",
    )
    block_out, sum_two = summed(
        functools.partial(output_kernel, rows, len(hiddens)),
        hiddens, downs, firsts, 0,
        (middle, mask, cotangent, bd, sc2),
        [shape_of((rows, width)), shape_of((1, width), F32)],
        per, chunk, "output",
    )

    natural = tuple(range(bits))
    orders = [natural[i:] + natural[:i] for i in range(bits)]
    by_x, by_z = orders[0], orders[2 % bits]
    by_y = natural[1:2] + natural[0:1] + natural[2:]
    done = {}

    def part(sources, low, high):
        return [s[:, :, low:high] for s in sources]

    groups = []
    for cut, (down, up) in enumerate(grads):
        cols = down[0].shape[2]
        at = cols * 3 // 4
        groups.append([
            (("down", cut, 0), Scatter(part(down, 0, at), by_x)),
            (("up", cut, 0), Scatter(part(up, 0, at), by_y)),
            (("rest", cut, 0), Scatter([jnp.concatenate([d[:, :, at:], u[:, :, at:]], axis=2) for d, u in zip(down, up)], by_z)),
        ])
    cols = gw.shape[2]
    lows = [0, cols * 3 // 8, cols * 3 // 4, cols]
    groups.append([
        (("attention", 0, i), Scatter(part((gw, gw2), lows[i], lows[i + 1]), (by_x, by_y, by_z)[i])) for i in range(3)
    ])
    for group in groups:
        for j in range(bits):
            for _, one in group:
                one.hop(j)
        for name, one in group:
            done[name] = one.result()
    downs_, ups_ = [], []
    for cut in range(cuts):
        rest = done["rest", cut, 0]
        mid = rest.shape[1] // 2
        downs_ += [done["down", cut, 0], rest[:, :mid]]
        ups_ += [done["up", cut, 0], rest[:, mid:]]
    grad_w_down = jnp.concatenate(downs_, axis=1).T
    grad_w_up = jnp.concatenate(ups_, axis=1)
    attention = jnp.concatenate([done["attention", 0, i] for i in range(3)], axis=1)

    same = jnp.concatenate([sums_one.reshape(-1), sums_two.reshape(-1), sum_go.reshape(-1), sum_two.reshape(-1)])
    own_sums = jnp.concatenate([sums_b.reshape(-1)] + [s.reshape(-1) for s in sums_up])
    other_sums = jnp.concatenate([sums_b2.reshape(-1)] + [s.reshape(-1) for s in sums_up2])
    vector = jnp.concatenate([same, own_sums]).reshape(-1, 128)
    vector += swap(jnp.concatenate([same, other_sums]).reshape(-1, 128))
    for bit in range(bits):
        vector += lax.ppermute(vector, "dp", pairs(n, bit))
    vector = vector.reshape(-1)
    rep = [vector[i * width : (i + 1) * width] for i in range(9)]
    (grad_mask_token, grad_gain_one, grad_shift_one, grad_gain_two, grad_shift_two, grad_scale_one,
     grad_b_out, grad_b_down, grad_scale_two) = rep
    own = vector[9 * width :]
    return (
        block_out,
        grad_tokens,
        grad_mask_token,
        grad_gain_one,
        grad_shift_one,
        attention[:, :half],
        attention[:, half : 2 * half],
        attention[:, 2 * half : 3 * half],
        own[:half],
        own[half : 2 * half],
        attention[:, 3 * half :].T,
        grad_b_out,
        grad_scale_one,
        grad_gain_two,
        grad_shift_two,
        grad_w_up,
        own[2 * half :],
        grad_w_down,
        grad_b_down,
        grad_scale_two,
    )


def pl_back(rows, me, gbr, wo, ctx, q, k, v, normed, n, attend_flops):
    tall, cols = q.shape
    width = gbr.shape[1]
    narrow = shape_of((tall, cols))
    return whole_call(
        functools.partial(back_kernel, rows),
        [narrow, narrow, narrow, shape_of((n, width // n, 4 * cols)), shape_of((2, cols), F32)],
        (me, gbr, wo, ctx, q, k, v, normed),
        10 * rows * width * cols + 3 * attend_flops,
        scratch=[pltpu.VMEM((tall, cols), BF16)],
        name="back",
        scalars=1,
    )


def solution(mesh):
    placed = (
        P(("dp", "tp"), None),
        P(("dp", "tp")),
        P(("dp", "tp"), None),
        P(),
        P(),
        P(),
        P(None, "tp"),
        P(None, "tp"),
        P(None, "tp"),
        P("tp"),
        P("tp"),
        P("tp", None),
        P(),
        P(),
        P(),
        P(),
        P(None, "tp"),
        P("tp"),
        P("tp", None),
        P(),
        P(),
    )
    fits = mesh.shape["tp"] == 2 and mesh.shape["dp"].bit_count() == 1
    return jax.shard_map(
        local_body if fits else gathered_body,
        mesh=mesh,
        in_specs=placed,
        out_specs=(
            P(("dp", "tp"), None),
            P(("dp", "tp"), None),
            P(),
            P(),
            P(),
            P("dp", "tp"),
            P("dp", "tp"),
            P("dp", "tp"),
            P("tp"),
            P("tp"),
            P("tp", "dp"),
            P(),
            P(),
            P(),
            P(),
            P("dp", "tp"),
            P("tp"),
            P("tp", "dp"),
            P(),
            P(),
        ),
        check_vma=False,
    )
```

```python
import functools
import math

import jax
import jax.numpy as jnp
from jax import lax
from jax.experimental import pallas as pl
from jax.experimental.pallas import tpu as pltpu
from jax.sharding import PartitionSpec as P

SEQ = 197
HD = 64
PAIR = 2 * HD
EPSILON = 1e-06
BF16 = jnp.bfloat16
F32 = jnp.float32
MIB = 2**20
LOWEST = -1e30

def layer_norm(rows_in, gain_vec, shift_vec):
    center = rows_in - jnp.mean(rows_in, axis=-1, keepdims=True)
    spread = jnp.mean(center * center, axis=-1, keepdims=True)
    return center * lax.rsqrt(spread + EPSILON) * gain_vec + shift_vec


def norm_backward(rows_in, gain_vec, shift_vec, grad_rows):
    unused, pull = jax.vjp(layer_norm, rows_in, gain_vec, shift_vec)
    return pull(grad_rows)


def gelu_exact(values):
    return jax.nn.gelu(values, approximate=False)


def product(left, right):
    return jnp.dot(left, right, preferred_element_type=jnp.float32)


def times_transposed(left, right):
    return lax.dot_general(
        left, right, (((1,), (1,)), ((), ())), preferred_element_type=jnp.float32
    )


def transposed_times(left, right):
    return lax.dot_general(
        left, right, (((0,), (0,)), ((), ())), preferred_element_type=jnp.float32
    )


def attend_forward(queries, key_rows, values, factor):
    scores = (
        jnp.einsum("iqhd,ikhd->ihqk", queries, key_rows, preferred_element_type=jnp.float32)
        * factor
    )
    row_max = jnp.max(scores, axis=-1, keepdims=True)
    raised = jnp.exp(scores - row_max)
    sum_exp = jnp.sum(raised, axis=-1, keepdims=True)
    probs_low = (raised / sum_exp).astype(jnp.bfloat16)
    context = jnp.einsum("ihqk,ikhd->iqhd", probs_low, values, preferred_element_type=jnp.float32)
    return (context, row_max + jnp.log(sum_exp))


def attend_backward(queries, key_rows, values, log_total, grad_context, factor):
    scores = (
        jnp.einsum("iqhd,ikhd->ihqk", queries, key_rows, preferred_element_type=jnp.float32)
        * factor
    )
    probs = jnp.exp(scores - log_total)
    grad_probs = jnp.einsum(
        "iqhd,ikhd->ihqk", grad_context, values, preferred_element_type=jnp.float32
    )
    inner = jnp.sum(grad_probs * probs, axis=-1, keepdims=True)
    grad_scores = (probs * (grad_probs - inner)).astype(jnp.bfloat16)
    grad_queries = (
        jnp.einsum("ihqk,ikhd->iqhd", grad_scores, key_rows, preferred_element_type=jnp.float32)
        * factor
    )
    grad_keys = (
        jnp.einsum("ihqk,iqhd->ikhd", grad_scores, queries, preferred_element_type=jnp.float32)
        * factor
    )
    grad_values = jnp.einsum(
        "ihqk,iqhd->ikhd",
        probs.astype(jnp.bfloat16),
        grad_context,
        preferred_element_type=jnp.float32,
    )
    return (grad_queries, grad_keys, grad_values)


def gathered_body(
    tokens,
    masked,
    cotangent,
    mask_token,
    gain_one,
    shift_one,
    w_query,
    w_key,
    w_value,
    b_query,
    b_value,
    w_out,
    b_out,
    scale_one,
    gain_two,
    shift_two,
    w_up,
    b_up,
    w_down,
    b_down,
    scale_two,
):
    local_cols = w_query.shape[1]
    local_heads = local_cols // HD
    factor = 1.0 / math.sqrt(HD)
    chosen = (masked > 0)[:, None]
    initial = jnp.where(chosen, mask_token[None, :], tokens.astype(jnp.float32))
    normed = layer_norm(initial, gain_one, shift_one).astype(jnp.bfloat16)
    w_joined = jnp.concatenate([w_query, w_key, w_value], axis=1)
    b_joined = jnp.concatenate([b_query, jnp.zeros_like(b_query), b_value])
    gathered = lax.all_gather(normed, "tp", axis=0, tiled=True)
    joined = (product(gathered, w_joined) + b_joined).astype(jnp.bfloat16)
    group_rows = gathered.shape[0]
    head_shape = (group_rows // SEQ, SEQ, local_heads, HD)
    queries = joined[:, :local_cols].reshape(head_shape)
    key_rows = joined[:, local_cols : 2 * local_cols].reshape(head_shape)
    values = joined[:, 2 * local_cols :].reshape(head_shape)
    context, log_total = attend_forward(queries, key_rows, values, factor)
    context = context.reshape(group_rows, local_cols).astype(jnp.bfloat16)
    branch = (
        lax.psum_scatter(
            product(context, w_out).astype(jnp.bfloat16), "tp", scatter_dimension=0, tiled=True
        ).astype(jnp.float32)
        + b_out
    )
    middle = initial + scale_one * branch
    normed_two = layer_norm(middle, gain_two, shift_two).astype(jnp.bfloat16)
    gathered_two = lax.all_gather(normed_two, "tp", axis=0, tiled=True)
    pre_act = product(gathered_two, w_up) + b_up
    hidden = gelu_exact(pre_act).astype(jnp.bfloat16)
    output = (
        lax.psum_scatter(
            product(hidden, w_down).astype(jnp.bfloat16), "tp", scatter_dimension=0, tiled=True
        ).astype(jnp.float32)
        + b_down
    )
    block_out = (middle + scale_two * output).astype(jnp.bfloat16)
    grad_block = cotangent.astype(jnp.float32) * chosen.astype(jnp.float32)
    grad_output = (scale_two * grad_block).astype(jnp.bfloat16)
    grad_scale_two = jnp.sum(grad_block * output, axis=0)
    grad_b_down = jnp.sum(grad_output.astype(jnp.float32), axis=0)
    portion = lax.all_gather(grad_output, "tp", axis=0, tiled=True)
    grad_hidden = times_transposed(portion, w_down)
    grad_w_down = transposed_times(hidden, portion)
    grad_hidden, grad_w_down = (grad_hidden, grad_w_down)
    unused, gelu_pull = jax.vjp(gelu_exact, pre_act)
    grad_pre = gelu_pull(grad_hidden)[0].astype(jnp.bfloat16)
    grad_b_up = jnp.sum(grad_pre.astype(jnp.float32), axis=0)
    grad_normed_two = lax.psum_scatter(
        times_transposed(grad_pre, w_up).astype(jnp.bfloat16), "tp", scatter_dimension=0, tiled=True
    ).astype(jnp.float32)
    grad_w_up = transposed_times(lax.all_gather(normed_two, "tp", axis=0, tiled=True), grad_pre)
    grad_middle_norm, grad_gain_two, grad_shift_two = norm_backward(
        middle, gain_two, shift_two, grad_normed_two
    )
    grad_middle = grad_block + grad_middle_norm
    grad_branch = (scale_one * grad_middle).astype(jnp.bfloat16)
    grad_scale_one = jnp.sum(grad_middle * branch, axis=0)
    grad_b_out = jnp.sum(grad_branch.astype(jnp.float32), axis=0)
    portion = lax.all_gather(grad_branch, "tp", axis=0, tiled=True)
    grad_context = times_transposed(portion, w_out)
    grad_w_out = transposed_times(context, portion)
    grad_context, grad_w_out = (grad_context, grad_w_out)
    grad_context = grad_context.astype(jnp.bfloat16).reshape(head_shape)
    grad_queries, grad_keys, grad_values = attend_backward(
        queries, key_rows, values, log_total, grad_context, factor
    )
    grad_joined = jnp.concatenate(
        [
            grad_queries.reshape(group_rows, local_cols),
            grad_keys.reshape(group_rows, local_cols),
            grad_values.reshape(group_rows, local_cols),
        ],
        axis=1,
    ).astype(jnp.bfloat16)
    grad_b_query = jnp.sum(grad_joined[:, :local_cols].astype(jnp.float32), axis=0)
    grad_b_value = jnp.sum(grad_joined[:, 2 * local_cols :].astype(jnp.float32), axis=0)
    grad_normed = lax.psum_scatter(
        times_transposed(grad_joined, w_joined).astype(jnp.bfloat16),
        "tp",
        scatter_dimension=0,
        tiled=True,
    ).astype(jnp.float32)
    grad_w_joined = transposed_times(lax.all_gather(normed, "tp", axis=0, tiled=True), grad_joined)
    grad_initial_norm, grad_gain_one, grad_shift_one = norm_backward(
        initial, gain_one, shift_one, grad_normed
    )
    grad_initial = grad_middle + grad_initial_norm
    grad_tokens = jnp.where(chosen, 0.0, grad_initial)
    grad_mask_token = jnp.sum(jnp.where(chosen, grad_initial, 0.0), axis=0)
    (
        grad_mask_token,
        grad_gain_one,
        grad_shift_one,
        grad_b_out,
        grad_scale_one,
        grad_gain_two,
        grad_shift_two,
        grad_b_down,
        grad_scale_two,
    ) = lax.psum(
        (
            grad_mask_token,
            grad_gain_one,
            grad_shift_one,
            grad_b_out,
            grad_scale_one,
            grad_gain_two,
            grad_shift_two,
            grad_b_down,
            grad_scale_two,
        ),
        ("dp", "tp"),
    )
    grad_b_query, grad_b_value, grad_b_up = lax.psum((grad_b_query, grad_b_value, grad_b_up), "dp")
    grad_w_joined, grad_w_out, grad_w_up, grad_w_down = (
        lax.psum_scatter(
            grad_w_joined.astype(jnp.bfloat16), "dp", scatter_dimension=0, tiled=True
        ).astype(jnp.float32),
        lax.psum_scatter(
            grad_w_out.astype(jnp.bfloat16), "dp", scatter_dimension=1, tiled=True
        ).astype(jnp.float32),
        lax.psum_scatter(
            grad_w_up.astype(jnp.bfloat16), "dp", scatter_dimension=0, tiled=True
        ).astype(jnp.float32),
        lax.psum_scatter(
            grad_w_down.astype(jnp.bfloat16), "dp", scatter_dimension=1, tiled=True
        ).astype(jnp.float32),
    )
    grad_w_query = grad_w_joined[:, :local_cols]
    grad_w_key = grad_w_joined[:, local_cols : 2 * local_cols]
    grad_w_value = grad_w_joined[:, 2 * local_cols :]
    return (
        block_out,
        grad_tokens,
        grad_mask_token,
        grad_gain_one,
        grad_shift_one,
        grad_w_query,
        grad_w_key,
        grad_w_value,
        grad_b_query,
        grad_b_value,
        grad_w_out,
        grad_b_out,
        grad_scale_one,
        grad_gain_two,
        grad_shift_two,
        grad_w_up,
        grad_b_up,
        grad_w_down,
        grad_b_down,
        grad_scale_two,
    )


def nn(left, right):
    return lax.dot_general(left, right, (((1,), (0,)), ((), ())), preferred_element_type=F32)


def nt(left, right):
    return lax.dot_general(left, right, (((1,), (1,)), ((), ())), preferred_element_type=F32)


def tn(left, right):
    return lax.dot_general(left, right, (((0,), (0,)), ((), ())), preferred_element_type=F32)


def padded(rows):
    return -(-rows // 32) * 32


def windows(rows):
    found = []
    for image in range(rows // SEQ):
        first = image * SEQ
        start = first // 16 * 16
        found.append((start, -(-(first - start + SEQ) // 16) * 16, first - start))
    return found


def row_blocks(total, size=160):
    return [slice(s, min(s + size, total)) for s in range(0, total, size)]


def inside(shape, axis, offset):
    at = lax.broadcasted_iota(jnp.int32, shape, axis)
    return (at >= offset) & (at < offset + SEQ)


def col_sum(values):
    return jnp.sum(values, axis=0, keepdims=True)


def row_mean(values):
    return jnp.mean(values, axis=-1, keepdims=True)


def moments(rows_in):
    center = rows_in - row_mean(rows_in)
    return center, lax.rsqrt(row_mean(center * center) + EPSILON)


def norm_pull(rows_in, gain, grad):
    center, inv = moments(rows_in)
    hat = center * inv
    scaled = grad * gain
    back = (scaled - row_mean(scaled) - hat * row_mean(scaled * hat)) * inv
    return back, col_sum(grad * hat), col_sum(grad)


def gelu_parts(v):
    size = jnp.abs(v)
    t = 1.0 / (1.0 + (0.3275911 * 0.7071067811865476) * size)
    e = jnp.exp(-0.5 * v * v)
    tail = (
        t
        * (
            0.5 * 0.254829592
            + t
            * (
                0.5 * -0.284496736
                + t * (0.5 * 1.421413741 + t * (0.5 * -1.453152027 + t * (0.5 * 1.061405429)))
            )
        )
        * e
    )
    return jnp.where(v < 0, tail, 1.0 - tail), v * e * 0.3989422804014327


def attend(rows, q_ref, k_ref, v_ref, ctx_ref):
    ctx_ref[padded(rows) - 32 :, :] = jnp.zeros((32, ctx_ref.shape[1]), BF16)

    def one_pair(pair, carry):
        lanes = pl.ds(pl.multiple_of(pair * PAIR, PAIR), PAIR)
        for start, size, offset in windows(rows):
            win = slice(start, start + size)
            q, k, v = q_ref[win, lanes], k_ref[win, lanes], v_ref[win, lanes]
            low_half = lax.broadcasted_iota(jnp.int32, (size, PAIR), 1) < HD
            here = inside((size, size), 1, offset)
            total = None
            for mine in (low_half, ~low_half):
                zero = jnp.zeros_like(k)
                scores = jnp.where(here, nt(q, jnp.where(mine, k, zero)), LOWEST)
                raised = jnp.exp(scores - jnp.max(scores, axis=-1, keepdims=True))
                share = 1.0 / jnp.sum(raised, axis=-1, keepdims=True)
                part = nn((raised * share).astype(BF16), jnp.where(mine, v, zero))
                total = part if total is None else total + part
            keep = inside((size, PAIR), 0, offset)
            ctx_ref[win, lanes] = jnp.where(keep, total.astype(BF16), ctx_ref[win, lanes])
        return carry

    lax.fori_loop(0, q_ref.shape[1] // PAIR, one_pair, 0)


def project(normed_ref, weights, bq_ref, bv_ref, q_ref, k_ref, v_ref):
    normed = normed_ref[...]
    wq, wk, wv = weights
    q_ref[...] = (nn(normed, wq) + bq_ref[...]).astype(BF16) * BF16(1.0 / math.sqrt(HD))
    k_ref[...] = nn(normed, wk).astype(BF16)
    v_ref[...] = (nn(normed, wv) + bv_ref[...]).astype(BF16)


def thirds(ref):
    cols = ref.shape[1] // 3
    return [ref[:, i * cols : (i + 1) * cols] for i in range(3)]


def first_kernel(
    rows, tok_ref, mask_ref, mt_ref, gain_ref, shift_ref, wq_ref, wk_ref, wv_ref, bq_ref, bv_ref,
    normed_ref, q_ref, k_ref, v_ref, ctx_ref,
):
    for block in row_blocks(rows):
        initial = jnp.where(mask_ref[block] > 0, mt_ref[...], tok_ref[block].astype(F32))
        center, inv = moments(initial)
        normed_ref[block] = (center * inv * gain_ref[...] + shift_ref[...]).astype(BF16)
    over = padded(rows) - rows
    normed_ref[rows:] = jnp.zeros((over, normed_ref.shape[1]), BF16)
    project(normed_ref, (wq_ref[...], wk_ref[...], wv_ref[...]), bq_ref, bv_ref, q_ref, k_ref, v_ref)
    attend(rows, q_ref, k_ref, v_ref, ctx_ref)


def second_kernel(
    rows, normed_ref, joined_ref, bq_ref, bv_ref, ctx_ref, wo_ref, wo2_ref, bo_ref,
    s1_ref, gain_ref, shift_ref, tok_ref, mask_ref, mt_ref, cot_ref, s2_ref,
    q_ref, k_ref, v_ref, ctx2_ref, middle_ref, normed2_ref, go_ref, sums_ref,
):
    project(normed_ref, thirds(joined_ref), bq_ref, bv_ref, q_ref, k_ref, v_ref)
    attend(rows, q_ref, k_ref, v_ref, ctx2_ref)
    over = padded(rows) - rows
    width = middle_ref.shape[1]
    total = jnp.zeros((1, width), F32)
    for block in row_blocks(rows):
        branch = nn(ctx_ref[block], wo_ref[...]) + nn(ctx2_ref[block], wo2_ref[...]) + bo_ref[...]
        masked = mask_ref[block] > 0
        initial = jnp.where(masked, mt_ref[...], tok_ref[block].astype(F32))
        middle = initial + s1_ref[...] * branch
        middle_ref[block] = middle
        center, inv = moments(middle)
        normed2_ref[block] = (center * inv * gain_ref[...] + shift_ref[...]).astype(BF16)
        grad_out = (jnp.where(masked, cot_ref[block].astype(F32), 0.0) * s2_ref[...]).astype(BF16)
        go_ref[block] = grad_out
        total += col_sum(grad_out.astype(F32))
    sums_ref[...] = total
    normed2_ref[rows:] = jnp.zeros((over, width), BF16)
    go_ref[rows:] = jnp.zeros((over, width), BF16)


def feed_kernel(
    me_ref, n2_ref, go_ref, wu_ref, wd_ref, bu_ref, hidden_ref, gp_ref, grads_ref, gb_ref
):
    pre = nn(n2_ref[...], wu_ref[...]) + bu_ref[...]
    grad_hidden = nt(go_ref[...], wd_ref[...])
    cdf, slope = gelu_parts(pre)
    hidden = (pre * cdf).astype(BF16)
    grad_pre = (grad_hidden * (cdf + slope)).astype(BF16)
    hidden_ref[...] = hidden
    gp_ref[...] = grad_pre
    gb_ref[...] = col_sum(grad_pre.astype(F32))
    store_blocks(me_ref[0], tn(go_ref[...], hidden), grads_ref, 0)
    store_blocks(me_ref[0], tn(n2_ref[...], grad_pre), grads_ref, hidden.shape[1])


def store_blocks(me, product_rows, out_ref, at):
    parts, size, _ = out_ref.shape
    cols = product_rows.shape[1]
    for b in range(parts):
        out_ref[b ^ me, :, at : at + cols] = product_rows[b * size : (b + 1) * size].astype(BF16)


def middle_kernel(
    rows, count, *refs
):
    gps, wus = refs[:count], refs[count : 2 * count]
    (middle_ref, tok_ref, mask_ref, mt_ref, cot_ref, gain_ref, s1_ref) = refs[2 * count : 2 * count + 7]
    gm_ref, gbr_ref, sums_ref, acc_ref = refs[2 * count + 7 :]
    step = pl.program_id(0)
    part = None
    for gp_ref, wu_ref in zip(gps, wus):
        one = nt(gp_ref[...], wu_ref[...])
        part = one if part is None else part + one

    @pl.when(step == 0)
    def first():
        acc_ref[...] = part

    @pl.when(step > 0)
    def later():
        acc_ref[...] += part

    @pl.when(step == pl.num_programs(0) - 1)
    def last():
        width = gm_ref.shape[1]
        sums = [jnp.zeros((1, width), F32)] * 4
        for block in row_blocks(rows):
            masked = mask_ref[block] > 0
            middle = middle_ref[block]
            back, grad_gain, grad_shift = norm_pull(middle, gain_ref[...], acc_ref[block])
            grad_middle = jnp.where(masked, cot_ref[block].astype(F32), 0.0) + back
            gm_ref[block] = grad_middle
            grad_branch = (s1_ref[...] * grad_middle).astype(BF16)
            gbr_ref[block] = grad_branch
            initial = jnp.where(masked, mt_ref[...], tok_ref[block].astype(F32))
            new = (
                grad_gain,
                grad_shift,
                col_sum(grad_middle * (middle - initial)) / s1_ref[...],
                col_sum(grad_branch.astype(F32)),
            )
            sums = [a + b for a, b in zip(sums, new)]
        for i, one in enumerate(sums):
            sums_ref[i : i + 1] = one
        over = padded(rows) - rows
        gbr_ref[rows:] = jnp.zeros((over, width), BF16)


def back_kernel(
    rows, me_ref, gbr_ref, wo_ref, ctx_ref, q_ref, k_ref, v_ref, n1_ref,
    dq_ref, dk_ref, dv_ref, grads_ref, sums_ref, gc_ref,
):
    me = me_ref[0]
    cols = q_ref.shape[1]
    gc_ref[...] = nt(gbr_ref[...], wo_ref[...]).astype(BF16)
    factor = 1.0 / math.sqrt(HD)
    for ref in (dq_ref, dk_ref, dv_ref):
        ref[padded(rows) - 32 :, :] = jnp.zeros((32, cols), BF16)

    def one_pair(pair, carry):
        lanes = pl.ds(pl.multiple_of(pair * PAIR, PAIR), PAIR)
        for start, size, offset in windows(rows):
            win = slice(start, start + size)
            q, k, v = q_ref[win, lanes], k_ref[win, lanes], v_ref[win, lanes]
            keep = inside((size, PAIR), 0, offset)
            gc = jnp.where(keep, gc_ref[win, lanes], jnp.zeros((size, PAIR), BF16))
            low_half = lax.broadcasted_iota(jnp.int32, (size, PAIR), 1) < HD
            here = inside((size, size), 0, offset)
            got = []
            for mine in (low_half, ~low_half):
                zero = jnp.zeros_like(k)
                k_one = jnp.where(mine, k, zero)
                scores = jnp.where(here, nt(k_one, q), LOWEST)
                raised = jnp.exp(scores - jnp.max(scores, axis=0, keepdims=True))
                probs = raised * (1.0 / jnp.sum(raised, axis=0, keepdims=True))
                grad_probs = nt(jnp.where(mine, v, zero), gc)
                inner = jnp.sum(grad_probs * probs, axis=0, keepdims=True)
                grad_scores = (probs * (grad_probs - inner)).astype(BF16)
                got.append((tn(grad_scores, k_one), nn(grad_scores, q), nn(probs.astype(BF16), gc)))
            low, high = got
            for ref, new in (
                (dq_ref, (low[0] + high[0]) * factor),
                (dk_ref, jnp.where(low_half, low[1], high[1])),
                (dv_ref, jnp.where(low_half, low[2], high[2])),
            ):
                ref[win, lanes] = jnp.where(keep, new.astype(BF16), ref[win, lanes])
        return carry

    lax.fori_loop(0, cols // PAIR, one_pair, 0)
    for i, ref in enumerate((dq_ref, dk_ref, dv_ref)):
        store_blocks(me, tn(n1_ref[...], ref[...]), grads_ref, i * cols)
        if i != 1:
            sums_ref[:, i // 2 * cols : (i // 2 + 1) * cols] = col_sum(ref[...].astype(F32))
    store_blocks(me, tn(gbr_ref[...], ctx_ref[...]), grads_ref, 3 * cols)


def input_kernel(
    rows, *refs
):
    grads, (wq_ref, wk_ref, wv_ref, joined_ref) = refs[:6], refs[6:10]
    tok_ref, mask_ref, mt_ref, gain_ref, gm_ref, out_ref, sums_ref = refs[10:]
    weights = [wq_ref[...], wk_ref[...], wv_ref[...]] + thirds(joined_ref)
    width = out_ref.shape[1]
    sums = [jnp.zeros((1, width), F32)] * 3
    for block in row_blocks(rows):
        grad_normed = None
        for grad_ref, w in zip(grads, weights):
            one = nt(grad_ref[block], w)
            grad_normed = one if grad_normed is None else grad_normed + one
        masked = mask_ref[block] > 0
        initial = jnp.where(masked, mt_ref[...], tok_ref[block].astype(F32))
        back, grad_gain, grad_shift = norm_pull(initial, gain_ref[...], grad_normed)
        grad_initial = gm_ref[block] + back
        out_ref[block] = jnp.where(masked, 0.0, grad_initial)
        new = (col_sum(jnp.where(masked, grad_initial, 0.0)), grad_gain, grad_shift)
        sums = [a + b for a, b in zip(sums, new)]
    for i, one in enumerate(sums):
        sums_ref[i : i + 1] = one


def output_kernel(
    rows, count, *refs
):
    hiddens, wds = refs[:count], refs[count : 2 * count]
    middle_ref, mask_ref, cot_ref, bd_ref, s2_ref = refs[2 * count : 2 * count + 5]
    out_ref, sums_ref, acc_ref = refs[2 * count + 5 :]
    step = pl.program_id(0)
    part = None
    for hidden_ref, wd_ref in zip(hiddens, wds):
        one = nn(hidden_ref[...], wd_ref[...])
        part = one if part is None else part + one

    @pl.when(step == 0)
    def first():
        acc_ref[...] = part

    @pl.when(step > 0)
    def later():
        acc_ref[...] += part

    @pl.when(step == pl.num_programs(0) - 1)
    def last():
        total = jnp.zeros((1, out_ref.shape[1]), F32)
        for block in row_blocks(rows):
            output = acc_ref[block] + bd_ref[...]
            out_ref[block] = (middle_ref[block] + s2_ref[...] * output).astype(BF16)
            grad_block = jnp.where(mask_ref[block] > 0, cot_ref[block].astype(F32), 0.0)
            total += col_sum(grad_block * output)
        sums_ref[...] = total


def shape_of(shape, dtype=BF16):
    return jax.ShapeDtypeStruct(shape, dtype)


def cost(flops, *arrays):
    moved = sum(a.size * a.dtype.itemsize for a in arrays)
    return pl.CostEstimate(flops=flops, bytes_accessed=moved, transcendentals=0)


def without(kernel, at, count):
    def inner(*refs):
        kernel(*refs[:at], *refs[at + count :])

    return inner


def whole_call(kernel, outs, args, flops, scratch=(), name=None, scalars=0, after=()):
    vmem = pl.BlockSpec(memory_space=pltpu.VMEM)
    smem = pl.BlockSpec(memory_space=pltpu.SMEM)
    anywhere = [pl.BlockSpec(memory_space=pl.ANY)] * len(after)
    return pl.pallas_call(
        without(kernel, 0, len(after)),
        in_specs=anywhere + [smem] * scalars + [vmem] * (len(args) - scalars),
        out_specs=[vmem] * len(outs),
        out_shape=outs,
        scratch_shapes=list(scratch),
        compiler_params=pltpu.CompilerParams(vmem_limit_bytes=56 * MIB),
        cost_estimate=cost(flops, *args, *outs),
        name=name,
    )(*after, *args)


def feed(me, n2, go, w_up, w_down, b_up, first, count, chunk, n, after=()):
    tall, width = n2.shape
    cols = count * chunk
    outs = [
        shape_of((tall, cols)),
        shape_of((tall, cols)),
        shape_of((n, width // n, 2 * cols)),
        shape_of((1, cols), F32),
    ]

    def all_of(array):
        return pl.BlockSpec(array.shape, lambda c, me: (0, 0))

    def along(size, base):
        return pl.BlockSpec((size, chunk), lambda c, me: (0, c + base))

    blocks = pl.BlockSpec((n, width // n, 2 * chunk), lambda c, me: (0, 0, c))
    return pl.pallas_call(
        without(feed_kernel, 1, len(after)),
        grid_spec=pltpu.PrefetchScalarGridSpec(
            num_scalar_prefetch=1,
            grid=(count,),
            in_specs=[pl.BlockSpec(memory_space=pl.ANY)] * len(after)
            + [
                all_of(n2),
                all_of(go),
                along(width, first),
                pl.BlockSpec((chunk, width), lambda c, me: (c + first, 0)),
                along(1, first),
            ],
            out_specs=[along(tall, 0), along(tall, 0), blocks, along(1, 0)],
        ),
        out_shape=outs,
        compiler_params=pltpu.CompilerParams(vmem_limit_bytes=56 * MIB),
        cost_estimate=cost(8 * tall * width * cols, n2, go, *outs),
        name="feed",
    )(me, *after, n2, go, w_up, w_down, b_up)


def summed(kernel, lefts, rights, picks, rights_axis, others, outs, steps, chunk, name, after=()):
    tall = lefts[0].shape[0]
    width = rights[0].shape[1 - rights_axis]
    specs = [pl.BlockSpec(memory_space=pl.ANY)] * len(after)
    specs += [pl.BlockSpec((tall, chunk), lambda c: (0, c)) for _ in lefts]
    for base in picks:
        if rights_axis:
            specs.append(pl.BlockSpec((width, chunk), lambda c, base=base: (0, c + base)))
        else:
            specs.append(pl.BlockSpec((chunk, width), lambda c, base=base: (c + base, 0)))
    specs += [pl.BlockSpec(a.shape, lambda c: (0, 0)) for a in others]
    return pl.pallas_call(
        without(kernel, 0, len(after)),
        grid=(steps,),
        in_specs=specs,
        out_specs=[pl.BlockSpec(o.shape, lambda c: (0, 0)) for o in outs],
        out_shape=outs,
        scratch_shapes=[pltpu.VMEM((tall, width), F32)],
        compiler_params=pltpu.CompilerParams(vmem_limit_bytes=56 * MIB),
        cost_estimate=cost(2 * tall * width * chunk * steps * len(lefts), *lefts, *others, *outs),
        name=name,
    )(*after, *lefts, *rights, *others)


def pairs(n, bit):
    return [(i, i ^ (1 << bit)) for i in range(n)]


class Piece:
    def __init__(self, segments, order, used=()):
        self.segments, self.order, self.used = segments, list(order), list(used)
        self.width = sum(width for width, _ in segments)
        self.result = None

    def job(self, steps):
        bit = self.order[0] if self.order else None
        tall = self.segments[0][1][0][0].shape[-2]
        rows = tall // steps

        def spec(bits, place, width):
            block = tuple(None if b in self.used or b == bit else 2 for b in bits)
            index = tuple(int(b == bit) for b in bits)
            return pl.BlockSpec(block + (rows, width), lambda r: index + (r, place))

        parts, at = [], 0
        for width, terms in self.segments:
            one = [(array, spec(bits, place, width)) for array, bits, place in terms]
            parts.append((one, slice(at, at + width)))
            at += width
        dims = (2,) * (len(self.order) - 1)
        out = pl.BlockSpec(dims + (rows, self.width), lambda r: (0,) * len(dims) + (r, 0))
        return parts, shape_of(dims + (tall, self.width), F32 if bit is None else BF16), out

    def take(self, sent):
        if not self.order:
            self.result = sent
            return
        bit = self.order.pop(0)
        self.used.append(bit)
        got = lax.ppermute(sent, "dp", pairs(lax.axis_size("dp"), bit))
        bits, at = sorted(self.order, reverse=True), 0
        for width, terms in self.segments:
            terms.append((got, bits, at // width))
            at += width

    def joined(self, other):
        return Piece(self.segments + other.segments, self.order, self.used)


def piece_of(arrays, place, width, order):
    bits = sorted(order, reverse=True)
    dims = (2,) * len(bits)
    return Piece([(width, [(a.reshape(dims + a.shape[1:]), bits, place) for a in arrays])], order)


def joining(pieces):
    kept = []
    for piece in pieces:
        if kept and piece.result is None and kept[-1].order == piece.order and piece.used:
            kept[-1] = kept[-1].joined(piece)
        else:
            kept.append(piece)
    return kept


class Sums:
    def __init__(self, same, own, other, bits):
        self.parts, self.own = same + other, same + own
        self.rounds = [bits[i : i + 2] for i in range(0, len(bits), 2)]
        self.stage, self.terms, self.result = 0, [], None

    def job(self, steps):
        def spec(array):
            return pl.BlockSpec(array.shape, lambda r: (0, 0))

        height = -(-sum(p.size // p.shape[-1] for p in self.parts) // 8) * 8
        width = max(p.shape[-1] for p in self.parts)
        shape = shape_of((height, width), F32)
        packed = {0: self.parts, 1: self.own}.get(self.stage, [])
        places, row, col = [], 0, 0
        for p in packed:
            if col + p.shape[1] > width:
                row, col = row + 1, 0
            places.append((slice(row, row + p.shape[0]), slice(col, col + p.shape[1])))
            col += p.shape[1]
            if col == width:
                row, col = row + p.shape[0], 0
        return [(p, spec(p)) for p in packed], places, [(t, spec(t)) for t in self.terms], shape, spec(shape)

    def take(self, sent):
        n = lax.axis_size("dp")
        if self.stage == 0:
            self.terms = [swap(sent)]
        elif self.stage <= len(self.rounds):
            bits = self.rounds[self.stage - 1]
            self.terms = [sent]
            for some in range(1, 1 << len(bits)):
                flip = sum(1 << b for i, b in enumerate(bits) if some >> i & 1)
                self.terms.append(lax.ppermute(sent, "dp", [(d, d ^ flip) for d in range(n)]))
        else:
            self.result = sent
        self.stage += 1


def exchange(pieces, after, sums=None, carry=None, steps=2):
    jobs = [p.job(steps) for p in pieces]
    arrays = [a for parts, _, _ in jobs for one, _ in parts for a, _ in one]
    specs = [b for parts, _, _ in jobs for one, _ in parts for _, b in one]
    out_specs = [out for _, _, out in jobs]
    out_shapes = [shape for _, shape, _ in jobs]
    packed, places, terms = [], [], []
    if sums is not None:
        packed, places, terms, shape, spec = sums.job(steps)
        arrays += [a for a, _ in packed + terms]
        specs += [b for _, b in packed + terms]
        out_specs.append(spec)
        out_shapes.append(shape)
    passed = [] if carry is None else [carry]
    hbm = pl.BlockSpec(memory_space=pl.ANY)
    count = len(after) + len(passed)

    def kernel(*refs):
        ins, outs = list(refs[: len(arrays)]), refs[len(arrays) :]
        for (parts, _, _), out in zip(jobs, outs):
            for one, cols in parts:
                total = None
                for _ in one:
                    term = ins.pop(0)[...].astype(F32)
                    total = term if total is None else total + term
                out[..., cols] = total.astype(out.dtype)
        if sums is not None:
            out = outs[len(jobs)]
            if not packed:
                out[...] = functools.reduce(jnp.add, [r[...] for r in ins])
            else:
                if not terms:
                    out[...] = jnp.zeros(out.shape, F32)
                else:
                    out[...] = ins[-1][...]
                for ref, place in zip(ins, places):
                    out[place] += ref[...]

    outs = pl.pallas_call(
        without(kernel, 0, count),
        grid=(steps,),
        in_specs=[hbm] * count + specs,
        out_specs=out_specs + [hbm] * len(passed),
        out_shape=out_shapes + [shape_of(p.shape, p.dtype) for p in passed],
        input_output_aliases={len(after): len(out_specs)} if passed else {},
        compiler_params=pltpu.CompilerParams(vmem_limit_bytes=40 * MIB),
        cost_estimate=cost(0, *out_shapes),
        name="exchange",
    )(*after, *passed, *arrays)
    for piece, out in zip(pieces, outs):
        piece.take(out)
    if sums is not None:
        sums.take(outs[len(jobs)])
    sent = list(outs[: len(out_specs)])
    return sent if carry is None else (sent, outs[-1])


def swap(array):
    return lax.ppermute(array, "tp", [(0, 1), (1, 0)])


def local_body(
    tokens, masked, cotangent, mask_token, gain_one, shift_one, w_query, w_key, w_value, b_query,
    b_value, w_out, b_out, scale_one, gain_two, shift_two, w_up, b_up, w_down, b_down, scale_two,
):
    rows, width = tokens.shape
    tall = padded(rows)
    half = w_query.shape[1]
    units = w_up.shape[1]
    n = lax.axis_size("dp")
    bits = n.bit_length() - 1
    me = lax.axis_index("dp").astype(jnp.int32).reshape(1)
    biases = jnp.concatenate([b_query, b_value, b_up]).reshape(-1, 128)

    joined2 = swap(jnp.concatenate([w_query, w_key, w_value], axis=1))
    biases2 = swap(biases).reshape(-1)
    wo2 = swap(w_out)
    wu2, wd2 = swap(w_up), swap(w_down)
    row = lambda v: v.reshape(1, -1)
    bq2, bv2, bu2 = row(biases2[:half]), row(biases2[half : 2 * half]), row(biases2[2 * half :])
    bq, bv, bu = row(b_query), row(b_value), row(b_up)
    mt, g1, s1, bo, sc1 = row(mask_token), row(gain_one), row(shift_one), row(b_out), row(scale_one)
    g2, s2, bd, sc2 = row(gain_two), row(shift_two), row(b_down), row(scale_two)
    mask = masked.reshape(rows, 1)

    narrow = shape_of((tall, half))
    wide = shape_of((tall, width))
    attend_flops = 2 * 2 * 256 * SEQ * rows * half // HD
    normed, q, k, v, ctx = whole_call(
        functools.partial(first_kernel, rows),
        [wide, narrow, narrow, narrow, narrow],
        (tokens, mask, mt, g1, s1, w_query, w_key, w_value, bq, bv),
        6 * rows * width * half + attend_flops,
        name="first",
    )
    q2, k2, v2, ctx2, middle, normed2, go, sum_go = whole_call(
        functools.partial(second_kernel, rows),
        [narrow, narrow, narrow, narrow, shape_of((rows, width), F32), wide, wide, shape_of((1, width), F32)],
        (normed, joined2, bq2, bv2, ctx, w_out, wo2, bo, sc1, g2, s2, tokens, mask, mt, cotangent, sc2),
        10 * rows * width * half + attend_flops,
        name="second",
    )

    natural = tuple(range(bits))
    by_x, by_y = natural, natural[1:2] + natural[0:1] + natural[2:]
    by_z = natural[2 % bits :] + natural[: 2 % bits]

    chunk = min(512, units)
    per = units // chunk // 2
    part = per * chunk
    hiddens, gps, firsts, sums_up, sums_up2 = [], [], [], [], []

    def three(own, theirs):
        cols = own.shape[2]
        both = (own, theirs)
        return [
            piece_of(both, 0, cols * 3 // 8, by_x),
            piece_of(both, 1, cols * 3 // 8, by_y),
            piece_of(both, 3, cols // 4, by_z),
        ]

    def keep(out, first, sums):
        hiddens.append(out[0])
        gps.append(out[1])
        firsts.append(first)
        sums.append(out[3])

    args = (me, normed2, go)
    his = feed(*args, wu2, wd2, bu2, 0, per, chunk, n)
    keep(his, 0, sums_up2)
    theirs = swap(his[2])
    own = feed(*args, w_up, w_down, bu, 0, per, chunk, n, after=[his[3]])
    keep(own, 0, sums_up)
    a = three(own[2], theirs)
    sent = exchange(a, [own[3]])
    his = feed(*args, wu2, wd2, bu2, per, per, chunk, n, after=sent)
    keep(his, per, sums_up2)
    sent, carried = exchange(a, [his[3]], carry=his[2])
    theirs = swap(carried)
    a = joining(a)
    own = feed(*args, w_up, w_down, bu, per, per, chunk, n, after=sent)
    keep(own, per, sums_up)
    b = three(own[2], theirs)
    sent = exchange(a + b, [own[3]])
    ups, downs = [wu2, w_up] * 2, [wd2, w_down] * 2

    gm, gbr, sums_two = summed(
        functools.partial(middle_kernel, rows, len(gps)),
        gps, ups, firsts, 1,
        (middle, tokens, mask, mt, cotangent, g2, sc1),
        [shape_of((rows, width), F32), wide, shape_of((4, width), F32)],
        per, chunk, "middle", after=sent,
    )
    sent = exchange(a + b, [sums_two])
    b = joining(b)

    def back(wo, ctx, q, k, v, after):
        return pl_back(rows, me, gbr, wo, ctx, q, k, v, normed, n, attend_flops, after)

    dq2, dk2, dv2, gw2, sums_b2 = back(wo2, ctx2, q2, k2, v2, sent)
    sent, gw2 = exchange(a + b, [sums_b2], carry=gw2)
    gw2 = swap(gw2)
    dq, dk, dv, gw, sums_b = back(w_out, ctx, q, k, v, sent)
    c = three(gw, gw2)
    sent = exchange(c + b, [sums_b])

    grad_tokens, sums_one = whole_call(
        functools.partial(input_kernel, rows),
        [shape_of((rows, width), F32), shape_of((3, width), F32)],
        (dq, dk, dv, dq2, dk2, dv2, w_query, w_key, w_value, joined2, tokens, mask, mt, g1, gm),
        12 * rows * width * half,
        name="input",
        after=sent,
    )
    sent = exchange(c + b, [sums_one])
    c = joining(c)
    block_out, sum_two = summed(
        functools.partial(output_kernel, rows, len(hiddens)),
        hiddens, downs, firsts, 0,
        (middle, mask, cotangent, bd, sc2),
        [shape_of((rows, width)), shape_of((1, width), F32)],
        per, chunk, "output", after=sent,
    )
    done = []
    same = [sums_one, sums_two, sum_go, sum_two]
    sums = Sums(same, [sums_b] + sums_up, [sums_b2] + sums_up2, list(natural))
    last = sum_two
    while sums.result is None:
        c = [piece for piece in c if piece.result is None]
        done += [piece for piece in c if not piece.order]
        last = exchange(c, [last], sums=sums)[-1]

    def columns(group):
        return jnp.concatenate([piece.result for piece in group], axis=1)

    def unmixed(group):
        both = columns(group).reshape(-1, per, 2, chunk)
        return both[:, :, 0].reshape(-1, part), both[:, :, 1].reshape(-1, part)

    (down_a, up_a), (down_b, up_b) = unmixed(a), unmixed(b)
    grad_w_down = jnp.concatenate([down_a, down_b], axis=1).T
    grad_w_up = jnp.concatenate([up_a, up_b], axis=1)
    attention = columns(done)

    rep = [sums.result[i] for i in range(9)]
    (grad_mask_token, grad_gain_one, grad_shift_one, grad_gain_two, grad_shift_two, grad_scale_one,
     grad_b_out, grad_b_down, grad_scale_two) = rep
    own = sums.result[9:].reshape(-1)
    return (
        block_out,
        grad_tokens,
        grad_mask_token,
        grad_gain_one,
        grad_shift_one,
        attention[:, :half],
        attention[:, half : 2 * half],
        attention[:, 2 * half : 3 * half],
        own[:half],
        own[half : 2 * half],
        attention[:, 3 * half :].T,
        grad_b_out,
        grad_scale_one,
        grad_gain_two,
        grad_shift_two,
        grad_w_up,
        own[2 * half : 2 * half + units],
        grad_w_down,
        grad_b_down,
        grad_scale_two,
    )


def pl_back(rows, me, gbr, wo, ctx, q, k, v, normed, n, attend_flops, after):
    tall, cols = q.shape
    width = gbr.shape[1]
    narrow = shape_of((tall, cols))
    return whole_call(
        functools.partial(back_kernel, rows),
        [narrow, narrow, narrow, shape_of((n, width // n, 4 * cols)), shape_of((1, 2 * cols), F32)],
        (me, gbr, wo, ctx, q, k, v, normed),
        10 * rows * width * cols + 3 * attend_flops,
        scratch=[pltpu.VMEM((tall, cols), BF16)],
        name="back",
        scalars=1,
        after=after,
    )


def solution(mesh):
    placed = (
        P(("dp", "tp"), None),
        P(("dp", "tp")),
        P(("dp", "tp"), None),
        P(),
        P(),
        P(),
        P(None, "tp"),
        P(None, "tp"),
        P(None, "tp"),
        P("tp"),
        P("tp"),
        P("tp", None),
        P(),
        P(),
        P(),
        P(),
        P(None, "tp"),
        P("tp"),
        P("tp", None),
        P(),
        P(),
    )
    fits = mesh.shape["tp"] == 2 and mesh.shape["dp"].bit_count() == 1
    return jax.shard_map(
        local_body if fits else gathered_body,
        mesh=mesh,
        in_specs=placed,
        out_specs=(
            P(("dp", "tp"), None),
            P(("dp", "tp"), None),
            P(),
            P(),
            P(),
            P("dp", "tp"),
            P("dp", "tp"),
            P("dp", "tp"),
            P("tp"),
            P("tp"),
            P("tp", "dp"),
            P(),
            P(),
            P(),
            P(),
            P("dp", "tp"),
            P("tp"),
            P("tp", "dp"),
            P(),
            P(),
        ),
        check_vma=False,
    )
```

```python
import functools
import math

import jax
import jax.numpy as jnp
from jax import lax
from jax.experimental import pallas as pl
from jax.experimental.pallas import tpu as pltpu
from jax.sharding import PartitionSpec as P

SEQ = 197
HD = 64
PAIR = 2 * HD
EPSILON = 1e-06
BF16 = jnp.bfloat16
F32 = jnp.float32
MIB = 2**20
LOWEST = -1e30
KERNEL_VMEM = 63 * MIB
EXCHANGE_VMEM = 63 * MIB

def layer_norm(rows_in, gain_vec, shift_vec):
    center = rows_in - jnp.mean(rows_in, axis=-1, keepdims=True)
    spread = jnp.mean(center * center, axis=-1, keepdims=True)
    return center * lax.rsqrt(spread + EPSILON) * gain_vec + shift_vec


def norm_backward(rows_in, gain_vec, shift_vec, grad_rows):
    unused, pull = jax.vjp(layer_norm, rows_in, gain_vec, shift_vec)
    return pull(grad_rows)


def gelu_exact(values):
    return jax.nn.gelu(values, approximate=False)


def product(left, right):
    return jnp.dot(left, right, preferred_element_type=jnp.float32)


def times_transposed(left, right):
    return lax.dot_general(
        left, right, (((1,), (1,)), ((), ())), preferred_element_type=jnp.float32
    )


def transposed_times(left, right):
    return lax.dot_general(
        left, right, (((0,), (0,)), ((), ())), preferred_element_type=jnp.float32
    )


def attend_forward(queries, key_rows, values, factor):
    scores = (
        jnp.einsum("iqhd,ikhd->ihqk", queries, key_rows, preferred_element_type=jnp.float32)
        * factor
    )
    row_max = jnp.max(scores, axis=-1, keepdims=True)
    raised = jnp.exp(scores - row_max)
    sum_exp = jnp.sum(raised, axis=-1, keepdims=True)
    probs_low = (raised / sum_exp).astype(jnp.bfloat16)
    context = jnp.einsum("ihqk,ikhd->iqhd", probs_low, values, preferred_element_type=jnp.float32)
    return (context, row_max + jnp.log(sum_exp))


def attend_backward(queries, key_rows, values, log_total, grad_context, factor):
    scores = (
        jnp.einsum("iqhd,ikhd->ihqk", queries, key_rows, preferred_element_type=jnp.float32)
        * factor
    )
    probs = jnp.exp(scores - log_total)
    grad_probs = jnp.einsum(
        "iqhd,ikhd->ihqk", grad_context, values, preferred_element_type=jnp.float32
    )
    inner = jnp.sum(grad_probs * probs, axis=-1, keepdims=True)
    grad_scores = (probs * (grad_probs - inner)).astype(jnp.bfloat16)
    grad_queries = (
        jnp.einsum("ihqk,ikhd->iqhd", grad_scores, key_rows, preferred_element_type=jnp.float32)
        * factor
    )
    grad_keys = (
        jnp.einsum("ihqk,iqhd->ikhd", grad_scores, queries, preferred_element_type=jnp.float32)
        * factor
    )
    grad_values = jnp.einsum(
        "ihqk,iqhd->ikhd",
        probs.astype(jnp.bfloat16),
        grad_context,
        preferred_element_type=jnp.float32,
    )
    return (grad_queries, grad_keys, grad_values)


def gathered_body(
    tokens,
    masked,
    cotangent,
    mask_token,
    gain_one,
    shift_one,
    w_query,
    w_key,
    w_value,
    b_query,
    b_value,
    w_out,
    b_out,
    scale_one,
    gain_two,
    shift_two,
    w_up,
    b_up,
    w_down,
    b_down,
    scale_two,
):
    local_cols = w_query.shape[1]
    local_heads = local_cols // HD
    factor = 1.0 / math.sqrt(HD)
    chosen = (masked > 0)[:, None]
    initial = jnp.where(chosen, mask_token[None, :], tokens.astype(jnp.float32))
    normed = layer_norm(initial, gain_one, shift_one).astype(jnp.bfloat16)
    w_joined = jnp.concatenate([w_query, w_key, w_value], axis=1)
    b_joined = jnp.concatenate([b_query, jnp.zeros_like(b_query), b_value])
    gathered = lax.all_gather(normed, "tp", axis=0, tiled=True)
    joined = (product(gathered, w_joined) + b_joined).astype(jnp.bfloat16)
    group_rows = gathered.shape[0]
    head_shape = (group_rows // SEQ, SEQ, local_heads, HD)
    queries = joined[:, :local_cols].reshape(head_shape)
    key_rows = joined[:, local_cols : 2 * local_cols].reshape(head_shape)
    values = joined[:, 2 * local_cols :].reshape(head_shape)
    context, log_total = attend_forward(queries, key_rows, values, factor)
    context = context.reshape(group_rows, local_cols).astype(jnp.bfloat16)
    branch = (
        lax.psum_scatter(
            product(context, w_out).astype(jnp.bfloat16), "tp", scatter_dimension=0, tiled=True
        ).astype(jnp.float32)
        + b_out
    )
    middle = initial + scale_one * branch
    normed_two = layer_norm(middle, gain_two, shift_two).astype(jnp.bfloat16)
    gathered_two = lax.all_gather(normed_two, "tp", axis=0, tiled=True)
    pre_act = product(gathered_two, w_up) + b_up
    hidden = gelu_exact(pre_act).astype(jnp.bfloat16)
    output = (
        lax.psum_scatter(
            product(hidden, w_down).astype(jnp.bfloat16), "tp", scatter_dimension=0, tiled=True
        ).astype(jnp.float32)
        + b_down
    )
    block_out = (middle + scale_two * output).astype(jnp.bfloat16)
    grad_block = cotangent.astype(jnp.float32) * chosen.astype(jnp.float32)
    grad_output = (scale_two * grad_block).astype(jnp.bfloat16)
    grad_scale_two = jnp.sum(grad_block * output, axis=0)
    grad_b_down = jnp.sum(grad_output.astype(jnp.float32), axis=0)
    portion = lax.all_gather(grad_output, "tp", axis=0, tiled=True)
    grad_hidden = times_transposed(portion, w_down)
    grad_w_down = transposed_times(hidden, portion)
    grad_hidden, grad_w_down = (grad_hidden, grad_w_down)
    unused, gelu_pull = jax.vjp(gelu_exact, pre_act)
    grad_pre = gelu_pull(grad_hidden)[0].astype(jnp.bfloat16)
    grad_b_up = jnp.sum(grad_pre.astype(jnp.float32), axis=0)
    grad_normed_two = lax.psum_scatter(
        times_transposed(grad_pre, w_up).astype(jnp.bfloat16), "tp", scatter_dimension=0, tiled=True
    ).astype(jnp.float32)
    grad_w_up = transposed_times(lax.all_gather(normed_two, "tp", axis=0, tiled=True), grad_pre)
    grad_middle_norm, grad_gain_two, grad_shift_two = norm_backward(
        middle, gain_two, shift_two, grad_normed_two
    )
    grad_middle = grad_block + grad_middle_norm
    grad_branch = (scale_one * grad_middle).astype(jnp.bfloat16)
    grad_scale_one = jnp.sum(grad_middle * branch, axis=0)
    grad_b_out = jnp.sum(grad_branch.astype(jnp.float32), axis=0)
    portion = lax.all_gather(grad_branch, "tp", axis=0, tiled=True)
    grad_context = times_transposed(portion, w_out)
    grad_w_out = transposed_times(context, portion)
    grad_context, grad_w_out = (grad_context, grad_w_out)
    grad_context = grad_context.astype(jnp.bfloat16).reshape(head_shape)
    grad_queries, grad_keys, grad_values = attend_backward(
        queries, key_rows, values, log_total, grad_context, factor
    )
    grad_joined = jnp.concatenate(
        [
            grad_queries.reshape(group_rows, local_cols),
            grad_keys.reshape(group_rows, local_cols),
            grad_values.reshape(group_rows, local_cols),
        ],
        axis=1,
    ).astype(jnp.bfloat16)
    grad_b_query = jnp.sum(grad_joined[:, :local_cols].astype(jnp.float32), axis=0)
    grad_b_value = jnp.sum(grad_joined[:, 2 * local_cols :].astype(jnp.float32), axis=0)
    grad_normed = lax.psum_scatter(
        times_transposed(grad_joined, w_joined).astype(jnp.bfloat16),
        "tp",
        scatter_dimension=0,
        tiled=True,
    ).astype(jnp.float32)
    grad_w_joined = transposed_times(lax.all_gather(normed, "tp", axis=0, tiled=True), grad_joined)
    grad_initial_norm, grad_gain_one, grad_shift_one = norm_backward(
        initial, gain_one, shift_one, grad_normed
    )
    grad_initial = grad_middle + grad_initial_norm
    grad_tokens = jnp.where(chosen, 0.0, grad_initial)
    grad_mask_token = jnp.sum(jnp.where(chosen, grad_initial, 0.0), axis=0)
    (
        grad_mask_token,
        grad_gain_one,
        grad_shift_one,
        grad_b_out,
        grad_scale_one,
        grad_gain_two,
        grad_shift_two,
        grad_b_down,
        grad_scale_two,
    ) = lax.psum(
        (
            grad_mask_token,
            grad_gain_one,
            grad_shift_one,
            grad_b_out,
            grad_scale_one,
            grad_gain_two,
            grad_shift_two,
            grad_b_down,
            grad_scale_two,
        ),
        ("dp", "tp"),
    )
    grad_b_query, grad_b_value, grad_b_up = lax.psum((grad_b_query, grad_b_value, grad_b_up), "dp")
    grad_w_joined, grad_w_out, grad_w_up, grad_w_down = (
        lax.psum_scatter(
            grad_w_joined.astype(jnp.bfloat16), "dp", scatter_dimension=0, tiled=True
        ).astype(jnp.float32),
        lax.psum_scatter(
            grad_w_out.astype(jnp.bfloat16), "dp", scatter_dimension=1, tiled=True
        ).astype(jnp.float32),
        lax.psum_scatter(
            grad_w_up.astype(jnp.bfloat16), "dp", scatter_dimension=0, tiled=True
        ).astype(jnp.float32),
        lax.psum_scatter(
            grad_w_down.astype(jnp.bfloat16), "dp", scatter_dimension=1, tiled=True
        ).astype(jnp.float32),
    )
    grad_w_query = grad_w_joined[:, :local_cols]
    grad_w_key = grad_w_joined[:, local_cols : 2 * local_cols]
    grad_w_value = grad_w_joined[:, 2 * local_cols :]
    return (
        block_out,
        grad_tokens,
        grad_mask_token,
        grad_gain_one,
        grad_shift_one,
        grad_w_query,
        grad_w_key,
        grad_w_value,
        grad_b_query,
        grad_b_value,
        grad_w_out,
        grad_b_out,
        grad_scale_one,
        grad_gain_two,
        grad_shift_two,
        grad_w_up,
        grad_b_up,
        grad_w_down,
        grad_b_down,
        grad_scale_two,
    )


def nn(left, right):
    return lax.dot_general(left, right, (((1,), (0,)), ((), ())), preferred_element_type=F32)


def nt(left, right):
    return lax.dot_general(left, right, (((1,), (1,)), ((), ())), preferred_element_type=F32)


def tn(left, right):
    return lax.dot_general(left, right, (((0,), (0,)), ((), ())), preferred_element_type=F32)


def padded(rows):
    return -(-rows // 32) * 32


def windows(rows):
    found = []
    for image in range(rows // SEQ):
        first = image * SEQ
        start = first // 16 * 16
        found.append((start, -(-(first - start + SEQ) // 16) * 16, first - start))
    return found


def row_blocks(total, size=160):
    return [slice(s, min(s + size, total)) for s in range(0, total, size)]


def inside(shape, axis, offset):
    at = lax.broadcasted_iota(jnp.int32, shape, axis)
    return (at >= offset) & (at < offset + SEQ)


def col_sum(values):
    return jnp.sum(values, axis=0, keepdims=True)


def row_mean(values):
    return jnp.mean(values, axis=-1, keepdims=True)


def moments(rows_in):
    center = rows_in - row_mean(rows_in)
    return center, lax.rsqrt(row_mean(center * center) + EPSILON)


def norm_pull(rows_in, gain, grad):
    center, inv = moments(rows_in)
    hat = center * inv
    scaled = grad * gain
    back = (scaled - row_mean(scaled) - hat * row_mean(scaled * hat)) * inv
    return back, col_sum(grad * hat), col_sum(grad)


def gelu_parts(v):
    size = jnp.abs(v)
    t = 1.0 / (1.0 + (0.3275911 * 0.7071067811865476) * size)
    e = jnp.exp(-0.5 * v * v)
    tail = (
        t
        * (
            0.5 * 0.254829592
            + t
            * (
                0.5 * -0.284496736
                + t * (0.5 * 1.421413741 + t * (0.5 * -1.453152027 + t * (0.5 * 1.061405429)))
            )
        )
        * e
    )
    return jnp.where(v < 0, tail, 1.0 - tail), v * e * 0.3989422804014327


def rows_outside(values, offset, fill):
    size = values.shape[0]

    def edge(part, base):
        at = lax.broadcasted_iota(jnp.int32, part.shape, 0) + base
        return jnp.where((at >= offset) & (at < offset + SEQ), part, fill)

    head = edge(values[:16], 0) if offset else values[:16]
    return jnp.concatenate([head, values[16:-32], edge(values[-32:], size - 32)], axis=0)


def one_head(shape, head):
    return (lax.broadcasted_iota(jnp.int32, shape, 1) < HD) == (head == 0)


def in_turn(rows, lead, begin, finish):
    units = [(window, head) for window in windows(rows) for head in (0, 1)]
    begun = [begin(*unit) for unit in units[:lead]]
    for i, unit in enumerate(units):
        if i + lead < len(units):
            begun.append(begin(*units[i + lead]))
        finish(i, *unit, begun[i])
        begun[i] = None


def norm_rows(rows, cols):
    return (cols // HD * (rows // SEQ), 256)


def attend(rows, q_ref, k_ref, v_ref, ctx_ref, log_ref):
    ctx_ref[padded(rows) - 32 :, :] = jnp.zeros((32, ctx_ref.shape[1]), BF16)
    count = 2 * (rows // SEQ)

    def one_pair(pair, carry):
        lanes = pl.ds(pl.multiple_of(pair * PAIR, PAIR), PAIR)
        halves = {}

        def begin(window, head):
            start, size, _ = window
            win = slice(start, start + size)
            k = k_ref[win, lanes]
            return nt(jnp.where(one_head(k.shape, head), k, jnp.zeros_like(k)), q_ref[win, lanes])

        def finish(i, window, head, scores):
            start, size, offset = window
            win = slice(start, start + size)
            scores = rows_outside(scores, offset, LOWEST)
            top = jnp.max(scores, axis=0, keepdims=True)
            raised = jnp.exp(scores - top)
            total = jnp.sum(raised, axis=0, keepdims=True)
            out = tn(v_ref[win, lanes], raised.astype(BF16))
            halves[head] = out[head * HD : (head + 1) * HD] * (1.0 / total)
            log_ref[pl.ds(pair * count + i, 1), :size] = top + jnp.log(total)
            if head == 1:
                both = jnp.concatenate([halves[0], halves[1]], axis=0).T.astype(BF16)
                keep = inside((size, PAIR), 0, offset)
                ctx_ref[win, lanes] = jnp.where(keep, both, ctx_ref[win, lanes])

        in_turn(rows, 2, begin, finish)
        return carry

    lax.fori_loop(0, q_ref.shape[1] // PAIR, one_pair, 0)


def attend_back(rows, q_ref, k_ref, v_ref, gc_ref, log_ref, dq_ref, dk_ref, dv_ref):
    for ref in (dq_ref, dk_ref, dv_ref):
        ref[padded(rows) - 32 :, :] = jnp.zeros((32, ref.shape[1]), BF16)
    factor = 1.0 / math.sqrt(HD)
    count = 2 * (rows // SEQ)

    def one_pair(pair, carry):
        lanes = pl.ds(pl.multiple_of(pair * PAIR, PAIR), PAIR)
        halves = {}

        def begin(window, head):
            start, size, offset = window
            win = slice(start, start + size)
            zero = jnp.zeros((size, PAIR), BF16)
            mine = one_head(zero.shape, head)
            k = jnp.where(mine, k_ref[win, lanes], zero)
            v = jnp.where(mine, v_ref[win, lanes], zero)
            gc = jnp.where(inside(zero.shape, 0, offset), gc_ref[win, lanes], zero)
            q = q_ref[win, lanes]
            return nt(k, q), nt(v, gc), k, q, gc

        def finish(i, window, head, begun):
            start, size, offset = window
            win = slice(start, start + size)
            scores, grad_probs, k, q, gc = begun
            scores = rows_outside(scores, offset, LOWEST)
            probs = jnp.exp(scores - log_ref[pl.ds(pair * count + i, 1), :size])
            inner = jnp.sum(grad_probs * probs, axis=0, keepdims=True)
            grad_scores = (probs * (grad_probs - inner)).astype(BF16)
            halves[head] = tn(grad_scores, k), nn(grad_scores, q), nn(probs.astype(BF16), gc)
            if head == 1:
                keep = inside((size, PAIR), 0, offset)
                first = one_head((size, PAIR), 0)
                low, high = halves[0], halves[1]
                for ref, new in (
                    (dq_ref, (low[0] + high[0]) * factor),
                    (dk_ref, jnp.where(first, low[1], high[1])),
                    (dv_ref, jnp.where(first, low[2], high[2])),
                ):
                    ref[win, lanes] = jnp.where(keep, new.astype(BF16), ref[win, lanes])

        in_turn(rows, 2, begin, finish)
        return carry

    lax.fori_loop(0, q_ref.shape[1] // PAIR, one_pair, 0)


class Moved:
    def __init__(self, far, near, line, pieces=(None,)):
        self.far, self.near, self.line, self.pieces = far, near, line, pieces
        self.copies = [line.add(*self.views(p)) for p in pieces]

    def views(self, p):
        return (self.far, self.near) if p is None else (self.far.at[p], self.near.at[p])

    def part(self, i):
        self.line.wait(self.copies[i])
        return self.views(self.pieces[i])[1]

    @property
    def ref(self):
        for copy in self.copies:
            self.line.wait(copy)
        return self.near

    def send(self, p=None):
        far, near = self.views(p)
        self.line.send(near, far)


class Line:
    def __init__(self, sems, count):
        self.sems, self.free = sems, iter(range(count))
        self.queue, self.waves, self.started, self.waited, self.sent = [], [], 0, set(), []

    def copy(self, source, target):
        return pltpu.make_async_copy(source, target, self.sems.at[next(self.free)])

    def add(self, source, target):
        self.queue.append(self.copy(source, target))
        return len(self.queue) - 1

    def begin(self, waves=()):
        first = [i for wave in waves for i in wave]
        rest = [i for i in range(len(self.queue)) if i not in first]
        self.waves = [list(wave) for wave in waves] + [rest]
        self.start_to(1)

    def start_to(self, stop):
        while self.started < min(stop, len(self.waves)):
            for i in self.waves[self.started]:
                self.queue[i].start()
            self.started += 1

    def wait(self, i):
        if i in self.waited:
            return
        wave = next(k for k, some in enumerate(self.waves) if i in some)
        self.start_to(wave + 1)
        self.queue[i].wait()
        self.waited.add(i)
        self.start_to(wave + 2)

    def send(self, source, target):
        copy = self.copy(source, target)
        copy.start()
        self.sent.append(copy)

    def finish(self):
        for i in range(len(self.queue)):
            self.wait(i)
        for copy in self.sent:
            copy.wait()


class View:
    def __init__(self, array, axis=0, start=0, size=None):
        self.array, self.shape, self.index = array, array.shape, None
        if size is not None:
            p = slice(start, start + size)
            self.index = (slice(None),) * axis + (p,)
            self.shape = tuple(size if i == axis else n for i, n in enumerate(array.shape))


def cut_in(size, axis, count):
    step = size // count
    spans = [slice(i * step, (i + 1) * step) for i in range(count)]
    return [(slice(None),) * axis + (p,) for p in spans]


def moved_call(kernel, outs, args, flops, sends, scratch=(), name=None, after=(), cuts=None, waves=()):
    hbm = pl.BlockSpec(memory_space=pl.ANY)
    cuts = cuts or {}
    views = [a if isinstance(a, View) else View(a) for a in args]
    args = [view.array for view in views]
    n_in, n_out = len(args), len(outs)
    pieces = [
        cut_in(v.shape[cuts[i][0]], *cuts[i]) if i in cuts else [None] for i, v in enumerate(views)
    ]
    n_sems = sum(len(p) for p in pieces) + sends
    buffers = [pltpu.VMEM(v.shape, v.array.dtype) for v in views]
    buffers += [pltpu.VMEM(o.shape, o.dtype) for o in outs]

    def inner(*refs):
        refs = refs[len(after) :]
        far_in, far_out, rest = refs[:n_in], refs[n_in : n_in + n_out], list(refs[n_in + n_out :])
        line = Line(rest.pop(), n_sems)
        ins = []
        for far, view, p in zip(far_in, views, pieces):
            far = far if view.index is None else far.at[view.index]
            ins.append(Moved(far, rest.pop(0), line, p))
        line.begin([[ins[i].copies[j] for i, j in wave] for wave in waves])
        results = [Moved(far, rest.pop(0), line, ()) for far in far_out]
        kernel(*ins, *results, *rest)
        line.finish()

    return pl.pallas_call(
        inner,
        in_specs=[hbm] * (len(after) + n_in),
        out_specs=[hbm] * n_out,
        out_shape=outs,
        scratch_shapes=buffers + list(scratch) + [pltpu.SemaphoreType.DMA((n_sems,))],
        compiler_params=pltpu.CompilerParams(vmem_limit_bytes=KERNEL_VMEM),
        cost_estimate=cost(flops, *args, *outs),
        name=name,
    )(*after, *args)


def halves_of(tall):
    middle = tall // 2 // 16 * 16
    return [slice(0, middle), slice(middle, tall)]


def blocks_within(part, rows, size=80):
    stop = min(part.stop, rows)
    return [slice(s, min(s + size, stop)) for s in range(part.start, stop, size)]


def first_kernel(
    rows, tok, mask, mt, gain, shift, wq, wk, wv, bq, bv,
    normed, q, k, v, ctx, log,
):
    normed_ref = normed.near
    tok_ref, mask_ref = tok.ref, mask.ref
    mt_ref, gain_ref, shift_ref = mt.ref, gain.ref, shift.ref
    for block in blocks_within(slice(0, rows), rows):
        initial = jnp.where(mask_ref[block] > 0, mt_ref[...], tok_ref[block].astype(F32))
        center, inv = moments(initial)
        normed_ref[block] = (center * inv * gain_ref[...] + shift_ref[...]).astype(BF16)
    over = padded(rows) - rows
    normed_ref[rows:] = jnp.zeros((over, normed_ref.shape[1]), BF16)
    normed.send()
    project(normed_ref, [wq, wk, wv], bq, bv, q, k, v)
    attend(rows, q.near, k.near, v.near, ctx.near, log.near)
    ctx.send()
    log.send()


def project(normed_ref, weights, bq, bv, q, k, v):
    scale = BF16(1.0 / math.sqrt(HD))
    wq, wk, wv = weights
    q.near[...] = (nn(normed_ref[...], wq.ref[...]) + bq.ref[...]).astype(BF16) * scale
    q.send()
    k.near[...] = nn(normed_ref[...], wk.ref[...]).astype(BF16)
    k.send()
    v.near[...] = (nn(normed_ref[...], wv.ref[...]) + bv.ref[...]).astype(BF16)
    v.send()


class Third:
    def __init__(self, moved, i):
        self.moved, self.i = moved, i

    @property
    def ref(self):
        return self.moved.part(self.i)


def second_kernel(
    rows, normed, joined, bq, bv, ctx, wo, wo2, bo,
    s1, gain, shift, tok, mask, mt, cot, s2,
    q, k, v, ctx2, log, middle, normed2, go, sums, acc_ref,
):
    project(normed.ref, [Third(joined, i) for i in range(3)], bq, bv, q, k, v)
    attend(rows, q.near, k.near, v.near, ctx2.near, log.near)
    ctx2.send()
    log.send()
    over = padded(rows) - rows
    width = acc_ref.shape[1]
    total = jnp.zeros((1, width), F32)
    ctx_ref, wo_ref, wo2_ref = ctx.ref, wo.ref, wo2.ref
    tok_ref, mask_ref, cot_ref = tok.ref, mask.ref, cot.ref
    bo_ref, s1_ref, gain_ref, shift_ref, mt_ref, s2_ref = (v.ref for v in (bo, s1, gain, shift, mt, s2))
    for half in halves_of(padded(rows)):
        acc_ref[half] = nn(ctx_ref[half], wo_ref[...]) + nn(ctx2.near[half], wo2_ref[...])
    for half in halves_of(padded(rows)):
        for block in blocks_within(half, rows):
            masked = mask_ref[block] > 0
            initial = jnp.where(masked, mt_ref[...], tok_ref[block].astype(F32))
            one = initial + s1_ref[...] * (acc_ref[block] + bo_ref[...])
            middle.near[block] = one
            center, inv = moments(one)
            normed2.near[block] = (center * inv * gain_ref[...] + shift_ref[...]).astype(BF16)
            grad_out = jnp.where(masked, cot_ref[block].astype(F32), 0.0) * s2_ref[...]
            grad_out = grad_out.astype(BF16)
            go.near[block] = grad_out
            total += col_sum(grad_out.astype(F32))
        if half.stop == padded(rows):
            middle.near[rows:] = jnp.zeros((over, width), F32)
            normed2.near[rows:] = jnp.zeros((over, width), BF16)
            go.near[rows:] = jnp.zeros((over, width), BF16)
        for one in (normed2, go, middle):
            one.send(half)
    sums.near[...] = total
    sums.send()


def feed_kernel(chunk, n2, wu, go, wd, bu, hidden, gp, grads, sums, scale_sum):
    me = lax.axis_index("dp")
    cols = hidden.near.shape[1]
    width = n2.near.shape[1]
    lanes = None
    for i in range(cols // chunk):
        at = slice(i * chunk, (i + 1) * chunk)
        pre = nn(n2.ref[...], wu.part(i)[...]) + bu.ref[:, at]
        grad_hidden = nt(go.ref[...], wd.part(i)[...])
        cdf, slope = gelu_parts(pre)
        new_hidden = (pre * cdf).astype(BF16)
        grad_pre = (grad_hidden * (cdf + slope)).astype(BF16)
        hidden.near[:, at] = new_hidden
        gp.near[:, at] = grad_pre
        hidden.send((slice(None), at))
        gp.send((slice(None), at))
        sums.near[:, at] = col_sum(grad_pre.astype(F32))
        down = tn(go.ref[...], new_hidden)
        weighed = down * wd.part(i)[...].T.astype(F32)
        for k in range(0, chunk, 128):
            part = weighed[:, k : k + 128]
            lanes = part if lanes is None else lanes + part
        for j, grad in enumerate((down, tn(n2.ref[...], grad_pre))):
            base = (2 * i + j) * chunk
            store_blocks(me, grad, grads.near, base)
            grads.send((slice(None), slice(None), slice(base, base + chunk)))
    sums.send()
    scale_sum.near[...] = col_sum(lanes.T)
    scale_sum.send()


def store_blocks(me, product_rows, out_ref, at):
    parts, size, _ = out_ref.shape
    cols = product_rows.shape[1]
    for b in range(parts):
        out_ref[b ^ me, :, at : at + cols] = product_rows[b * size : (b + 1) * size].astype(BF16)


def middle_kernel(rows, count, *refs):
    gps, wus = refs[:count], refs[count : 2 * count]
    middle, tok, mask, mt, cot, gain, s1 = refs[2 * count : 2 * count + 7]
    gm, gbr, sums, acc_ref = refs[2 * count + 7 :]
    width = acc_ref.shape[1]
    total = [jnp.zeros((1, width), F32)] * 4
    halves = halves_of(padded(rows))
    for i, (one, w) in enumerate(zip(gps, wus)):
        for half in halves:
            part = nt(one.ref[half], w.ref[...])
            acc_ref[half] = part if i == 0 else acc_ref[half] + part
    middle_ref, tok_ref, mask_ref, cot_ref = middle.ref, tok.ref, mask.ref, cot.ref
    mt_ref, gain_ref, s1_ref = mt.ref, gain.ref, s1.ref
    over = padded(rows) - rows
    for half in halves:
        for block in blocks_within(half, rows):
            masked = mask_ref[block] > 0
            one = middle_ref[block]
            back, grad_gain, grad_shift = norm_pull(one, gain_ref[...], acc_ref[block])
            grad_middle = jnp.where(masked, cot_ref[block].astype(F32), 0.0) + back
            gm.near[block] = grad_middle
            grad_branch = (s1_ref[...] * grad_middle).astype(BF16)
            gbr.near[block] = grad_branch
            initial = jnp.where(masked, mt_ref[...], tok_ref[block].astype(F32))
            new = (
                grad_gain,
                grad_shift,
                col_sum(grad_middle * (one - initial)) / s1_ref[...],
                col_sum(grad_branch.astype(F32)),
            )
            total = [a + b for a, b in zip(total, new)]
        if half.stop == padded(rows):
            gm.near[rows:] = jnp.zeros((over, width), F32)
            gbr.near[rows:] = jnp.zeros((over, width), BF16)
        gbr.send(half)
        gm.send(half)
    for i, one in enumerate(total):
        sums.near[i : i + 1] = one
    sums.send()


def back_kernel(
    rows, gbr, wo, ctx, q, k, v, log, n1,
    dq, dk, dv, grads, sums, gc_ref,
):
    me = lax.axis_index("dp")
    cols = dq.near.shape[1]
    gc_ref[...] = nt(gbr.ref[...], wo.ref[...]).astype(BF16)
    store_blocks(me, tn(gbr.ref[...], ctx.ref[...]), grads.near, 3 * cols)
    grads.send((slice(None), slice(None), slice(3 * cols, 4 * cols)))
    attend_back(rows, q.ref, k.ref, v.ref, gc_ref, log.ref, dq.near, dk.near, dv.near)
    for i, one in enumerate((dq, dk, dv)):
        one.send()
        store_blocks(me, tn(n1.ref[...], one.near[...]), grads.near, i * cols)
        grads.send((slice(None), slice(None), slice(i * cols, (i + 1) * cols)))
        if i != 1:
            at = i // 2 * cols
            sums.near[:, at : at + cols] = col_sum(one.near[...].astype(F32))
    sums.send()


def middle_back_kernel(rows, count, *refs):
    first, others = refs[: 2 * count + 7], refs[2 * count + 7 : 2 * count + 14]
    (gm, gbr, sums), outs = refs[2 * count + 14 : 2 * count + 17], refs[2 * count + 17 : 2 * count + 22]
    acc_ref, gc_ref = refs[2 * count + 22 :]
    middle_kernel(rows, count, *first, gm, gbr, sums, acc_ref)
    back_kernel(rows, gbr, *others, *outs, gc_ref)


def input_kernel(rows, *refs):
    grads, weights = refs[:6], list(refs[6:9]) + [Third(refs[9], i) for i in range(3)]
    tok, mask, mt, gain, gm, out, sums, acc_ref = refs[10:]
    width = acc_ref.shape[1]
    halves = halves_of(padded(rows))
    for i, (one, w) in enumerate(zip(grads, weights)):
        for half in halves:
            part = nt(one.ref[half], w.ref[...])
            acc_ref[half] = part if i == 0 else acc_ref[half] + part
    total = [jnp.zeros((1, width), F32)] * 3
    tok_ref, mask_ref, gm_ref, mt_ref, gain_ref = tok.ref, mask.ref, gm.ref, mt.ref, gain.ref
    for half in halves:
        for block in blocks_within(half, rows):
            masked = mask_ref[block] > 0
            initial = jnp.where(masked, mt_ref[...], tok_ref[block].astype(F32))
            back, grad_gain, grad_shift = norm_pull(initial, gain_ref[...], acc_ref[block])
            grad_initial = gm_ref[block] + back
            out.near[block] = jnp.where(masked, 0.0, grad_initial)
            new = (col_sum(jnp.where(masked, grad_initial, 0.0)), grad_gain, grad_shift)
            total = [a + b for a, b in zip(total, new)]
    out.send()
    for i, one in enumerate(total):
        sums.near[i : i + 1] = one
    sums.send()


def output_kernel(rows, count, *refs):
    hiddens, wds = refs[:count], refs[count : 2 * count]
    middle, bd, s2, out, acc_ref = refs[2 * count :]
    halves = halves_of(padded(rows))
    for i, (one, w) in enumerate(zip(hiddens, wds)):
        for half in halves:
            part = nn(one.ref[half], w.ref[...])
            acc_ref[half] = part if i == 0 else acc_ref[half] + part
    middle_ref, bd_ref, s2_ref = middle.ref, bd.ref, s2.ref
    for block in blocks_within(slice(0, rows), rows):
        output = acc_ref[block] + bd_ref[...]
        out.near[block] = (middle_ref[block] + s2_ref[...] * output).astype(BF16)
    out.send()


def shape_of(shape, dtype=BF16):
    return jax.ShapeDtypeStruct(shape, dtype)


def cost(flops, *arrays):
    moved = sum(a.size * a.dtype.itemsize for a in arrays)
    return pl.CostEstimate(flops=flops, bytes_accessed=moved, transcendentals=0)


def without(kernel, at, count):
    def inner(*refs):
        kernel(*refs[:at], *refs[at + count :])

    return inner


def pairs(n, bit):
    return [(i, i ^ (1 << bit)) for i in range(n)]


class Piece:
    def __init__(self, segments, order, used=()):
        self.segments, self.order, self.used = segments, list(order), list(used)
        self.width = sum(width for width, _ in segments)
        self.result = None

    def job(self):
        bit = self.order[0] if self.order else None
        tall = self.segments[0][1][0][0].shape[-2]
        dims = (2,) * (len(self.order) - 1)

        def view(array, bits, place, width):
            one = View(array)
            one.index = tuple(0 if b in self.used else 1 if b == bit else slice(None) for b in bits)
            one.index += (slice(None), slice(place * width, (place + 1) * width))
            one.shape = dims + (tall, width)
            return one

        parts, at = [], 0
        for width, terms in self.segments:
            one = [view(array, bits, place, width) for array, bits, place in terms]
            parts.append((one, slice(at, at + width)))
            at += width
        return parts, shape_of(dims + (tall, self.width), F32 if bit is None else BF16)

    def take(self, sent):
        if not self.order:
            self.result = sent
            return
        bit = self.order.pop(0)
        self.used.append(bit)
        got = lax.ppermute(sent, "dp", pairs(lax.axis_size("dp"), bit))
        bits, at = sorted(self.order, reverse=True), 0
        for width, terms in self.segments:
            terms.append((got, bits, at // width))
            at += width

    def joined(self, other):
        return Piece(self.segments + other.segments, self.order, self.used)


def piece_of(terms, start, width, order):
    bits = sorted(order, reverse=True)
    dims = (2,) * len(bits)
    parts = [(a.reshape(dims + a.shape[1:]), bits, (base + start) // width) for a, base in terms]
    return Piece([(width, parts)], order)


def joining(pieces):
    kept = []
    for piece in pieces:
        if kept and piece.result is None and kept[-1].order == piece.order and piece.used:
            kept[-1] = kept[-1].joined(piece)
        else:
            kept.append(piece)
    return kept


class Sums:
    def __init__(self, same, own, other, bits):
        self.parts, self.own = same + other, same + own
        self.rounds = [bits[i : i + 2] for i in range(0, len(bits), 2)]
        self.stage, self.terms, self.result = 0, [], None

    def job(self):
        width = self.parts[0].shape[1]
        height = -(-sum(p.size for p in self.parts) // (8 * width)) * 8
        packed = {0: self.parts, 1: self.own}.get(self.stage, [])
        places, row, col = [], 0, 0
        for p in packed:
            steps = []
            for at in range(0, p.shape[1], width):
                size = min(width, p.shape[1] - at)
                steps.append(((slice(row, row + p.shape[0]), slice(col, col + size)), slice(at, at + size)))
                col += size
                if col == width:
                    row, col = row + p.shape[0], 0
            places.append(steps)
        return packed, places, self.terms, shape_of((height, width), F32)

    @property
    def last(self):
        return self.stage == len(self.rounds) + 1

    def take(self, sent):
        n = lax.axis_size("dp")
        if self.last:
            self.result = sent
        elif self.stage == 0:
            self.terms = [swap(sent[0])]
        else:
            bits = self.rounds[self.stage - 1]
            self.terms = list(sent)
            for some in range(1, 1 << len(bits)):
                flip = sum(1 << b for i, b in enumerate(bits) if some >> i & 1)
                self.terms.append(lax.ppermute(sent[0], "dp", [(d, d ^ flip) for d in range(n)]))
        self.stage += 1


def exchange(pieces, after, sums=None, carry=None):
    jobs = [p.job() for p in pieces]
    views = [v for parts, _ in jobs for one, _ in parts for v in one]
    shapes = [shape for _, shape in jobs]
    packed, places, terms = [], [], []
    if sums is not None:
        packed, places, terms, shape = sums.job()
        views += [View(a) for a in packed + terms]
        rows = shape.shape[0] if sums.last else 1
        shapes += [shape_of((1, shape.shape[1]), F32)] * rows if sums.last else [shape]
    passed = [] if carry is None else [carry]
    hbm = pl.BlockSpec(memory_space=pl.ANY)
    skipped, n_in, n_out = len(after) + len(passed), len(views), len(shapes)

    def kernel(*refs):
        far_in, far_out = refs[skipped : skipped + n_in], refs[skipped + n_in :][:n_out]
        buffers = list(refs[skipped + n_in + n_out + len(passed) :])
        line = Line(buffers.pop(), n_in + n_out)
        ins = []
        for far, view in zip(far_in, views):
            far = far if view.index is None else far.at[view.index]
            ins.append(Moved(far, buffers.pop(0), line))
        line.begin()
        outs = [Moved(far, buffers.pop(0), line, ()) for far in far_out]
        for (parts, made), out in zip(jobs, outs):
            for one, cols in parts:
                some = [ins.pop(0).ref for _ in one]
                for at in range(max(1, math.prod(made.shape[:-2]))):
                    index, left = [], at
                    for size in made.shape[:-2][::-1]:
                        index.append(left % size)
                        left //= size
                    index = tuple(index[::-1])
                    total = functools.reduce(jnp.add, [r[index].astype(F32) for r in some])
                    out.near[(*index, slice(None), cols)] = total.astype(made.dtype)
            out.send()
        if sums is not None:
            new = outs[len(jobs) :]
            if packed:
                new[0].near[...] = ins[-1].ref[...] if terms else jnp.zeros(shape.shape, F32)
                for one, steps in zip(ins, places):
                    for place, cols in steps:
                        new[0].near[place] += one.ref[:, cols]
                new[0].send()
            else:
                total = functools.reduce(jnp.add, [one.ref[...] for one in ins])
                for i, out in enumerate(new):
                    out.near[...] = total[i : i + 1] if len(new) > 1 else total
                    out.send()
        line.finish()

    outs = pl.pallas_call(
        kernel,
        in_specs=[hbm] * (skipped + n_in),
        out_specs=[hbm] * (n_out + len(passed)),
        out_shape=shapes + [shape_of(p.shape, p.dtype) for p in passed],
        input_output_aliases={len(after): n_out} if passed else {},
        scratch_shapes=[pltpu.VMEM(v.shape, v.array.dtype) for v in views]
        + [pltpu.VMEM(o.shape, o.dtype) for o in shapes]
        + [pltpu.SemaphoreType.DMA((n_in + n_out,))],
        compiler_params=pltpu.CompilerParams(vmem_limit_bytes=EXCHANGE_VMEM),
        cost_estimate=cost(0, *shapes),
        name="exchange",
    )(*after, *passed, *[v.array for v in views])
    for piece, out in zip(pieces, outs):
        piece.take(out)
    if sums is not None:
        sums.take(list(outs[len(jobs) : n_out]))
    sent = list(outs[:n_out])
    return sent if carry is None else (sent, outs[-1])


def swap(array):
    return lax.ppermute(array, "tp", [(0, 1), (1, 0)])


def local_body(
    tokens, masked, cotangent, mask_token, gain_one, shift_one, w_query, w_key, w_value, b_query,
    b_value, w_out, b_out, scale_one, gain_two, shift_two, w_up, b_up, w_down, b_down, scale_two,
):
    rows, width = tokens.shape
    tall = padded(rows)
    half = w_query.shape[1]
    units = w_up.shape[1]
    n = lax.axis_size("dp")
    bits = n.bit_length() - 1
    me = lax.axis_index("dp").astype(jnp.int32).reshape(1)
    biases = jnp.concatenate([b_query, b_value, b_up]).reshape(-1, 128)

    joined2 = swap(jnp.concatenate([w_query, w_key, w_value], axis=1))
    biases2 = swap(biases).reshape(-1)
    wo2 = swap(w_out)
    wu2, wd2 = swap(w_up), swap(w_down)
    row = lambda v: v.reshape(1, -1)
    bq2, bv2, bu2 = row(biases2[:half]), row(biases2[half : 2 * half]), row(biases2[2 * half :])
    bq, bv, bu = row(b_query), row(b_value), row(b_up)
    mt, g1, s1, bo, sc1 = row(mask_token), row(gain_one), row(shift_one), row(b_out), row(scale_one)
    g2, s2, bd, sc2 = row(gain_two), row(shift_two), row(b_down), row(scale_two)
    mask = masked.reshape(rows, 1)

    narrow = shape_of((tall, half))
    wide = shape_of((tall, width))
    attend_flops = 2 * 2 * 256 * SEQ * rows * half // HD
    logs = shape_of(norm_rows(rows, half), F32)
    normed, q, k, v, ctx, log = moved_call(
        functools.partial(first_kernel, rows),
        [wide, narrow, narrow, narrow, narrow, logs],
        (tokens, mask, mt, g1, s1, w_query, w_key, w_value, bq, bv),
        6 * rows * width * half + attend_flops,
        6,
        name="first",
        waves=[[(i, 0) for i in range(5)]],
    )
    tall_f32 = shape_of((tall, width), F32)
    scratch = [pltpu.VMEM((tall, width), F32)]
    one_row = shape_of((1, width), F32)
    q2, k2, v2, ctx2, log2, middle, normed2, go, sum_go = moved_call(
        functools.partial(second_kernel, rows),
        [narrow, narrow, narrow, narrow, logs, tall_f32, wide, wide, one_row],
        (normed, joined2, bq2, bv2, ctx, w_out, wo2, bo, sc1, g2, s2, tokens, mask, mt, cotangent, sc2),
        10 * rows * width * half + attend_flops,
        12,
        scratch=scratch,
        name="second",
        cuts={1: (1, 3)},
        waves=[[(0, 0), (1, 0), (2, 0)], [(1, 1), (1, 2), (3, 0)]],
    )

    natural = tuple(range(bits))
    by_x, by_y = natural, natural[1:2] + natural[0:1] + natural[2:]
    by_z = natural[2 % bits :] + natural[: 2 % bits]

    part = units // 2
    chunk = min(512, part)
    hiddens, gps, ups, downs = [], [], [], []

    def feed(weights, first, size, after=()):
        w_up, w_down, b_up = weights
        count = size // chunk
        hidden, gp, grads, sums, scale_sum = moved_call(
            functools.partial(feed_kernel, chunk),
            [
                shape_of((tall, size)),
                shape_of((tall, size)),
                shape_of((n, width // n, 2 * size)),
                shape_of((1, size), F32),
                one_row,
            ],
            (normed2, View(w_up, 1, first, size), go, View(w_down, 0, first, size), View(b_up, 1, first, size)),
            8 * tall * width * size,
            4 * count + 2,
            name="feed",
            after=after,
            cuts={1: (1, count), 3: (0, count)},
            waves=[[(0, 0), (1, 0)], [(2, 0), (3, 0), (4, 0)]],
        )
        hiddens.append(hidden)
        gps.append(gp)
        ups.append(View(w_up, 1, first, size))
        downs.append(View(w_down, 0, first, size))
        scale_sums.append(scale_sum)
        return grads, sums

    def in_three(size, *terms):
        return [
            piece_of(terms, 0, size * 3 // 8, by_x),
            piece_of(terms, size * 3 // 8, size * 3 // 8, by_y),
            piece_of(terms, size * 3 // 4, size // 4, by_z),
        ]

    def in_two(size, *terms):
        return [piece_of(terms, i * size // 2, size // 2, order) for i, order in enumerate((by_x, by_y))]

    mine, other = (w_up, w_down, bu), (wu2, wd2, bu2)
    scale_sums = []
    theirs, sums_up2 = feed(other, 0, units)
    theirs = swap(theirs)
    own, sums_up_a = feed(mine, 0, part, [sums_up2])
    a = in_three(2 * part, (own, 0), (theirs, 0))
    sent = exchange(a, [sums_up_a])
    own, sums_up_b = feed(mine, part, part, sent)
    b = in_two(2 * part, (own, 0), (theirs, 2 * part))
    sent = exchange(a + b, [sums_up_b])
    a = joining(a)

    back_outs = [narrow, narrow, narrow, shape_of((n, width // n, 4 * half)), shape_of((1, 2 * half), F32)]
    back_flops = 10 * rows * width * half + 3 * attend_flops
    back_scratch = [pltpu.VMEM((tall, half), BF16)]
    gm, gbr, sums_two, dq2, dk2, dv2, gw2, sums_b2 = moved_call(
        functools.partial(middle_back_kernel, rows, len(gps)),
        [tall_f32, wide, shape_of((4, width), F32)] + back_outs,
        (*gps, *ups, middle, tokens, mask, mt, cotangent, g2, sc1, wo2, ctx2, q2, k2, v2, log2, normed),
        8 * tall * width * part + back_flops,
        13,
        scratch=scratch + back_scratch,
        name="middle",
        after=sent,
        waves=[[(i, 0), (len(gps) + i, 0)] for i in range(len(gps))],
    )
    sent, gw2 = exchange(a + b, [sums_b2], carry=gw2)
    b = joining(b)
    gw2 = swap(gw2)

    def back(wo, ctx, q, k, v, log, after):
        return moved_call(
            functools.partial(back_kernel, rows),
            back_outs,
            (gbr, wo, ctx, q, k, v, log, normed),
            back_flops,
            8,
            scratch=back_scratch,
            name="back",
            after=after,
            waves=[[(0, 0), (1, 0)], [(2, 0)]],
        )

    dq, dk, dv, gw, sums_b = back(w_out, ctx, q, k, v, log, sent)
    c = in_two(4 * half, (gw, 0), (gw2, 0))
    sent = exchange(c + b + a, [sums_b])

    grad_tokens, sums_one = moved_call(
        functools.partial(input_kernel, rows),
        [shape_of((rows, width), F32), shape_of((3, width), F32)],
        (dq, dk, dv, dq2, dk2, dv2, w_query, w_key, w_value, joined2, tokens, mask, mt, g1, gm),
        12 * rows * width * half,
        2,
        scratch=scratch,
        cuts={9: (1, 3)},
        waves=[[(0, 0), (6, 0)], [(1, 0), (7, 0)], [(2, 0), (8, 0), (3, 0), (9, 0)]],
        name="input",
        after=sent,
    )
    same = [sums_one, sums_two, sum_go, *scale_sums]
    sums = Sums(same, [sums_b, sums_up_a, sums_up_b], [sums_b2, sums_up2], list(natural))
    sent = exchange(c + b + a, [sums_one], sums=sums)
    c = joining(c)
    block_out = moved_call(
        functools.partial(output_kernel, rows, len(hiddens)),
        [shape_of((rows, width))],
        (*hiddens, *downs, middle, bd, sc2),
        8 * tall * width * part,
        1,
        scratch=scratch,
        waves=[[(i, 0), (len(gps) + i, 0)] for i in range(len(gps))],
        name="output",
        after=sent,
    )[0]
    last, open_pieces = block_out, c + b
    while sums.result is None:
        open_pieces = [piece for piece in open_pieces if piece.result is None]
        last = exchange(open_pieces, [last], sums=sums)[-1]

    def columns(group):
        return jnp.concatenate([piece.result for piece in group], axis=1)

    feed_grads = jnp.concatenate([columns(a), columns(b)], axis=1).reshape(-1, units // chunk, 2, chunk)
    grad_w_down = feed_grads[:, :, 0].reshape(-1, units).T
    grad_w_up = feed_grads[:, :, 1].reshape(-1, units)
    attention = columns(c)

    rep = [one.reshape(-1) for one in sums.result[:8]]
    (grad_mask_token, grad_gain_one, grad_shift_one, grad_gain_two, grad_shift_two, grad_scale_one,
     grad_b_out, grad_b_down) = rep
    scale_total = sum(one.reshape(-1) for one in sums.result[8 : 8 + len(scale_sums)])
    grad_scale_two = (scale_total + b_down * grad_b_down) / scale_two
    own = jnp.concatenate(sums.result[8 + len(scale_sums) :], axis=1).reshape(-1)
    return (
        block_out,
        grad_tokens,
        grad_mask_token,
        grad_gain_one,
        grad_shift_one,
        attention[:, :half],
        attention[:, half : 2 * half],
        attention[:, 2 * half : 3 * half],
        own[:half],
        own[half : 2 * half],
        attention[:, 3 * half :].T,
        grad_b_out,
        grad_scale_one,
        grad_gain_two,
        grad_shift_two,
        grad_w_up,
        own[2 * half : 2 * half + units],
        grad_w_down,
        grad_b_down,
        grad_scale_two,
    )


def solution(mesh):
    placed = (
        P(("dp", "tp"), None),
        P(("dp", "tp")),
        P(("dp", "tp"), None),
        P(),
        P(),
        P(),
        P(None, "tp"),
        P(None, "tp"),
        P(None, "tp"),
        P("tp"),
        P("tp"),
        P("tp", None),
        P(),
        P(),
        P(),
        P(),
        P(None, "tp"),
        P("tp"),
        P("tp", None),
        P(),
        P(),
    )
    fits = mesh.shape["tp"] == 2 and mesh.shape["dp"].bit_count() == 1
    return jax.shard_map(
        local_body if fits else gathered_body,
        mesh=mesh,
        in_specs=placed,
        out_specs=(
            P(("dp", "tp"), None),
            P(("dp", "tp"), None),
            P(),
            P(),
            P(),
            P("dp", "tp"),
            P("dp", "tp"),
            P("dp", "tp"),
            P("tp"),
            P("tp"),
            P("tp", "dp"),
            P(),
            P(),
            P(),
            P(),
            P("dp", "tp"),
            P("tp"),
            P("tp", "dp"),
            P(),
            P(),
        ),
        check_vma=False,
    )
```

```python
import functools
import math

import jax
import jax.numpy as jnp
from jax import lax
from jax.experimental import pallas as pl
from jax.experimental.pallas import tpu as pltpu
from jax.sharding import PartitionSpec as P

SEQ = 197
HD = 64
PAIR = 2 * HD
EPSILON = 1e-06
BF16 = jnp.bfloat16
F32 = jnp.float32
MIB = 2**20
LOWEST = -1e30
KERNEL_VMEM = 64 * MIB
EXCHANGE_VMEM = 64 * MIB

def layer_norm(rows_in, gain_vec, shift_vec):
    center = rows_in - jnp.mean(rows_in, axis=-1, keepdims=True)
    spread = jnp.mean(center * center, axis=-1, keepdims=True)
    return center * lax.rsqrt(spread + EPSILON) * gain_vec + shift_vec


def norm_backward(rows_in, gain_vec, shift_vec, grad_rows):
    unused, pull = jax.vjp(layer_norm, rows_in, gain_vec, shift_vec)
    return pull(grad_rows)


def gelu_exact(values):
    return jax.nn.gelu(values, approximate=False)


def product(left, right):
    return jnp.dot(left, right, preferred_element_type=jnp.float32)


def times_transposed(left, right):
    return lax.dot_general(
        left, right, (((1,), (1,)), ((), ())), preferred_element_type=jnp.float32
    )


def transposed_times(left, right):
    return lax.dot_general(
        left, right, (((0,), (0,)), ((), ())), preferred_element_type=jnp.float32
    )


def attend_forward(queries, key_rows, values, factor):
    scores = (
        jnp.einsum("iqhd,ikhd->ihqk", queries, key_rows, preferred_element_type=jnp.float32)
        * factor
    )
    row_max = jnp.max(scores, axis=-1, keepdims=True)
    raised = jnp.exp(scores - row_max)
    sum_exp = jnp.sum(raised, axis=-1, keepdims=True)
    probs_low = (raised / sum_exp).astype(jnp.bfloat16)
    context = jnp.einsum("ihqk,ikhd->iqhd", probs_low, values, preferred_element_type=jnp.float32)
    return (context, row_max + jnp.log(sum_exp))


def attend_backward(queries, key_rows, values, log_total, grad_context, factor):
    scores = (
        jnp.einsum("iqhd,ikhd->ihqk", queries, key_rows, preferred_element_type=jnp.float32)
        * factor
    )
    probs = jnp.exp(scores - log_total)
    grad_probs = jnp.einsum(
        "iqhd,ikhd->ihqk", grad_context, values, preferred_element_type=jnp.float32
    )
    inner = jnp.sum(grad_probs * probs, axis=-1, keepdims=True)
    grad_scores = (probs * (grad_probs - inner)).astype(jnp.bfloat16)
    grad_queries = (
        jnp.einsum("ihqk,ikhd->iqhd", grad_scores, key_rows, preferred_element_type=jnp.float32)
        * factor
    )
    grad_keys = (
        jnp.einsum("ihqk,iqhd->ikhd", grad_scores, queries, preferred_element_type=jnp.float32)
        * factor
    )
    grad_values = jnp.einsum(
        "ihqk,iqhd->ikhd",
        probs.astype(jnp.bfloat16),
        grad_context,
        preferred_element_type=jnp.float32,
    )
    return (grad_queries, grad_keys, grad_values)


def gathered_body(
    tokens,
    masked,
    cotangent,
    mask_token,
    gain_one,
    shift_one,
    w_query,
    w_key,
    w_value,
    b_query,
    b_value,
    w_out,
    b_out,
    scale_one,
    gain_two,
    shift_two,
    w_up,
    b_up,
    w_down,
    b_down,
    scale_two,
):
    local_cols = w_query.shape[1]
    local_heads = local_cols // HD
    factor = 1.0 / math.sqrt(HD)
    chosen = (masked > 0)[:, None]
    initial = jnp.where(chosen, mask_token[None, :], tokens.astype(jnp.float32))
    normed = layer_norm(initial, gain_one, shift_one).astype(jnp.bfloat16)
    w_joined = jnp.concatenate([w_query, w_key, w_value], axis=1)
    b_joined = jnp.concatenate([b_query, jnp.zeros_like(b_query), b_value])
    gathered = lax.all_gather(normed, "tp", axis=0, tiled=True)
    joined = (product(gathered, w_joined) + b_joined).astype(jnp.bfloat16)
    group_rows = gathered.shape[0]
    head_shape = (group_rows // SEQ, SEQ, local_heads, HD)
    queries = joined[:, :local_cols].reshape(head_shape)
    key_rows = joined[:, local_cols : 2 * local_cols].reshape(head_shape)
    values = joined[:, 2 * local_cols :].reshape(head_shape)
    context, log_total = attend_forward(queries, key_rows, values, factor)
    context = context.reshape(group_rows, local_cols).astype(jnp.bfloat16)
    branch = (
        lax.psum_scatter(
            product(context, w_out).astype(jnp.bfloat16), "tp", scatter_dimension=0, tiled=True
        ).astype(jnp.float32)
        + b_out
    )
    middle = initial + scale_one * branch
    normed_two = layer_norm(middle, gain_two, shift_two).astype(jnp.bfloat16)
    gathered_two = lax.all_gather(normed_two, "tp", axis=0, tiled=True)
    pre_act = product(gathered_two, w_up) + b_up
    hidden = gelu_exact(pre_act).astype(jnp.bfloat16)
    output = (
        lax.psum_scatter(
            product(hidden, w_down).astype(jnp.bfloat16), "tp", scatter_dimension=0, tiled=True
        ).astype(jnp.float32)
        + b_down
    )
    block_out = (middle + scale_two * output).astype(jnp.bfloat16)
    grad_block = cotangent.astype(jnp.float32) * chosen.astype(jnp.float32)
    grad_output = (scale_two * grad_block).astype(jnp.bfloat16)
    grad_scale_two = jnp.sum(grad_block * output, axis=0)
    grad_b_down = jnp.sum(grad_output.astype(jnp.float32), axis=0)
    portion = lax.all_gather(grad_output, "tp", axis=0, tiled=True)
    grad_hidden = times_transposed(portion, w_down)
    grad_w_down = transposed_times(hidden, portion)
    grad_hidden, grad_w_down = (grad_hidden, grad_w_down)
    unused, gelu_pull = jax.vjp(gelu_exact, pre_act)
    grad_pre = gelu_pull(grad_hidden)[0].astype(jnp.bfloat16)
    grad_b_up = jnp.sum(grad_pre.astype(jnp.float32), axis=0)
    grad_normed_two = lax.psum_scatter(
        times_transposed(grad_pre, w_up).astype(jnp.bfloat16), "tp", scatter_dimension=0, tiled=True
    ).astype(jnp.float32)
    grad_w_up = transposed_times(lax.all_gather(normed_two, "tp", axis=0, tiled=True), grad_pre)
    grad_middle_norm, grad_gain_two, grad_shift_two = norm_backward(
        middle, gain_two, shift_two, grad_normed_two
    )
    grad_middle = grad_block + grad_middle_norm
    grad_branch = (scale_one * grad_middle).astype(jnp.bfloat16)
    grad_scale_one = jnp.sum(grad_middle * branch, axis=0)
    grad_b_out = jnp.sum(grad_branch.astype(jnp.float32), axis=0)
    portion = lax.all_gather(grad_branch, "tp", axis=0, tiled=True)
    grad_context = times_transposed(portion, w_out)
    grad_w_out = transposed_times(context, portion)
    grad_context, grad_w_out = (grad_context, grad_w_out)
    grad_context = grad_context.astype(jnp.bfloat16).reshape(head_shape)
    grad_queries, grad_keys, grad_values = attend_backward(
        queries, key_rows, values, log_total, grad_context, factor
    )
    grad_joined = jnp.concatenate(
        [
            grad_queries.reshape(group_rows, local_cols),
            grad_keys.reshape(group_rows, local_cols),
            grad_values.reshape(group_rows, local_cols),
        ],
        axis=1,
    ).astype(jnp.bfloat16)
    grad_b_query = jnp.sum(grad_joined[:, :local_cols].astype(jnp.float32), axis=0)
    grad_b_value = jnp.sum(grad_joined[:, 2 * local_cols :].astype(jnp.float32), axis=0)
    grad_normed = lax.psum_scatter(
        times_transposed(grad_joined, w_joined).astype(jnp.bfloat16),
        "tp",
        scatter_dimension=0,
        tiled=True,
    ).astype(jnp.float32)
    grad_w_joined = transposed_times(lax.all_gather(normed, "tp", axis=0, tiled=True), grad_joined)
    grad_initial_norm, grad_gain_one, grad_shift_one = norm_backward(
        initial, gain_one, shift_one, grad_normed
    )
    grad_initial = grad_middle + grad_initial_norm
    grad_tokens = jnp.where(chosen, 0.0, grad_initial)
    grad_mask_token = jnp.sum(jnp.where(chosen, grad_initial, 0.0), axis=0)
    (
        grad_mask_token,
        grad_gain_one,
        grad_shift_one,
        grad_b_out,
        grad_scale_one,
        grad_gain_two,
        grad_shift_two,
        grad_b_down,
        grad_scale_two,
    ) = lax.psum(
        (
            grad_mask_token,
            grad_gain_one,
            grad_shift_one,
            grad_b_out,
            grad_scale_one,
            grad_gain_two,
            grad_shift_two,
            grad_b_down,
            grad_scale_two,
        ),
        ("dp", "tp"),
    )
    grad_b_query, grad_b_value, grad_b_up = lax.psum((grad_b_query, grad_b_value, grad_b_up), "dp")
    grad_w_joined, grad_w_out, grad_w_up, grad_w_down = (
        lax.psum_scatter(
            grad_w_joined.astype(jnp.bfloat16), "dp", scatter_dimension=0, tiled=True
        ).astype(jnp.float32),
        lax.psum_scatter(
            grad_w_out.astype(jnp.bfloat16), "dp", scatter_dimension=1, tiled=True
        ).astype(jnp.float32),
        lax.psum_scatter(
            grad_w_up.astype(jnp.bfloat16), "dp", scatter_dimension=0, tiled=True
        ).astype(jnp.float32),
        lax.psum_scatter(
            grad_w_down.astype(jnp.bfloat16), "dp", scatter_dimension=1, tiled=True
        ).astype(jnp.float32),
    )
    grad_w_query = grad_w_joined[:, :local_cols]
    grad_w_key = grad_w_joined[:, local_cols : 2 * local_cols]
    grad_w_value = grad_w_joined[:, 2 * local_cols :]
    return (
        block_out,
        grad_tokens,
        grad_mask_token,
        grad_gain_one,
        grad_shift_one,
        grad_w_query,
        grad_w_key,
        grad_w_value,
        grad_b_query,
        grad_b_value,
        grad_w_out,
        grad_b_out,
        grad_scale_one,
        grad_gain_two,
        grad_shift_two,
        grad_w_up,
        grad_b_up,
        grad_w_down,
        grad_b_down,
        grad_scale_two,
    )


def nn(left, right):
    return lax.dot_general(left, right, (((1,), (0,)), ((), ())), preferred_element_type=F32)


def nt(left, right):
    return lax.dot_general(left, right, (((1,), (1,)), ((), ())), preferred_element_type=F32)


def tn(left, right):
    return lax.dot_general(left, right, (((0,), (0,)), ((), ())), preferred_element_type=F32)


def padded(rows):
    return -(-rows // 32) * 32


def windows(rows):
    found = []
    for image in range(rows // SEQ):
        first = image * SEQ
        start = first // 16 * 16
        found.append((start, -(-(first - start + SEQ) // 16) * 16, first - start))
    return found


def row_blocks(total, size=160):
    return [slice(s, min(s + size, total)) for s in range(0, total, size)]


def inside(shape, axis, offset):
    at = lax.broadcasted_iota(jnp.int32, shape, axis)
    return (at >= offset) & (at < offset + SEQ)


def col_sum(values):
    return jnp.sum(values, axis=0, keepdims=True)


def row_mean(values):
    return jnp.mean(values, axis=-1, keepdims=True)


def moments(rows_in):
    center = rows_in - row_mean(rows_in)
    return center, lax.rsqrt(row_mean(center * center) + EPSILON)


def norm_pull(rows_in, gain, grad):
    center, inv = moments(rows_in)
    hat = center * inv
    scaled = grad * gain
    back = (scaled - row_mean(scaled) - hat * row_mean(scaled * hat)) * inv
    return back, col_sum(grad * hat), col_sum(grad)


def gelu_parts(v):
    cdf = 0.5 + 0.5 * lax.erf(v * math.sqrt(0.5))
    return cdf, v * (jnp.exp(-0.5 * (v * v)) * (1.0 / math.sqrt(2.0 * math.pi)))


def rows_outside(values, offset, fill):
    size = values.shape[0]

    def edge(part, base):
        at = lax.broadcasted_iota(jnp.int32, part.shape, 0) + base
        return jnp.where((at >= offset) & (at < offset + SEQ), part, fill)

    head = edge(values[:16], 0) if offset else values[:16]
    return jnp.concatenate([head, values[16:-32], edge(values[-32:], size - 32)], axis=0)


def one_head(shape, head):
    return (lax.broadcasted_iota(jnp.int32, shape, 1) < HD) == (head == 0)


def in_turn(rows, lead, begin, finish):
    units = [(window, head) for window in windows(rows) for head in (0, 1)]
    begun = [begin(*unit) for unit in units[:lead]]
    for i, unit in enumerate(units):
        if i + lead < len(units):
            begun.append(begin(*units[i + lead]))
        finish(i, *unit, begun[i])
        begun[i] = None


def norm_rows(rows, cols):
    return (cols // HD * (rows // SEQ), 256)


def attend(rows, q_ref, k_ref, v_ref, ctx_ref, log_ref):
    ctx_ref[padded(rows) - 32 :, :] = jnp.zeros((32, ctx_ref.shape[1]), BF16)
    count = 2 * (rows // SEQ)

    def one_pair(pair, carry):
        lanes = pl.ds(pl.multiple_of(pair * PAIR, PAIR), PAIR)
        halves = {}

        def begin(window, head):
            start, size, _ = window
            win = slice(start, start + size)
            k = k_ref[win, lanes]
            return nt(jnp.where(one_head(k.shape, head), k, jnp.zeros_like(k)), q_ref[win, lanes])

        def finish(i, window, head, scores):
            start, size, offset = window
            win = slice(start, start + size)
            scores = rows_outside(scores, offset, LOWEST)
            top = jnp.max(scores, axis=0, keepdims=True)
            raised = jnp.exp(scores - top)
            total = jnp.sum(raised, axis=0, keepdims=True)
            out = tn(v_ref[win, lanes], raised.astype(BF16))
            halves[head] = out[head * HD : (head + 1) * HD] * (1.0 / total)
            log_ref[pl.ds(pair * count + i, 1), :size] = top + jnp.log(total)
            if head == 1:
                both = jnp.concatenate([halves[0], halves[1]], axis=0).T.astype(BF16)
                keep = inside((size, PAIR), 0, offset)
                ctx_ref[win, lanes] = jnp.where(keep, both, ctx_ref[win, lanes])

        in_turn(rows, 2, begin, finish)
        return carry

    lax.fori_loop(0, q_ref.shape[1] // PAIR, one_pair, 0)


def attend_back(rows, q_ref, k_ref, v_ref, gc_ref, log_ref, dq_ref, dk_ref, dv_ref):
    for ref in (dq_ref, dk_ref, dv_ref):
        ref[padded(rows) - 32 :, :] = jnp.zeros((32, ref.shape[1]), BF16)
    factor = 1.0 / math.sqrt(HD)
    count = 2 * (rows // SEQ)

    def one_pair(pair, carry):
        lanes = pl.ds(pl.multiple_of(pair * PAIR, PAIR), PAIR)
        halves = {}

        def begin(window, head):
            start, size, offset = window
            win = slice(start, start + size)
            zero = jnp.zeros((size, PAIR), BF16)
            mine = one_head(zero.shape, head)
            k = jnp.where(mine, k_ref[win, lanes], zero)
            v = jnp.where(mine, v_ref[win, lanes], zero)
            gc = jnp.where(inside(zero.shape, 0, offset), gc_ref[win, lanes], zero)
            q = q_ref[win, lanes]
            return nt(k, q), nt(v, gc), k, q, gc

        def finish(i, window, head, begun):
            start, size, offset = window
            win = slice(start, start + size)
            scores, grad_probs, k, q, gc = begun
            scores = rows_outside(scores, offset, LOWEST)
            probs = jnp.exp(scores - log_ref[pl.ds(pair * count + i, 1), :size])
            inner = jnp.sum(grad_probs * probs, axis=0, keepdims=True)
            grad_scores = (probs * (grad_probs - inner)).astype(BF16)
            halves[head] = tn(grad_scores, k), nn(grad_scores, q), nn(probs.astype(BF16), gc)
            if head == 1:
                keep = inside((size, PAIR), 0, offset)
                first = one_head((size, PAIR), 0)
                low, high = halves[0], halves[1]
                for ref, new in (
                    (dq_ref, (low[0] + high[0]) * factor),
                    (dk_ref, jnp.where(first, low[1], high[1])),
                    (dv_ref, jnp.where(first, low[2], high[2])),
                ):
                    ref[win, lanes] = jnp.where(keep, new.astype(BF16), ref[win, lanes])

        in_turn(rows, 2, begin, finish)
        return carry

    lax.fori_loop(0, q_ref.shape[1] // PAIR, one_pair, 0)


class Moved:
    def __init__(self, far, near, line, pieces=(None,)):
        self.far, self.near, self.line, self.pieces = far, near, line, pieces
        self.copies = [line.add(*self.views(p)) for p in pieces]

    def views(self, p):
        return (self.far, self.near) if p is None else (self.far.at[p], self.near.at[p])

    def part(self, i):
        self.line.wait(self.copies[i])
        return self.views(self.pieces[i])[1]

    @property
    def ref(self):
        for copy in self.copies:
            self.line.wait(copy)
        return self.near

    def send(self, p=None):
        far, near = self.views(p)
        self.line.send(near, far)


class Line:
    def __init__(self, sems, count):
        self.sems, self.free = sems, iter(range(count))
        self.queue, self.waves, self.started, self.waited, self.sent = [], [], 0, set(), []

    def copy(self, source, target):
        return pltpu.make_async_copy(source, target, self.sems.at[next(self.free)])

    def add(self, source, target):
        self.queue.append(self.copy(source, target))
        return len(self.queue) - 1

    def begin(self, waves=()):
        first = [i for wave in waves for i in wave]
        rest = [i for i in range(len(self.queue)) if i not in first]
        self.waves = [list(wave) for wave in waves] + [rest]
        self.start_to(1)

    def start_to(self, stop):
        while self.started < min(stop, len(self.waves)):
            for i in self.waves[self.started]:
                self.queue[i].start()
            self.started += 1

    def wait(self, i):
        if i in self.waited:
            return
        wave = next(k for k, some in enumerate(self.waves) if i in some)
        self.start_to(wave + 1)
        self.queue[i].wait()
        self.waited.add(i)
        self.start_to(wave + 2)

    def send(self, source, target):
        copy = self.copy(source, target)
        copy.start()
        self.sent.append(copy)

    def finish(self):
        for i in range(len(self.queue)):
            self.wait(i)
        for copy in self.sent:
            copy.wait()


class View:
    def __init__(self, array, axis=0, start=0, size=None):
        self.array, self.shape, self.index = array, array.shape, None
        if size is not None:
            p = slice(start, start + size)
            self.index = (slice(None),) * axis + (p,)
            self.shape = tuple(size if i == axis else n for i, n in enumerate(array.shape))


def cut_in(size, axis, count):
    step = size // count
    spans = [slice(i * step, (i + 1) * step) for i in range(count)]
    return [(slice(None),) * axis + (p,) for p in spans]


def moved_call(kernel, outs, args, flops, sends, scratch=(), name=None, after=(), cuts=None, waves=()):
    hbm = pl.BlockSpec(memory_space=pl.ANY)
    cuts = cuts or {}
    views = [a if isinstance(a, View) else View(a) for a in args]
    args = [view.array for view in views]
    n_in, n_out = len(args), len(outs)
    pieces = [
        cut_in(v.shape[cuts[i][0]], *cuts[i]) if i in cuts else [None] for i, v in enumerate(views)
    ]
    n_sems = sum(len(p) for p in pieces) + sends
    buffers = [pltpu.VMEM(v.shape, v.array.dtype) for v in views]
    buffers += [pltpu.VMEM(o.shape, o.dtype) for o in outs]

    def inner(*refs):
        refs = refs[len(after) :]
        far_in, far_out, rest = refs[:n_in], refs[n_in : n_in + n_out], list(refs[n_in + n_out :])
        line = Line(rest.pop(), n_sems)
        ins = []
        for far, view, p in zip(far_in, views, pieces):
            far = far if view.index is None else far.at[view.index]
            ins.append(Moved(far, rest.pop(0), line, p))
        line.begin([[ins[i].copies[j] for i, j in wave] for wave in waves])
        results = [Moved(far, rest.pop(0), line, ()) for far in far_out]
        kernel(*ins, *results, *rest)
        line.finish()

    return pl.pallas_call(
        inner,
        in_specs=[hbm] * (len(after) + n_in),
        out_specs=[hbm] * n_out,
        out_shape=outs,
        scratch_shapes=buffers + list(scratch) + [pltpu.SemaphoreType.DMA((n_sems,))],
        compiler_params=pltpu.CompilerParams(vmem_limit_bytes=KERNEL_VMEM),
        cost_estimate=cost(flops, *args, *outs),
        name=name,
    )(*after, *args)


def halves_of(tall):
    middle = tall // 2 // 16 * 16
    return [slice(0, middle), slice(middle, tall)]


def blocks_within(part, rows, size=80):
    stop = min(part.stop, rows)
    return [slice(s, min(s + size, stop)) for s in range(part.start, stop, size)]


def first_kernel(
    rows, tok, mask, mt, gain, shift, wq, wk, wv, bq, bv,
    normed, q, k, v, ctx, log,
):
    normed_ref = normed.near
    tok_ref, mask_ref = tok.ref, mask.ref
    mt_ref, gain_ref, shift_ref = mt.ref, gain.ref, shift.ref
    for block in blocks_within(slice(0, rows), rows):
        initial = jnp.where(mask_ref[block] > 0, mt_ref[...], tok_ref[block].astype(F32))
        center, inv = moments(initial)
        normed_ref[block] = (center * inv * gain_ref[...] + shift_ref[...]).astype(BF16)
    over = padded(rows) - rows
    normed_ref[rows:] = jnp.zeros((over, normed_ref.shape[1]), BF16)
    normed.send()
    project(normed_ref, [wq, wk, wv], bq, bv, q, k, v)
    attend(rows, q.near, k.near, v.near, ctx.near, log.near)
    ctx.send()
    log.send()


def project(normed_ref, weights, bq, bv, q, k, v):
    scale = BF16(1.0 / math.sqrt(HD))
    wq, wk, wv = weights
    q.near[...] = (nn(normed_ref[...], wq.ref[...]) + bq.ref[...]).astype(BF16) * scale
    q.send()
    k.near[...] = nn(normed_ref[...], wk.ref[...]).astype(BF16)
    k.send()
    v.near[...] = (nn(normed_ref[...], wv.ref[...]) + bv.ref[...]).astype(BF16)
    v.send()


class Third:
    def __init__(self, moved, i):
        self.moved, self.i = moved, i

    @property
    def ref(self):
        return self.moved.part(self.i)


def second_kernel(
    rows, normed, joined, bq, bv, ctx, wo, wo2, bo,
    s1, gain, shift, tok, mask, mt, cot, s2,
    q, k, v, ctx2, log, middle, normed2, go, sums, acc_ref,
):
    project(normed.ref, [Third(joined, i) for i in range(3)], bq, bv, q, k, v)
    attend(rows, q.near, k.near, v.near, ctx2.near, log.near)
    ctx2.send()
    log.send()
    over = padded(rows) - rows
    width = acc_ref.shape[1]
    total = jnp.zeros((1, width), F32)
    ctx_ref, wo_ref, wo2_ref = ctx.ref, wo.ref, wo2.ref
    tok_ref, mask_ref, cot_ref = tok.ref, mask.ref, cot.ref
    bo_ref, s1_ref, gain_ref, shift_ref, mt_ref, s2_ref = (v.ref for v in (bo, s1, gain, shift, mt, s2))
    for half in halves_of(padded(rows)):
        acc_ref[half] = nn(ctx_ref[half], wo_ref[...]) + nn(ctx2.near[half], wo2_ref[...])
    for half in halves_of(padded(rows)):
        for block in blocks_within(half, rows):
            masked = mask_ref[block] > 0
            initial = jnp.where(masked, mt_ref[...], tok_ref[block].astype(F32))
            one = initial + s1_ref[...] * (acc_ref[block] + bo_ref[...])
            middle.near[block] = one
            center, inv = moments(one)
            normed2.near[block] = (center * inv * gain_ref[...] + shift_ref[...]).astype(BF16)
            grad_out = jnp.where(masked, cot_ref[block].astype(F32), 0.0) * s2_ref[...]
            grad_out = grad_out.astype(BF16)
            go.near[block] = grad_out
            total += col_sum(grad_out.astype(F32))
        if half.stop == padded(rows):
            middle.near[rows:] = jnp.zeros((over, width), F32)
            normed2.near[rows:] = jnp.zeros((over, width), BF16)
            go.near[rows:] = jnp.zeros((over, width), BF16)
        for one in (normed2, go, middle):
            one.send(half)
    sums.near[...] = total
    sums.send()


def feed_kernel(chunk, n2, wu, go, wd, bu, hidden, gp, grads, sums, scale_sum):
    me = lax.axis_index("dp")
    cols = hidden.near.shape[1]
    width = n2.near.shape[1]
    lanes = None
    for i in range(cols // chunk):
        at = slice(i * chunk, (i + 1) * chunk)
        pre = nn(n2.ref[...], wu.part(i)[...]) + bu.ref[:, at]
        grad_hidden = nt(go.ref[...], wd.part(i)[...])
        cdf, slope = gelu_parts(pre)
        new_hidden = (pre * cdf).astype(BF16)
        grad_pre = (grad_hidden * (cdf + slope)).astype(BF16)
        hidden.near[:, at] = new_hidden
        gp.near[:, at] = grad_pre
        hidden.send((slice(None), at))
        gp.send((slice(None), at))
        sums.near[:, at] = col_sum(grad_pre.astype(F32))
        down = tn(go.ref[...], new_hidden)
        weighed = down * wd.part(i)[...].T.astype(F32)
        for k in range(0, chunk, 128):
            part = weighed[:, k : k + 128]
            lanes = part if lanes is None else lanes + part
        for j, grad in enumerate((down, tn(n2.ref[...], grad_pre))):
            base = (2 * i + j) * chunk
            store_blocks(me, grad, grads.near, base)
            grads.send((slice(None), slice(None), slice(base, base + chunk)))
    sums.send()
    scale_sum.near[...] = col_sum(lanes.T)
    scale_sum.send()


def store_blocks(me, product_rows, out_ref, at):
    parts, size, _ = out_ref.shape
    cols = product_rows.shape[1]
    for b in range(parts):
        out_ref[b ^ me, :, at : at + cols] = product_rows[b * size : (b + 1) * size].astype(BF16)


def in_pieces(*groups):
    for some in zip(*groups):
        for j in range(len(some[0].pieces)):
            yield [functools.partial(one.part, j) for one in some]


def middle_kernel(rows, count, *refs):
    gps, wus = refs[:count], refs[count : 2 * count]
    middle, tok, mask, mt, cot, gain, s1 = refs[2 * count : 2 * count + 7]
    gm, gbr, sums, acc_ref = refs[2 * count + 7 :]
    width = acc_ref.shape[1]
    total = [jnp.zeros((1, width), F32)] * 4
    halves = halves_of(padded(rows))
    for i, (one, w) in enumerate(in_pieces(gps, wus)):
        for half in halves:
            part = nt(one()[half], w()[...])
            acc_ref[half] = part if i == 0 else acc_ref[half] + part
    middle_ref, tok_ref, mask_ref, cot_ref = middle.ref, tok.ref, mask.ref, cot.ref
    mt_ref, gain_ref, s1_ref = mt.ref, gain.ref, s1.ref
    over = padded(rows) - rows
    for half in halves:
        for block in blocks_within(half, rows):
            masked = mask_ref[block] > 0
            one = middle_ref[block]
            back, grad_gain, grad_shift = norm_pull(one, gain_ref[...], acc_ref[block])
            grad_middle = jnp.where(masked, cot_ref[block].astype(F32), 0.0) + back
            gm.near[block] = grad_middle
            grad_branch = (s1_ref[...] * grad_middle).astype(BF16)
            gbr.near[block] = grad_branch
            initial = jnp.where(masked, mt_ref[...], tok_ref[block].astype(F32))
            new = (
                grad_gain,
                grad_shift,
                col_sum(grad_middle * (one - initial)) / s1_ref[...],
                col_sum(grad_branch.astype(F32)),
            )
            total = [a + b for a, b in zip(total, new)]
        if half.stop == padded(rows):
            gm.near[rows:] = jnp.zeros((over, width), F32)
            gbr.near[rows:] = jnp.zeros((over, width), BF16)
        gbr.send(half)
        gm.send(half)
    for i, one in enumerate(total):
        sums.near[i : i + 1] = one
    sums.send()


def back_kernel(
    rows, gbr, wo, ctx, q, k, v, log, n1,
    dq, dk, dv, grads, sums, gc_ref,
):
    me = lax.axis_index("dp")
    cols = dq.near.shape[1]
    gc_ref[...] = nt(gbr.ref[...], wo.ref[...]).astype(BF16)
    store_blocks(me, tn(gbr.ref[...], ctx.ref[...]), grads.near, 3 * cols)
    grads.send((slice(None), slice(None), slice(3 * cols, 4 * cols)))
    attend_back(rows, q.ref, k.ref, v.ref, gc_ref, log.ref, dq.near, dk.near, dv.near)
    for i, one in enumerate((dq, dk, dv)):
        one.send()
        store_blocks(me, tn(n1.ref[...], one.near[...]), grads.near, i * cols)
        grads.send((slice(None), slice(None), slice(i * cols, (i + 1) * cols)))
        if i != 1:
            at = i // 2 * cols
            sums.near[:, at : at + cols] = col_sum(one.near[...].astype(F32))
    sums.send()


def middle_back_kernel(rows, count, *refs):
    first, others = refs[: 2 * count + 7], refs[2 * count + 7 : 2 * count + 14]
    (gm, gbr, sums), outs = refs[2 * count + 14 : 2 * count + 17], refs[2 * count + 17 : 2 * count + 22]
    acc_ref, gc_ref = refs[2 * count + 22 :]
    middle_kernel(rows, count, *first, gm, gbr, sums, acc_ref)
    back_kernel(rows, gbr, *others, *outs, gc_ref)


def input_kernel(rows, *refs):
    grads, weights = refs[:6], list(refs[6:9]) + [Third(refs[9], i) for i in range(3)]
    tok, mask, mt, gain, gm, out, sums, acc_ref = refs[10:]
    width = acc_ref.shape[1]
    halves = halves_of(padded(rows))
    for i, (one, w) in enumerate(zip(grads, weights)):
        for half in halves:
            part = nt(one.ref[half], w.ref[...])
            acc_ref[half] = part if i == 0 else acc_ref[half] + part
    total = [jnp.zeros((1, width), F32)] * 3
    tok_ref, mask_ref, gm_ref, mt_ref, gain_ref = tok.ref, mask.ref, gm.ref, mt.ref, gain.ref
    for half in halves:
        for block in blocks_within(half, rows):
            masked = mask_ref[block] > 0
            initial = jnp.where(masked, mt_ref[...], tok_ref[block].astype(F32))
            back, grad_gain, grad_shift = norm_pull(initial, gain_ref[...], acc_ref[block])
            grad_initial = gm_ref[block] + back
            out.near[block] = jnp.where(masked, 0.0, grad_initial)
            new = (col_sum(jnp.where(masked, grad_initial, 0.0)), grad_gain, grad_shift)
            total = [a + b for a, b in zip(total, new)]
    out.send()
    for i, one in enumerate(total):
        sums.near[i : i + 1] = one
    sums.send()


def output_kernel(rows, count, *refs):
    hiddens, wds = refs[:count], refs[count : 2 * count]
    middle, bd, s2, out, acc_ref = refs[2 * count :]
    halves = halves_of(padded(rows))
    for i, (one, w) in enumerate(in_pieces(hiddens, wds)):
        for half in halves:
            part = nn(one()[half], w()[...])
            acc_ref[half] = part if i == 0 else acc_ref[half] + part
    middle_ref, bd_ref, s2_ref = middle.ref, bd.ref, s2.ref
    for block in blocks_within(slice(0, rows), rows):
        output = acc_ref[block] + bd_ref[...]
        out.near[block] = (middle_ref[block] + s2_ref[...] * output).astype(BF16)
    out.send()


def shape_of(shape, dtype=BF16):
    return jax.ShapeDtypeStruct(shape, dtype)


def cost(flops, *arrays):
    moved = sum(a.size * a.dtype.itemsize for a in arrays)
    return pl.CostEstimate(flops=flops, bytes_accessed=moved, transcendentals=0)


def without(kernel, at, count):
    def inner(*refs):
        kernel(*refs[:at], *refs[at + count :])

    return inner


def pairs(n, bit):
    return [(i, i ^ (1 << bit)) for i in range(n)]


TILE = 256


class Segment:
    def __init__(self, terms, start, width, order):
        self.start, self.width, self.order, self.used, self.got = start, width, list(order), [], []
        self.bits = sorted(order, reverse=True)
        dims = (2,) * len(self.bits)
        self.terms = [(a.reshape(dims + a.shape[1:]), base + start) for a, base in terms]
        self.rows = terms[0][0].shape[1]
        self.across = width // TILE

    @property
    def rest(self):
        return self.order[1:]

    @property
    def tiles(self):
        return self.across << len(self.rest)

    def views(self):
        bit, found = self.order[0] if self.order else None, []
        for array, start in self.terms:
            one = View(array)
            one.index = tuple(0 if b in self.used else 1 if b == bit else slice(None) for b in self.bits)
            one.index += (slice(None), slice(start, start + self.width))
            one.shape = (2,) * len(self.rest) + (self.rows, self.width)
            found.append(one)
        for array, start in self.got:
            found.append(View(array, 0, start + (self.tiles if self.order else 0), self.tiles))
        return found

    def add(self, refs):
        originals, got = refs[: len(self.terms)], refs[len(self.terms) :]
        for at in range(1 << len(self.rest)):
            side = {b: at >> (len(self.rest) - 1 - i) & 1 for i, b in enumerate(self.rest)}
            index = tuple(side[b] for b in self.bits if b in side)
            for c in range(self.across):
                cols, tile = slice(c * TILE, (c + 1) * TILE), at * self.across + c
                parts = [ref[(*index, slice(None), cols)] for ref in originals] + [ref[tile] for ref in got]
                yield tile, self.start + c * TILE, functools.reduce(jnp.add, [p.astype(F32) for p in parts])

    def received(self, array, start):
        self.used.append(self.order.pop(0))
        self.got.append((array, start))


class Group:
    def __init__(self, segments, block):
        self.segments, self.block, self.result = segments, block, None
        self.width = sum(s.width for s in segments)

    @property
    def last(self):
        return not self.segments[0].order


class Sums:
    def __init__(self, same, own, other, bits, last):
        self.parts, self.own, self.n_own, self.last_terms = same + other, same + own, len(own), last
        self.rounds = [bits[i : i + 2] for i in range(0, len(bits), 2)]
        self.stage, self.terms, self.result = 0, [], None

    def job(self):
        width = self.parts[0].shape[1]
        height = -(-sum(p.size for p in self.parts) // (8 * width)) * 8
        packed = {0: self.parts, 1: self.own}.get(self.stage, [])
        places, row, col = [], 0, 0
        for p in packed:
            steps = []
            for at in range(0, p.shape[1], width):
                size = min(width, p.shape[1] - at)
                steps.append(((slice(row, row + p.shape[0]), slice(col, col + size)), slice(at, at + size)))
                col += size
                if col == width:
                    row, col = row + p.shape[0], 0
            places.append(steps)
        return packed, places, self.terms, shape_of((height, width), F32)

    def final_shapes(self):
        own = self.own[len(self.own) - self.n_own :]
        width = own[0].shape[1]
        return [shape_of((1, width), F32)] * 9 + [shape_of((1, width // 2), F32)] * 2 + [
            shape_of((1, width * (len(own) - 1)), F32)
        ]

    def final(self, total, ins, outs):
        bias, scale = (one.ref[...] for one in ins)
        start = sum(p.shape[0] for p in self.own[: len(self.own) - self.n_own])
        rows = [total[i : i + 1] for i in range(total.shape[0])]
        for out, value in zip(outs, rows[:8]):
            out.near[...] = value
        outs[8].near[...] = (functools.reduce(jnp.add, rows[8:start]) + bias * rows[7]) / scale
        half = outs[9].near.shape[1]
        outs[9].near[...] = rows[start][:, :half]
        outs[10].near[...] = rows[start][:, half:]
        for i, value in enumerate(rows[start + 1 : start + self.n_own]):
            outs[11].near[:, i * 2 * half : (i + 1) * 2 * half] = value

    @property
    def last(self):
        return self.stage == len(self.rounds) + 1

    def take(self, sent):
        n = lax.axis_size("dp")
        if self.last:
            self.result = sent
        elif self.stage == 0:
            self.terms = [swap(sent[0])]
        else:
            bits = self.rounds[self.stage - 1]
            self.terms = list(sent)
            for some in range(1, 1 << len(bits)):
                flip = sum(1 << b for i, b in enumerate(bits) if some >> i & 1)
                self.terms.append(lax.ppermute(sent[0], "dp", [(d, d ^ flip) for d in range(n)]))
        self.stage += 1


def exchange(groups, after, sums=None, carry=None):
    buffers, shapes, plan = {}, [], []
    for segment in [s for g in groups if not g.last for s in g.segments]:
        buffers.setdefault(segment.order[0], []).append(segment)
    for some in buffers.values():
        starts = [sum(s.tiles for s in some[:i]) for i in range(len(some))]
        plan.append(list(zip(some, starts)))
        shapes.append(shape_of((sum(s.tiles for s in some), some[0].rows, TILE)))
    ending = [g for g in groups if g.last]
    for g in ending:
        shapes += [shape_of((g.segments[0].rows, g.block), F32)] * (g.width // g.block)
    views = [s.views() for one in plan for s, _ in one] + [s.views() for g in ending for s in g.segments]
    counts = [len(v) for v in views]
    views = [v for some in views for v in some]
    n_summed = len(shapes)
    packed, places, terms = [], [], []
    sums_last = sums is not None and sums.last
    if sums is not None:
        packed, places, terms, shape = sums.job()
        views += [View(a) for a in packed + terms + (sums.last_terms if sums_last else [])]
        shapes += sums.final_shapes() if sums_last else [shape]
    passed = [] if carry is None else [carry]
    hbm = pl.BlockSpec(memory_space=pl.ANY)
    skipped, n_in, n_out = len(after) + len(passed), len(views), len(shapes)

    def kernel(*refs):
        far_in, far_out = refs[skipped : skipped + n_in], refs[skipped + n_in :][:n_out]
        nears = list(refs[skipped + n_in + n_out + len(passed) :])
        line = Line(nears.pop(), n_in + n_out)
        ins = []
        for far, view in zip(far_in, views):
            far = far if view.index is None else far.at[view.index]
            ins.append(Moved(far, nears.pop(0), line))
        line.begin()
        outs = [Moved(far, nears.pop(0), line, ()) for far in far_out]
        sizes = list(counts)

        def taken():
            return [ins.pop(0).ref for _ in range(sizes.pop(0))]

        for one in plan:
            out = outs.pop(0)
            for segment, start in one:
                for tile, _, total in segment.add(taken()):
                    out.near[start + tile] = total.astype(BF16)
            out.send()
        for g in ending:
            mine = [outs.pop(0) for _ in range(g.width // g.block)]
            for segment in g.segments:
                for _, col, total in segment.add(taken()):
                    mine[col // g.block].near[:, col % g.block : col % g.block + TILE] = total
            for out in mine:
                out.send()
        if sums is not None:
            if packed:
                new = outs[0]
                new.near[...] = ins[-1].ref[...] if terms else jnp.zeros(shape.shape, F32)
                for one, steps in zip(ins, places):
                    for place, cols in steps:
                        new.near[place] += one.ref[:, cols]
            else:
                total = functools.reduce(jnp.add, [one.ref[...] for one in ins[: len(terms)]])
                if sums_last:
                    sums.final(total, ins[len(terms) :], outs)
                else:
                    outs[0].near[...] = total
            for out in outs:
                out.send()
        line.finish()

    outs = pl.pallas_call(
        kernel,
        in_specs=[hbm] * (skipped + n_in),
        out_specs=[hbm] * (n_out + len(passed)),
        out_shape=shapes + [shape_of(p.shape, p.dtype) for p in passed],
        input_output_aliases={len(after): n_out} if passed else {},
        scratch_shapes=[pltpu.VMEM(v.shape, v.array.dtype) for v in views]
        + [pltpu.VMEM(o.shape, o.dtype) for o in shapes]
        + [pltpu.SemaphoreType.DMA((n_in + n_out,))],
        compiler_params=pltpu.CompilerParams(vmem_limit_bytes=EXCHANGE_VMEM),
        cost_estimate=cost(0, *shapes),
        name="exchange",
    )(*after, *passed, *[v.array for v in views])
    n, left = lax.axis_size("dp"), list(outs[:n_summed])
    for bit, one in zip(buffers, plan):
        got = lax.ppermute(left.pop(0), "dp", pairs(n, bit))
        for segment, start in one:
            segment.received(got, start)
    for g in ending:
        g.result = [left.pop(0) for _ in range(g.width // g.block)]
    if sums is not None:
        sums.take(list(outs[n_summed:n_out]))
    sent = list(outs[:n_out])
    return sent if carry is None else (sent, outs[-1])


def swap(array):
    return lax.ppermute(array, "tp", [(0, 1), (1, 0)])


def local_body(
    tokens, masked, cotangent, mask_token, gain_one, shift_one, w_query, w_key, w_value, b_query,
    b_value, w_out, b_out, scale_one, gain_two, shift_two, w_up, b_up, w_down, b_down, scale_two,
):
    rows, width = tokens.shape
    tall = padded(rows)
    half = w_query.shape[1]
    units = w_up.shape[1]
    n = lax.axis_size("dp")
    bits = n.bit_length() - 1
    me = lax.axis_index("dp").astype(jnp.int32).reshape(1)
    biases = jnp.concatenate([b_query, b_value, b_up]).reshape(1, -1)

    joined2 = swap(jnp.concatenate([w_query, w_key, w_value], axis=1))
    biases2 = swap(biases)
    wo2 = swap(w_out)
    wu2, wd2 = swap(w_up), swap(w_down)
    row = lambda v: v.reshape(1, -1)
    bq2, bv2 = View(biases2, 1, 0, half), View(biases2, 1, half, half)
    bq, bv, bu = row(b_query), row(b_value), row(b_up)
    mt, g1, s1, bo, sc1 = row(mask_token), row(gain_one), row(shift_one), row(b_out), row(scale_one)
    g2, s2, bd, sc2 = row(gain_two), row(shift_two), row(b_down), row(scale_two)
    mask = masked.reshape(rows, 1)

    narrow = shape_of((tall, half))
    wide = shape_of((tall, width))
    attend_flops = 2 * 2 * 256 * SEQ * rows * half // HD
    logs = shape_of(norm_rows(rows, half), F32)
    normed, q, k, v, ctx, log = moved_call(
        functools.partial(first_kernel, rows),
        [wide, narrow, narrow, narrow, narrow, logs],
        (tokens, mask, mt, g1, s1, w_query, w_key, w_value, bq, bv),
        6 * rows * width * half + attend_flops,
        6,
        name="first",
        waves=[[(i, 0) for i in range(5)]],
    )
    tall_f32 = shape_of((tall, width), F32)
    scratch = [pltpu.VMEM((tall, width), F32)]
    one_row = shape_of((1, width), F32)
    q2, k2, v2, ctx2, log2, middle, normed2, go, sum_go = moved_call(
        functools.partial(second_kernel, rows),
        [narrow, narrow, narrow, narrow, logs, tall_f32, wide, wide, one_row],
        (normed, joined2, bq2, bv2, ctx, w_out, wo2, bo, sc1, g2, s2, tokens, mask, mt, cotangent, sc2),
        10 * rows * width * half + attend_flops,
        12,
        scratch=scratch,
        name="second",
        cuts={1: (1, 3)},
        waves=[[(0, 0), (1, 0), (2, 0)], [(1, 1), (1, 2), (3, 0)]],
    )

    natural = tuple(range(bits))
    by_x, by_y = natural, natural[1:2] + natural[0:1] + natural[2:]
    by_z = natural[2 % bits :] + natural[: 2 % bits]

    part = units // 2
    chunk = min(512, part)
    hiddens, gps, ups, downs = [], [], [], []

    def feed(weights, first, size, after=()):
        w_up, w_down, b_up, b_start = weights
        count = size // chunk
        hidden, gp, grads, sums, scale_sum = moved_call(
            functools.partial(feed_kernel, chunk),
            [
                shape_of((tall, size)),
                shape_of((tall, size)),
                shape_of((n, width // n, 2 * size)),
                shape_of((1, size), F32),
                one_row,
            ],
            (normed2, View(w_up, 1, first, size), go, View(w_down, 0, first, size),
             View(b_up, 1, b_start + first, size)),
            8 * tall * width * size,
            4 * count + 2,
            name="feed",
            after=after,
            cuts={1: (1, count), 3: (0, count)},
            waves=[[(0, 0), (1, 0)], [(2, 0), (3, 0), (4, 0)]],
        )
        hiddens.append(hidden)
        gps.append(gp)
        ups.append(View(w_up, 1, first, size))
        downs.append(View(w_down, 0, first, size))
        scale_sums.append(scale_sum)
        return grads, sums

    def grouped(size, block, *terms, third=None):
        parts = ((0, 3, by_x), (3, 3, by_y), (6, 2, third or by_z))
        return Group([Segment(terms, at * size // 8, w * size // 8, o) for at, w, o in parts], block)

    mine, other = (w_up, w_down, bu, 0), (wu2, wd2, biases2, 2 * half)
    scale_sums = []
    theirs, sums_up2 = feed(other, 0, units)
    theirs = swap(theirs)
    own, sums_up_a = feed(mine, 0, part, [sums_up2])
    a = grouped(2 * part, chunk, (own, 0), (theirs, 0))
    sent = exchange([a], [sums_up_a])
    own, sums_up_b = feed(mine, part, part, sent)
    b = grouped(2 * part, chunk, (own, 0), (theirs, 2 * part))
    sent = exchange([a, b], [sums_up_b])

    back_outs = [narrow, narrow, narrow, shape_of((n, width // n, 4 * half)), shape_of((1, 2 * half), F32)]
    back_flops = 10 * rows * width * half + 3 * attend_flops
    back_scratch = [pltpu.VMEM((tall, half), BF16)]
    gm, gbr, sums_two, dq2, dk2, dv2, gw2, sums_b2 = moved_call(
        functools.partial(middle_back_kernel, rows, len(gps)),
        [tall_f32, wide, shape_of((4, width), F32)] + back_outs,
        (*gps, *ups, middle, tokens, mask, mt, cotangent, g2, sc1, wo2, ctx2, q2, k2, v2, log2, normed),
        8 * tall * width * part + back_flops,
        13,
        scratch=scratch + back_scratch,
        name="middle",
        after=sent,
        cuts={0: (1, 2), 3: (1, 2)},
        waves=[[(0, 0), (3, 0)], [(0, 1), (3, 1)], [(1, 0), (4, 0)], [(2, 0), (5, 0)]],
    )
    sent, gw2 = exchange([a, b], [sums_b2], carry=gw2)
    gw2 = swap(gw2)

    def back(wo, ctx, q, k, v, log, after):
        return moved_call(
            functools.partial(back_kernel, rows),
            back_outs,
            (gbr, wo, ctx, q, k, v, log, normed),
            back_flops,
            8,
            scratch=back_scratch,
            name="back",
            after=after,
            waves=[[(0, 0), (1, 0)], [(2, 0)]],
        )

    dq, dk, dv, gw, sums_b = back(w_out, ctx, q, k, v, log, sent)
    by_z_last = natural[2:3] + natural[:2] + natural[3:]
    c = grouped(4 * half, half, (gw, 0), (gw2, 0), third=by_z_last)
    sent = exchange([c, b, a], [sums_b])

    grad_tokens, sums_one = moved_call(
        functools.partial(input_kernel, rows),
        [shape_of((rows, width), F32), shape_of((3, width), F32)],
        (dq, dk, dv, dq2, dk2, dv2, w_query, w_key, w_value, joined2, tokens, mask, mt, g1, gm),
        12 * rows * width * half,
        2,
        scratch=scratch,
        cuts={9: (1, 3)},
        waves=[[(0, 0), (6, 0)], [(1, 0), (7, 0)], [(2, 0), (8, 0), (3, 0), (9, 0)]],
        name="input",
        after=sent,
    )
    same = [sums_one, sums_two, sum_go, *scale_sums]
    sums = Sums(same, [sums_b, sums_up_a, sums_up_b], [sums_b2, sums_up2], list(natural), [bd, sc2])
    sent = exchange([c, b, a], [sums_one], sums=sums)
    block_out = moved_call(
        functools.partial(output_kernel, rows, len(hiddens)),
        [shape_of((rows, width))],
        (*hiddens, *downs, middle, bd, sc2),
        8 * tall * width * part,
        1,
        scratch=scratch,
        cuts={0: (1, 2), 3: (0, 2)},
        waves=[[(0, 0), (3, 0)], [(0, 1), (3, 1)], [(1, 0), (4, 0)], [(2, 0), (5, 0)]],
        name="output",
        after=sent,
    )[0]
    last = block_out
    while sums.result is None:
        last = exchange([g for g in (c, b, a) if g.result is None], [last], sums=sums)[-1]

    done = [one for group in (a, b) for one in group.result]
    grad_w_down = jnp.concatenate(done[0::2], axis=1).T
    grad_w_up = jnp.concatenate(done[1::2], axis=1)
    grad_w_query, grad_w_key, grad_w_value, grad_w_out = c.result
    (grad_mask_token, grad_gain_one, grad_shift_one, grad_gain_two, grad_shift_two, grad_scale_one, grad_b_out,
     grad_b_down, grad_scale_two, grad_b_query, grad_b_value, grad_b_up) = (
        one.reshape(-1) for one in sums.result
    )
    return (
        block_out,
        grad_tokens,
        grad_mask_token,
        grad_gain_one,
        grad_shift_one,
        grad_w_query,
        grad_w_key,
        grad_w_value,
        grad_b_query,
        grad_b_value,
        grad_w_out.T,
        grad_b_out,
        grad_scale_one,
        grad_gain_two,
        grad_shift_two,
        grad_w_up,
        grad_b_up,
        grad_w_down,
        grad_b_down,
        grad_scale_two,
    )


def solution(mesh):
    placed = (
        P(("dp", "tp"), None),
        P(("dp", "tp")),
        P(("dp", "tp"), None),
        P(),
        P(),
        P(),
        P(None, "tp"),
        P(None, "tp"),
        P(None, "tp"),
        P("tp"),
        P("tp"),
        P("tp", None),
        P(),
        P(),
        P(),
        P(),
        P(None, "tp"),
        P("tp"),
        P("tp", None),
        P(),
        P(),
    )
    fits = mesh.shape["tp"] == 2 and mesh.shape["dp"].bit_count() == 1
    return jax.shard_map(
        local_body if fits else gathered_body,
        mesh=mesh,
        in_specs=placed,
        out_specs=(
            P(("dp", "tp"), None),
            P(("dp", "tp"), None),
            P(),
            P(),
            P(),
            P("dp", "tp"),
            P("dp", "tp"),
            P("dp", "tp"),
            P("tp"),
            P("tp"),
            P("tp", "dp"),
            P(),
            P(),
            P(),
            P(),
            P("dp", "tp"),
            P("tp"),
            P("tp", "dp"),
            P(),
            P(),
        ),
        check_vma=False,
    )
```

```python
import functools
import math

import jax
import jax.numpy as jnp
from jax import lax
from jax.experimental import pallas as pl
from jax.experimental.pallas import tpu as pltpu
from jax.sharding import PartitionSpec as P

SEQ = 197
HD = 64
PAIR = 2 * HD
EPSILON = 1e-06
BF16 = jnp.bfloat16
F32 = jnp.float32
MIB = 2**20
LOWEST = -1e30
KERNEL_VMEM = 64 * MIB
EXCHANGE_VMEM = 64 * MIB

def layer_norm(rows_in, gain_vec, shift_vec):
    center = rows_in - jnp.mean(rows_in, axis=-1, keepdims=True)
    spread = jnp.mean(center * center, axis=-1, keepdims=True)
    return center * lax.rsqrt(spread + EPSILON) * gain_vec + shift_vec


def norm_backward(rows_in, gain_vec, shift_vec, grad_rows):
    unused, pull = jax.vjp(layer_norm, rows_in, gain_vec, shift_vec)
    return pull(grad_rows)


def gelu_exact(values):
    return jax.nn.gelu(values, approximate=False)


def product(left, right):
    return jnp.dot(left, right, preferred_element_type=jnp.float32)


def times_transposed(left, right):
    return lax.dot_general(
        left, right, (((1,), (1,)), ((), ())), preferred_element_type=jnp.float32
    )


def transposed_times(left, right):
    return lax.dot_general(
        left, right, (((0,), (0,)), ((), ())), preferred_element_type=jnp.float32
    )


def attend_forward(queries, key_rows, values, factor):
    scores = (
        jnp.einsum("iqhd,ikhd->ihqk", queries, key_rows, preferred_element_type=jnp.float32)
        * factor
    )
    row_max = jnp.max(scores, axis=-1, keepdims=True)
    raised = jnp.exp(scores - row_max)
    sum_exp = jnp.sum(raised, axis=-1, keepdims=True)
    probs_low = (raised / sum_exp).astype(jnp.bfloat16)
    context = jnp.einsum("ihqk,ikhd->iqhd", probs_low, values, preferred_element_type=jnp.float32)
    return (context, row_max + jnp.log(sum_exp))


def attend_backward(queries, key_rows, values, log_total, grad_context, factor):
    scores = (
        jnp.einsum("iqhd,ikhd->ihqk", queries, key_rows, preferred_element_type=jnp.float32)
        * factor
    )
    probs = jnp.exp(scores - log_total)
    grad_probs = jnp.einsum(
        "iqhd,ikhd->ihqk", grad_context, values, preferred_element_type=jnp.float32
    )
    inner = jnp.sum(grad_probs * probs, axis=-1, keepdims=True)
    grad_scores = (probs * (grad_probs - inner)).astype(jnp.bfloat16)
    grad_queries = (
        jnp.einsum("ihqk,ikhd->iqhd", grad_scores, key_rows, preferred_element_type=jnp.float32)
        * factor
    )
    grad_keys = (
        jnp.einsum("ihqk,iqhd->ikhd", grad_scores, queries, preferred_element_type=jnp.float32)
        * factor
    )
    grad_values = jnp.einsum(
        "ihqk,iqhd->ikhd",
        probs.astype(jnp.bfloat16),
        grad_context,
        preferred_element_type=jnp.float32,
    )
    return (grad_queries, grad_keys, grad_values)


def gathered_body(
    tokens,
    masked,
    cotangent,
    mask_token,
    gain_one,
    shift_one,
    w_query,
    w_key,
    w_value,
    b_query,
    b_value,
    w_out,
    b_out,
    scale_one,
    gain_two,
    shift_two,
    w_up,
    b_up,
    w_down,
    b_down,
    scale_two,
):
    local_cols = w_query.shape[1]
    local_heads = local_cols // HD
    factor = 1.0 / math.sqrt(HD)
    chosen = (masked > 0)[:, None]
    initial = jnp.where(chosen, mask_token[None, :], tokens.astype(jnp.float32))
    normed = layer_norm(initial, gain_one, shift_one).astype(jnp.bfloat16)
    w_joined = jnp.concatenate([w_query, w_key, w_value], axis=1)
    b_joined = jnp.concatenate([b_query, jnp.zeros_like(b_query), b_value])
    gathered = lax.all_gather(normed, "tp", axis=0, tiled=True)
    joined = (product(gathered, w_joined) + b_joined).astype(jnp.bfloat16)
    group_rows = gathered.shape[0]
    head_shape = (group_rows // SEQ, SEQ, local_heads, HD)
    queries = joined[:, :local_cols].reshape(head_shape)
    key_rows = joined[:, local_cols : 2 * local_cols].reshape(head_shape)
    values = joined[:, 2 * local_cols :].reshape(head_shape)
    context, log_total = attend_forward(queries, key_rows, values, factor)
    context = context.reshape(group_rows, local_cols).astype(jnp.bfloat16)
    branch = (
        lax.psum_scatter(
            product(context, w_out).astype(jnp.bfloat16), "tp", scatter_dimension=0, tiled=True
        ).astype(jnp.float32)
        + b_out
    )
    middle = initial + scale_one * branch
    normed_two = layer_norm(middle, gain_two, shift_two).astype(jnp.bfloat16)
    gathered_two = lax.all_gather(normed_two, "tp", axis=0, tiled=True)
    pre_act = product(gathered_two, w_up) + b_up
    hidden = gelu_exact(pre_act).astype(jnp.bfloat16)
    output = (
        lax.psum_scatter(
            product(hidden, w_down).astype(jnp.bfloat16), "tp", scatter_dimension=0, tiled=True
        ).astype(jnp.float32)
        + b_down
    )
    block_out = (middle + scale_two * output).astype(jnp.bfloat16)
    grad_block = cotangent.astype(jnp.float32) * chosen.astype(jnp.float32)
    grad_output = (scale_two * grad_block).astype(jnp.bfloat16)
    grad_scale_two = jnp.sum(grad_block * output, axis=0)
    grad_b_down = jnp.sum(grad_output.astype(jnp.float32), axis=0)
    portion = lax.all_gather(grad_output, "tp", axis=0, tiled=True)
    grad_hidden = times_transposed(portion, w_down)
    grad_w_down = transposed_times(hidden, portion)
    grad_hidden, grad_w_down = (grad_hidden, grad_w_down)
    unused, gelu_pull = jax.vjp(gelu_exact, pre_act)
    grad_pre = gelu_pull(grad_hidden)[0].astype(jnp.bfloat16)
    grad_b_up = jnp.sum(grad_pre.astype(jnp.float32), axis=0)
    grad_normed_two = lax.psum_scatter(
        times_transposed(grad_pre, w_up).astype(jnp.bfloat16), "tp", scatter_dimension=0, tiled=True
    ).astype(jnp.float32)
    grad_w_up = transposed_times(lax.all_gather(normed_two, "tp", axis=0, tiled=True), grad_pre)
    grad_middle_norm, grad_gain_two, grad_shift_two = norm_backward(
        middle, gain_two, shift_two, grad_normed_two
    )
    grad_middle = grad_block + grad_middle_norm
    grad_branch = (scale_one * grad_middle).astype(jnp.bfloat16)
    grad_scale_one = jnp.sum(grad_middle * branch, axis=0)
    grad_b_out = jnp.sum(grad_branch.astype(jnp.float32), axis=0)
    portion = lax.all_gather(grad_branch, "tp", axis=0, tiled=True)
    grad_context = times_transposed(portion, w_out)
    grad_w_out = transposed_times(context, portion)
    grad_context, grad_w_out = (grad_context, grad_w_out)
    grad_context = grad_context.astype(jnp.bfloat16).reshape(head_shape)
    grad_queries, grad_keys, grad_values = attend_backward(
        queries, key_rows, values, log_total, grad_context, factor
    )
    grad_joined = jnp.concatenate(
        [
            grad_queries.reshape(group_rows, local_cols),
            grad_keys.reshape(group_rows, local_cols),
            grad_values.reshape(group_rows, local_cols),
        ],
        axis=1,
    ).astype(jnp.bfloat16)
    grad_b_query = jnp.sum(grad_joined[:, :local_cols].astype(jnp.float32), axis=0)
    grad_b_value = jnp.sum(grad_joined[:, 2 * local_cols :].astype(jnp.float32), axis=0)
    grad_normed = lax.psum_scatter(
        times_transposed(grad_joined, w_joined).astype(jnp.bfloat16),
        "tp",
        scatter_dimension=0,
        tiled=True,
    ).astype(jnp.float32)
    grad_w_joined = transposed_times(lax.all_gather(normed, "tp", axis=0, tiled=True), grad_joined)
    grad_initial_norm, grad_gain_one, grad_shift_one = norm_backward(
        initial, gain_one, shift_one, grad_normed
    )
    grad_initial = grad_middle + grad_initial_norm
    grad_tokens = jnp.where(chosen, 0.0, grad_initial)
    grad_mask_token = jnp.sum(jnp.where(chosen, grad_initial, 0.0), axis=0)
    (
        grad_mask_token,
        grad_gain_one,
        grad_shift_one,
        grad_b_out,
        grad_scale_one,
        grad_gain_two,
        grad_shift_two,
        grad_b_down,
        grad_scale_two,
    ) = lax.psum(
        (
            grad_mask_token,
            grad_gain_one,
            grad_shift_one,
            grad_b_out,
            grad_scale_one,
            grad_gain_two,
            grad_shift_two,
            grad_b_down,
            grad_scale_two,
        ),
        ("dp", "tp"),
    )
    grad_b_query, grad_b_value, grad_b_up = lax.psum((grad_b_query, grad_b_value, grad_b_up), "dp")
    grad_w_joined, grad_w_out, grad_w_up, grad_w_down = (
        lax.psum_scatter(
            grad_w_joined.astype(jnp.bfloat16), "dp", scatter_dimension=0, tiled=True
        ).astype(jnp.float32),
        lax.psum_scatter(
            grad_w_out.astype(jnp.bfloat16), "dp", scatter_dimension=1, tiled=True
        ).astype(jnp.float32),
        lax.psum_scatter(
            grad_w_up.astype(jnp.bfloat16), "dp", scatter_dimension=0, tiled=True
        ).astype(jnp.float32),
        lax.psum_scatter(
            grad_w_down.astype(jnp.bfloat16), "dp", scatter_dimension=1, tiled=True
        ).astype(jnp.float32),
    )
    grad_w_query = grad_w_joined[:, :local_cols]
    grad_w_key = grad_w_joined[:, local_cols : 2 * local_cols]
    grad_w_value = grad_w_joined[:, 2 * local_cols :]
    return (
        block_out,
        grad_tokens,
        grad_mask_token,
        grad_gain_one,
        grad_shift_one,
        grad_w_query,
        grad_w_key,
        grad_w_value,
        grad_b_query,
        grad_b_value,
        grad_w_out,
        grad_b_out,
        grad_scale_one,
        grad_gain_two,
        grad_shift_two,
        grad_w_up,
        grad_b_up,
        grad_w_down,
        grad_b_down,
        grad_scale_two,
    )


def nn(left, right):
    return lax.dot_general(left, right, (((1,), (0,)), ((), ())), preferred_element_type=F32)


def nt(left, right):
    return lax.dot_general(left, right, (((1,), (1,)), ((), ())), preferred_element_type=F32)


def tn(left, right):
    return lax.dot_general(left, right, (((0,), (0,)), ((), ())), preferred_element_type=F32)


def padded(rows):
    return -(-rows // 32) * 32


def windows(rows):
    found = []
    for image in range(rows // SEQ):
        first = image * SEQ
        start = first // 16 * 16
        found.append((start, -(-(first - start + SEQ) // 16) * 16, first - start))
    return found


def row_blocks(total, size=160):
    return [slice(s, min(s + size, total)) for s in range(0, total, size)]


def inside(shape, axis, offset):
    at = lax.broadcasted_iota(jnp.int32, shape, axis)
    return (at >= offset) & (at < offset + SEQ)


def col_sum(values):
    return jnp.sum(values, axis=0, keepdims=True)


def row_mean(values):
    return jnp.mean(values, axis=-1, keepdims=True)


def moments(rows_in):
    center = rows_in - row_mean(rows_in)
    return center, lax.rsqrt(row_mean(center * center) + EPSILON)


def norm_pull(rows_in, gain, grad):
    center, inv = moments(rows_in)
    hat = center * inv
    scaled = grad * gain
    back = (scaled - row_mean(scaled) - hat * row_mean(scaled * hat)) * inv
    return back, col_sum(grad * hat), col_sum(grad)


def gelu_parts(v):
    cdf = 0.5 + 0.5 * lax.erf(v * math.sqrt(0.5))
    return cdf, v * (jnp.exp(-0.5 * (v * v)) * (1.0 / math.sqrt(2.0 * math.pi)))


def rows_outside(values, offset, fill):
    size = values.shape[0]

    def edge(part, base):
        at = lax.broadcasted_iota(jnp.int32, part.shape, 0) + base
        return jnp.where((at >= offset) & (at < offset + SEQ), part, fill)

    head = edge(values[:16], 0) if offset else values[:16]
    return jnp.concatenate([head, values[16:-32], edge(values[-32:], size - 32)], axis=0)


def one_head(shape, head):
    return (lax.broadcasted_iota(jnp.int32, shape, 1) < HD) == (head == 0)


def in_turn(rows, lead, begin, finish):
    units = [(window, head) for window in windows(rows) for head in (0, 1)]
    begun = [begin(*unit) for unit in units[:lead]]
    for i, unit in enumerate(units):
        if i + lead < len(units):
            begun.append(begin(*units[i + lead]))
        finish(i, *unit, begun[i])
        begun[i] = None


def norm_rows(rows, cols):
    return (cols // HD * (rows // SEQ), 256)


def attend(rows, q_ref, k_ref, v_ref, ctx_ref, log_ref):
    ctx_ref[padded(rows) - 32 :, :] = jnp.zeros((32, ctx_ref.shape[1]), BF16)
    count = 2 * (rows // SEQ)

    def one_pair(pair, carry):
        lanes = pl.ds(pl.multiple_of(pair * PAIR, PAIR), PAIR)
        halves = {}

        def begin(window, head):
            start, size, _ = window
            win = slice(start, start + size)
            k = k_ref[win, lanes]
            return nt(jnp.where(one_head(k.shape, head), k, jnp.zeros_like(k)), q_ref[win, lanes])

        def finish(i, window, head, scores):
            start, size, offset = window
            win = slice(start, start + size)
            scores = rows_outside(scores, offset, LOWEST)
            top = jnp.max(scores, axis=0, keepdims=True)
            raised = jnp.exp(scores - top)
            total = jnp.sum(raised, axis=0, keepdims=True)
            out = tn(v_ref[win, lanes], raised.astype(BF16))
            halves[head] = out[head * HD : (head + 1) * HD] * (1.0 / total)
            log_ref[pl.ds(pair * count + i, 1), :size] = top + jnp.log(total)
            if head == 1:
                both = jnp.concatenate([halves[0], halves[1]], axis=0).T.astype(BF16)
                keep = inside((size, PAIR), 0, offset)
                ctx_ref[win, lanes] = jnp.where(keep, both, ctx_ref[win, lanes])

        in_turn(rows, 4, begin, finish)
        return carry

    lax.fori_loop(0, q_ref.shape[1] // PAIR, one_pair, 0, unroll=2)


def attend_back(rows, q_ref, k_ref, v_ref, gc_ref, log_ref, dq_ref, dk_ref, dv_ref):
    for ref in (dq_ref, dk_ref, dv_ref):
        ref[padded(rows) - 32 :, :] = jnp.zeros((32, ref.shape[1]), BF16)
    factor = 1.0 / math.sqrt(HD)
    count = 2 * (rows // SEQ)

    def one_pair(pair, carry):
        lanes = pl.ds(pl.multiple_of(pair * PAIR, PAIR), PAIR)
        halves = {}

        def begin(window, head):
            start, size, offset = window
            win = slice(start, start + size)
            zero = jnp.zeros((size, PAIR), BF16)
            mine = one_head(zero.shape, head)
            k = jnp.where(mine, k_ref[win, lanes], zero)
            v = jnp.where(mine, v_ref[win, lanes], zero)
            gc = jnp.where(inside(zero.shape, 0, offset), gc_ref[win, lanes], zero)
            q = q_ref[win, lanes]
            return nt(k, q), nt(v, gc), k, q, gc

        def finish(i, window, head, begun):
            start, size, offset = window
            win = slice(start, start + size)
            scores, grad_probs, k, q, gc = begun
            scores = rows_outside(scores, offset, LOWEST)
            probs = jnp.exp(scores - log_ref[pl.ds(pair * count + i, 1), :size])
            inner = jnp.sum(grad_probs * probs, axis=0, keepdims=True)
            grad_scores = (probs * (grad_probs - inner)).astype(BF16)
            halves[head] = tn(grad_scores, k), nn(grad_scores, q), nn(probs.astype(BF16), gc)
            if head == 1:
                keep = inside((size, PAIR), 0, offset)
                first = one_head((size, PAIR), 0)
                low, high = halves[0], halves[1]
                for ref, new in (
                    (dq_ref, (low[0] + high[0]) * factor),
                    (dk_ref, jnp.where(first, low[1], high[1])),
                    (dv_ref, jnp.where(first, low[2], high[2])),
                ):
                    ref[win, lanes] = jnp.where(keep, new.astype(BF16), ref[win, lanes])

        in_turn(rows, 2, begin, finish)
        return carry

    lax.fori_loop(0, q_ref.shape[1] // PAIR, one_pair, 0, unroll=2)


class Moved:
    def __init__(self, far, near, line, pieces=(None,)):
        self.far, self.near, self.line, self.pieces = far, near, line, pieces
        self.copies = [line.add(*self.views(p)) for p in pieces]

    def views(self, p):
        return (self.far, self.near) if p is None else (self.far.at[p], self.near.at[p])

    def part(self, i):
        self.line.wait(self.copies[i])
        return self.views(self.pieces[i])[1]

    @property
    def ref(self):
        for copy in self.copies:
            self.line.wait(copy)
        return self.near

    def send(self, p=None):
        far, near = self.views(p)
        self.line.send(near, far)


class Line:
    def __init__(self, sems, count):
        self.sems, self.free = sems, iter(range(count))
        self.queue, self.waves, self.started, self.waited, self.sent = [], [], 0, set(), []

    def copy(self, source, target):
        return pltpu.make_async_copy(source, target, self.sems.at[next(self.free)])

    def add(self, source, target):
        self.queue.append(self.copy(source, target))
        return len(self.queue) - 1

    def begin(self, waves=()):
        first = [i for wave in waves for i in wave]
        rest = [i for i in range(len(self.queue)) if i not in first]
        self.waves = [list(wave) for wave in waves] + [rest]
        self.start_to(1)

    def start_to(self, stop):
        while self.started < min(stop, len(self.waves)):
            for i in self.waves[self.started]:
                self.queue[i].start()
            self.started += 1

    def wait(self, i):
        if i in self.waited:
            return
        wave = next(k for k, some in enumerate(self.waves) if i in some)
        self.start_to(wave + 1)
        self.queue[i].wait()
        self.waited.add(i)
        self.start_to(wave + 2)

    def send(self, source, target):
        copy = self.copy(source, target)
        copy.start()
        self.sent.append(copy)

    def finish(self):
        for i in range(len(self.queue)):
            self.wait(i)
        for copy in self.sent:
            copy.wait()


class View:
    def __init__(self, array, axis=0, start=0, size=None):
        self.array, self.shape, self.index = array, array.shape, None
        if size is not None:
            p = slice(start, start + size)
            self.index = (slice(None),) * axis + (p,)
            self.shape = tuple(size if i == axis else n for i, n in enumerate(array.shape))


def cut_in(size, axis, count):
    step = size // count
    spans = [slice(i * step, (i + 1) * step) for i in range(count)]
    return [(slice(None),) * axis + (p,) for p in spans]


def moved_call(kernel, outs, args, flops, sends, scratch=(), name=None, after=(), cuts=None, waves=()):
    hbm = pl.BlockSpec(memory_space=pl.ANY)
    cuts = cuts or {}
    views = [a if isinstance(a, View) else View(a) for a in args]
    args = [view.array for view in views]
    n_in, n_out = len(args), len(outs)
    pieces = [
        cut_in(v.shape[cuts[i][0]], *cuts[i]) if i in cuts else [None] for i, v in enumerate(views)
    ]
    n_sems = sum(len(p) for p in pieces) + sends
    buffers = [pltpu.VMEM(v.shape, v.array.dtype) for v in views]
    buffers += [pltpu.VMEM(o.shape, o.dtype) for o in outs]

    def inner(*refs):
        refs = refs[len(after) :]
        far_in, far_out, rest = refs[:n_in], refs[n_in : n_in + n_out], list(refs[n_in + n_out :])
        line = Line(rest.pop(), n_sems)
        ins = []
        for far, view, p in zip(far_in, views, pieces):
            far = far if view.index is None else far.at[view.index]
            ins.append(Moved(far, rest.pop(0), line, p))
        line.begin([[ins[i].copies[j] for i, j in wave] for wave in waves])
        results = [Moved(far, rest.pop(0), line, ()) for far in far_out]
        kernel(*ins, *results, *rest)
        line.finish()

    return pl.pallas_call(
        inner,
        in_specs=[hbm] * (len(after) + n_in),
        out_specs=[hbm] * n_out,
        out_shape=outs,
        scratch_shapes=buffers + list(scratch) + [pltpu.SemaphoreType.DMA((n_sems,))],
        compiler_params=pltpu.CompilerParams(vmem_limit_bytes=KERNEL_VMEM),
        cost_estimate=cost(flops, *args, *outs),
        name=name,
    )(*after, *args)


def halves_of(tall):
    middle = tall // 2 // 16 * 16
    return [slice(0, middle), slice(middle, tall)]


def blocks_within(part, rows, size=400):
    stop = min(part.stop, rows)
    return [slice(s, min(s + size, stop)) for s in range(part.start, stop, size)]


def first_kernel(
    rows, tok, mask, mt, gain, shift, wq, wk, wv, bq, bv,
    normed, q, k, v, ctx, log,
):
    normed_ref = normed.near
    tok_ref, mask_ref = tok.ref, mask.ref
    mt_ref, gain_ref, shift_ref = mt.ref, gain.ref, shift.ref
    for block in blocks_within(slice(0, rows), rows):
        initial = jnp.where(mask_ref[block] > 0, mt_ref[...], tok_ref[block].astype(F32))
        center, inv = moments(initial)
        normed_ref[block] = (center * inv * gain_ref[...] + shift_ref[...]).astype(BF16)
    over = padded(rows) - rows
    normed_ref[rows:] = jnp.zeros((over, normed_ref.shape[1]), BF16)
    normed.send()
    project(normed_ref, [wq, wk, wv], bq, bv, q, k, v)
    attend(rows, q.near, k.near, v.near, ctx.near, log.near)
    ctx.send()
    log.send()


def project(normed_ref, weights, bq, bv, q, k, v):
    scale = BF16(1.0 / math.sqrt(HD))
    wq, wk, wv = weights
    q.near[...] = (nn(normed_ref[...], wq.ref[...]) + bq.ref[...]).astype(BF16) * scale
    q.send()
    k.near[...] = nn(normed_ref[...], wk.ref[...]).astype(BF16)
    k.send()
    v.near[...] = (nn(normed_ref[...], wv.ref[...]) + bv.ref[...]).astype(BF16)
    v.send()


class Third:
    def __init__(self, moved, i):
        self.moved, self.i = moved, i

    @property
    def ref(self):
        return self.moved.part(self.i)


def second_kernel(
    rows, normed, joined, bq, bv, ctx, wo, wo2, bo,
    s1, gain, shift, tok, mask, mt, cot, s2,
    q, k, v, ctx2, log, middle, normed2, go, sums, acc_ref,
):
    project(normed.ref, [Third(joined, i) for i in range(3)], bq, bv, q, k, v)
    attend(rows, q.near, k.near, v.near, ctx2.near, log.near)
    ctx2.send()
    log.send()
    over = padded(rows) - rows
    width = acc_ref.shape[1]
    total = jnp.zeros((1, width), F32)
    ctx_ref, wo_ref, wo2_ref = ctx.ref, wo.ref, wo2.ref
    tok_ref, mask_ref, cot_ref = tok.ref, mask.ref, cot.ref
    bo_ref, s1_ref, gain_ref, shift_ref, mt_ref, s2_ref = (v.ref for v in (bo, s1, gain, shift, mt, s2))
    for half in halves_of(padded(rows)):
        acc_ref[half] = nn(ctx_ref[half], wo_ref[...]) + nn(ctx2.near[half], wo2_ref[...])
    for half in halves_of(padded(rows)):
        for block in blocks_within(half, rows):
            masked = mask_ref[block] > 0
            initial = jnp.where(masked, mt_ref[...], tok_ref[block].astype(F32))
            one = initial + s1_ref[...] * (acc_ref[block] + bo_ref[...])
            middle.near[block] = one
            center, inv = moments(one)
            normed2.near[block] = (center * inv * gain_ref[...] + shift_ref[...]).astype(BF16)
            grad_out = jnp.where(masked, cot_ref[block].astype(F32), 0.0) * s2_ref[...]
            grad_out = grad_out.astype(BF16)
            go.near[block] = grad_out
            total += col_sum(grad_out.astype(F32))
        if half.stop == padded(rows):
            middle.near[rows:] = jnp.zeros((over, width), F32)
            normed2.near[rows:] = jnp.zeros((over, width), BF16)
            go.near[rows:] = jnp.zeros((over, width), BF16)
        for one in (normed2, go, middle):
            one.send(half)
    sums.near[...] = total
    sums.send()


def feed_kernel(chunk, n2, wu, go, wd, bu, hidden, gp, grads, sums, scale_sum):
    me = lax.axis_index("dp")
    cols = hidden.near.shape[1]
    width = n2.near.shape[1]
    lanes = None
    for i in range(cols // chunk):
        at = slice(i * chunk, (i + 1) * chunk)
        pre = nn(n2.ref[...], wu.part(i)[...]) + bu.ref[:, at]
        grad_hidden = nt(go.ref[...], wd.part(i)[...])
        cdf, slope = gelu_parts(pre)
        new_hidden = (pre * cdf).astype(BF16)
        grad_pre = (grad_hidden * (cdf + slope)).astype(BF16)
        hidden.near[:, at] = new_hidden
        gp.near[:, at] = grad_pre
        hidden.send((slice(None), at))
        gp.send((slice(None), at))
        sums.near[:, at] = col_sum(grad_pre.astype(F32))
        down = tn(go.ref[...], new_hidden)
        weighed = down * wd.part(i)[...].T.astype(F32)
        for k in range(0, chunk, 128):
            part = weighed[:, k : k + 128]
            lanes = part if lanes is None else lanes + part
        for j, grad in enumerate((down, tn(n2.ref[...], grad_pre))):
            base = (2 * i + j) * chunk
            store_blocks(me, grad, grads.near, base)
            grads.send((slice(None), slice(None), slice(base, base + chunk)))
    sums.send()
    scale_sum.near[...] = col_sum(lanes.T)
    scale_sum.send()


def store_blocks(me, product_rows, out_ref, at):
    parts, size, _ = out_ref.shape
    cols = product_rows.shape[1]
    for b in range(parts):
        out_ref[b ^ me, :, at : at + cols] = product_rows[b * size : (b + 1) * size].astype(BF16)


def in_pieces(*groups):
    for some in zip(*groups):
        for j in range(len(some[0].pieces)):
            yield [functools.partial(one.part, j) for one in some]


def middle_kernel(rows, count, *refs):
    gps, wus = refs[:count], refs[count : 2 * count]
    middle, tok, mask, mt, cot, gain, s1 = refs[2 * count : 2 * count + 7]
    gm, gbr, sums, acc_ref = refs[2 * count + 7 :]
    width = acc_ref.shape[1]
    total = [jnp.zeros((1, width), F32)] * 4
    halves = halves_of(padded(rows))
    for i, (one, w) in enumerate(in_pieces(gps, wus)):
        for half in halves:
            part = nt(one()[half], w()[...])
            acc_ref[half] = part if i == 0 else acc_ref[half] + part
    middle_ref, tok_ref, mask_ref, cot_ref = middle.ref, tok.ref, mask.ref, cot.ref
    mt_ref, gain_ref, s1_ref = mt.ref, gain.ref, s1.ref
    over = padded(rows) - rows
    for half in halves:
        for block in blocks_within(half, rows):
            masked = mask_ref[block] > 0
            one = middle_ref[block]
            back, grad_gain, grad_shift = norm_pull(one, gain_ref[...], acc_ref[block])
            grad_middle = jnp.where(masked, cot_ref[block].astype(F32), 0.0) + back
            gm.near[block] = grad_middle
            grad_branch = (s1_ref[...] * grad_middle).astype(BF16)
            gbr.near[block] = grad_branch
            initial = jnp.where(masked, mt_ref[...], tok_ref[block].astype(F32))
            new = (
                grad_gain,
                grad_shift,
                col_sum(grad_middle * (one - initial)) / s1_ref[...],
                col_sum(grad_branch.astype(F32)),
            )
            total = [a + b for a, b in zip(total, new)]
        if half.stop == padded(rows):
            gm.near[rows:] = jnp.zeros((over, width), F32)
            gbr.near[rows:] = jnp.zeros((over, width), BF16)
        gbr.send(half)
        gm.send(half)
    for i, one in enumerate(total):
        sums.near[i : i + 1] = one
    sums.send()


def back_kernel(
    rows, gbr, wo, ctx, q, k, v, log, n1,
    dq, dk, dv, grads, sums, gc_ref,
):
    me = lax.axis_index("dp")
    cols = dq.near.shape[1]
    gc_ref[...] = nt(gbr.ref[...], wo.ref[...]).astype(BF16)
    store_blocks(me, tn(gbr.ref[...], ctx.ref[...]), grads.near, 3 * cols)
    grads.send((slice(None), slice(None), slice(3 * cols, 4 * cols)))
    attend_back(rows, q.ref, k.ref, v.ref, gc_ref, log.ref, dq.near, dk.near, dv.near)
    for i, one in enumerate((dq, dk, dv)):
        one.send()
        store_blocks(me, tn(n1.ref[...], one.near[...]), grads.near, i * cols)
        grads.send((slice(None), slice(None), slice(i * cols, (i + 1) * cols)))
        if i != 1:
            at = i // 2 * cols
            sums.near[:, at : at + cols] = col_sum(one.near[...].astype(F32))
    sums.send()


def middle_back_kernel(rows, count, *refs):
    first, others = refs[: 2 * count + 7], refs[2 * count + 7 : 2 * count + 14]
    (gm, gbr, sums), outs = refs[2 * count + 14 : 2 * count + 17], refs[2 * count + 17 : 2 * count + 22]
    acc_ref, gc_ref = refs[2 * count + 22 :]
    middle_kernel(rows, count, *first, gm, gbr, sums, acc_ref)
    back_kernel(rows, gbr, *others, *outs, gc_ref)


def input_kernel(rows, *refs):
    grads, weights = refs[:6], list(refs[6:9]) + [Third(refs[9], i) for i in range(3)]
    tok, mask, mt, gain, gm, out, sums, acc_ref = refs[10:]
    width = acc_ref.shape[1]
    halves = halves_of(padded(rows))
    for i, (one, w) in enumerate(zip(grads, weights)):
        for half in halves:
            part = nt(one.ref[half], w.ref[...])
            acc_ref[half] = part if i == 0 else acc_ref[half] + part
    total = [jnp.zeros((1, width), F32)] * 3
    tok_ref, mask_ref, gm_ref, mt_ref, gain_ref = tok.ref, mask.ref, gm.ref, mt.ref, gain.ref
    for half in halves:
        for block in blocks_within(half, rows):
            masked = mask_ref[block] > 0
            initial = jnp.where(masked, mt_ref[...], tok_ref[block].astype(F32))
            back, grad_gain, grad_shift = norm_pull(initial, gain_ref[...], acc_ref[block])
            grad_initial = gm_ref[block] + back
            out.near[block] = jnp.where(masked, 0.0, grad_initial)
            new = (col_sum(jnp.where(masked, grad_initial, 0.0)), grad_gain, grad_shift)
            total = [a + b for a, b in zip(total, new)]
    out.send()
    for i, one in enumerate(total):
        sums.near[i : i + 1] = one
    sums.send()


def output_kernel(rows, count, *refs):
    hiddens, wds = refs[:count], refs[count : 2 * count]
    middle, bd, s2, out, acc_ref = refs[2 * count :]
    halves = halves_of(padded(rows))
    for i, (one, w) in enumerate(in_pieces(hiddens, wds)):
        for half in halves:
            part = nn(one()[half], w()[...])
            acc_ref[half] = part if i == 0 else acc_ref[half] + part
    middle_ref, bd_ref, s2_ref = middle.ref, bd.ref, s2.ref
    for block in blocks_within(slice(0, rows), rows):
        output = acc_ref[block] + bd_ref[...]
        out.near[block] = (middle_ref[block] + s2_ref[...] * output).astype(BF16)
    out.send()


def shape_of(shape, dtype=BF16):
    return jax.ShapeDtypeStruct(shape, dtype)


def cost(flops, *arrays):
    moved = sum(a.size * a.dtype.itemsize for a in arrays)
    return pl.CostEstimate(flops=flops, bytes_accessed=moved, transcendentals=0)


def without(kernel, at, count):
    def inner(*refs):
        kernel(*refs[:at], *refs[at + count :])

    return inner


def pairs(n, bit):
    return [(i, i ^ (1 << bit)) for i in range(n)]


TILE = 256


class Segment:
    def __init__(self, terms, start, width, order):
        self.start, self.width, self.order, self.used, self.got = start, width, list(order), [], []
        self.bits = sorted(order, reverse=True)
        dims = (2,) * len(self.bits)
        self.terms = [(a.reshape(dims + a.shape[1:]), base + start) for a, base in terms]
        self.rows = terms[0][0].shape[1]
        self.across = width // TILE

    @property
    def rest(self):
        return self.order[1:]

    @property
    def tiles(self):
        return self.across << len(self.rest)

    def views(self):
        bit, found = self.order[0] if self.order else None, []
        for array, start in self.terms:
            one = View(array)
            one.index = tuple(0 if b in self.used else 1 if b == bit else slice(None) for b in self.bits)
            one.index += (slice(None), slice(start, start + self.width))
            one.shape = (2,) * len(self.rest) + (self.rows, self.width)
            found.append(one)
        for array, start in self.got:
            found.append(View(array, 0, start + (self.tiles if self.order else 0), self.tiles))
        return found

    def add(self, refs):
        originals, got = refs[: len(self.terms)], refs[len(self.terms) :]
        for at in range(1 << len(self.rest)):
            side = {b: at >> (len(self.rest) - 1 - i) & 1 for i, b in enumerate(self.rest)}
            index = tuple(side[b] for b in self.bits if b in side)
            for c in range(self.across):
                cols, tile = slice(c * TILE, (c + 1) * TILE), at * self.across + c
                parts = [ref[(*index, slice(None), cols)] for ref in originals] + [ref[tile] for ref in got]
                yield tile, self.start + c * TILE, functools.reduce(jnp.add, [p.astype(F32) for p in parts])

    def received(self, array, start):
        self.used.append(self.order.pop(0))
        self.got.append((array, start))


class Group:
    def __init__(self, segments, block):
        self.segments, self.block, self.result = segments, block, None
        self.width = sum(s.width for s in segments)

    @property
    def last(self):
        return not self.segments[0].order


class Sums:
    def __init__(self, same, own, other, bits, last):
        self.parts, self.own, self.n_own, self.last_terms = same + other, same + own, len(own), last
        self.rounds = [bits[i : i + 2] for i in range(0, len(bits), 2)]
        self.stage, self.terms, self.result = 0, [], None

    def job(self):
        width = self.parts[0].shape[1]
        height = -(-sum(p.size for p in self.parts) // (8 * width)) * 8
        packed = {0: self.parts, 1: self.own}.get(self.stage, [])
        places, row, col = [], 0, 0
        for p in packed:
            steps = []
            for at in range(0, p.shape[1], width):
                size = min(width, p.shape[1] - at)
                steps.append(((slice(row, row + p.shape[0]), slice(col, col + size)), slice(at, at + size)))
                col += size
                if col == width:
                    row, col = row + p.shape[0], 0
            places.append(steps)
        return packed, places, self.terms, shape_of((height, width), F32)

    def final_shapes(self):
        own = self.own[len(self.own) - self.n_own :]
        width = own[0].shape[1]
        return [shape_of((1, width), F32)] * 9 + [shape_of((1, width // 2), F32)] * 2 + [
            shape_of((1, width * (len(own) - 1)), F32)
        ]

    def final(self, total, ins, outs):
        bias, scale = (one.ref[...] for one in ins)
        start = sum(p.shape[0] for p in self.own[: len(self.own) - self.n_own])
        rows = [total[i : i + 1] for i in range(total.shape[0])]
        for out, value in zip(outs, rows[:8]):
            out.near[...] = value
        outs[8].near[...] = (functools.reduce(jnp.add, rows[8:start]) + bias * rows[7]) / scale
        half = outs[9].near.shape[1]
        outs[9].near[...] = rows[start][:, :half]
        outs[10].near[...] = rows[start][:, half:]
        for i, value in enumerate(rows[start + 1 : start + self.n_own]):
            outs[11].near[:, i * 2 * half : (i + 1) * 2 * half] = value

    @property
    def last(self):
        return self.stage == len(self.rounds) + 1

    def take(self, sent):
        n = lax.axis_size("dp")
        if self.last:
            self.result = sent
        elif self.stage == 0:
            self.terms = [swap(sent[0])]
        else:
            bits = self.rounds[self.stage - 1]
            self.terms = list(sent)
            for some in range(1, 1 << len(bits)):
                flip = sum(1 << b for i, b in enumerate(bits) if some >> i & 1)
                self.terms.append(lax.ppermute(sent[0], "dp", [(d, d ^ flip) for d in range(n)]))
        self.stage += 1


def exchange(groups, after, sums=None, carry=None):
    buffers, shapes, plan = {}, [], []
    for segment in [s for g in groups if not g.last for s in g.segments]:
        buffers.setdefault(segment.order[0], []).append(segment)
    for some in buffers.values():
        starts = [sum(s.tiles for s in some[:i]) for i in range(len(some))]
        plan.append(list(zip(some, starts)))
        shapes.append(shape_of((sum(s.tiles for s in some), some[0].rows, TILE)))
    ending = [g for g in groups if g.last]
    for g in ending:
        shapes += [shape_of((g.segments[0].rows, g.block), F32)] * (g.width // g.block)
    views = [s.views() for one in plan for s, _ in one] + [s.views() for g in ending for s in g.segments]
    counts = [len(v) for v in views]
    views = [v for some in views for v in some]
    n_summed = len(shapes)
    packed, places, terms = [], [], []
    sums_last = sums is not None and sums.last
    if sums is not None:
        packed, places, terms, shape = sums.job()
        views += [View(a) for a in packed + terms + (sums.last_terms if sums_last else [])]
        shapes += sums.final_shapes() if sums_last else [shape]
    passed = [] if carry is None else [carry]
    hbm = pl.BlockSpec(memory_space=pl.ANY)
    skipped, n_in, n_out = len(after) + len(passed), len(views), len(shapes)

    def kernel(*refs):
        far_in, far_out = refs[skipped : skipped + n_in], refs[skipped + n_in :][:n_out]
        nears = list(refs[skipped + n_in + n_out + len(passed) :])
        line = Line(nears.pop(), n_in + n_out)
        ins = []
        for far, view in zip(far_in, views):
            far = far if view.index is None else far.at[view.index]
            ins.append(Moved(far, nears.pop(0), line))
        line.begin()
        outs = [Moved(far, nears.pop(0), line, ()) for far in far_out]
        sizes = list(counts)

        def taken():
            return [ins.pop(0).ref for _ in range(sizes.pop(0))]

        for one in plan:
            out = outs.pop(0)
            for segment, start in one:
                for tile, _, total in segment.add(taken()):
                    out.near[start + tile] = total.astype(BF16)
            out.send()
        for g in ending:
            mine = [outs.pop(0) for _ in range(g.width // g.block)]
            for segment in g.segments:
                for _, col, total in segment.add(taken()):
                    mine[col // g.block].near[:, col % g.block : col % g.block + TILE] = total
            for out in mine:
                out.send()
        if sums is not None:
            if packed:
                new = outs[0]
                new.near[...] = ins[-1].ref[...] if terms else jnp.zeros(shape.shape, F32)
                for one, steps in zip(ins, places):
                    for place, cols in steps:
                        new.near[place] += one.ref[:, cols]
            else:
                total = functools.reduce(jnp.add, [one.ref[...] for one in ins[: len(terms)]])
                if sums_last:
                    sums.final(total, ins[len(terms) :], outs)
                else:
                    outs[0].near[...] = total
            for out in outs:
                out.send()
        line.finish()

    outs = pl.pallas_call(
        kernel,
        in_specs=[hbm] * (skipped + n_in),
        out_specs=[hbm] * (n_out + len(passed)),
        out_shape=shapes + [shape_of(p.shape, p.dtype) for p in passed],
        input_output_aliases={len(after): n_out} if passed else {},
        scratch_shapes=[pltpu.VMEM(v.shape, v.array.dtype) for v in views]
        + [pltpu.VMEM(o.shape, o.dtype) for o in shapes]
        + [pltpu.SemaphoreType.DMA((n_in + n_out,))],
        compiler_params=pltpu.CompilerParams(vmem_limit_bytes=EXCHANGE_VMEM),
        cost_estimate=cost(0, *shapes),
        name="exchange",
    )(*after, *passed, *[v.array for v in views])
    n, left = lax.axis_size("dp"), list(outs[:n_summed])
    for bit, one in zip(buffers, plan):
        got = lax.ppermute(left.pop(0), "dp", pairs(n, bit))
        for segment, start in one:
            segment.received(got, start)
    for g in ending:
        g.result = [left.pop(0) for _ in range(g.width // g.block)]
    if sums is not None:
        sums.take(list(outs[n_summed:n_out]))
    sent = list(outs[:n_out])
    return sent if carry is None else (sent, outs[-1])


def swap(array):
    return lax.ppermute(array, "tp", [(0, 1), (1, 0)])


def local_body(
    tokens, masked, cotangent, mask_token, gain_one, shift_one, w_query, w_key, w_value, b_query,
    b_value, w_out, b_out, scale_one, gain_two, shift_two, w_up, b_up, w_down, b_down, scale_two,
):
    rows, width = tokens.shape
    tall = padded(rows)
    half = w_query.shape[1]
    units = w_up.shape[1]
    n = lax.axis_size("dp")
    bits = n.bit_length() - 1
    me = lax.axis_index("dp").astype(jnp.int32).reshape(1)
    biases = jnp.concatenate([b_query, b_value, b_up]).reshape(1, -1)

    joined2 = swap(jnp.concatenate([w_query, w_key, w_value], axis=1))
    biases2 = swap(biases)
    wo2 = swap(w_out)
    wu2, wd2 = swap(w_up), swap(w_down)
    row = lambda v: v.reshape(1, -1)
    bq2, bv2 = View(biases2, 1, 0, half), View(biases2, 1, half, half)
    bq, bv, bu = row(b_query), row(b_value), row(b_up)
    mt, g1, s1, bo, sc1 = row(mask_token), row(gain_one), row(shift_one), row(b_out), row(scale_one)
    g2, s2, bd, sc2 = row(gain_two), row(shift_two), row(b_down), row(scale_two)
    mask = masked.reshape(rows, 1)

    narrow = shape_of((tall, half))
    wide = shape_of((tall, width))
    attend_flops = 2 * 2 * 256 * SEQ * rows * half // HD
    logs = shape_of(norm_rows(rows, half), F32)
    normed, q, k, v, ctx, log = moved_call(
        functools.partial(first_kernel, rows),
        [wide, narrow, narrow, narrow, narrow, logs],
        (tokens, mask, mt, g1, s1, w_query, w_key, w_value, bq, bv),
        6 * rows * width * half + attend_flops,
        6,
        name="first",
        waves=[[(i, 0) for i in range(5)]],
    )
    tall_f32 = shape_of((tall, width), F32)
    scratch = [pltpu.VMEM((tall, width), F32)]
    one_row = shape_of((1, width), F32)
    q2, k2, v2, ctx2, log2, middle, normed2, go, sum_go = moved_call(
        functools.partial(second_kernel, rows),
        [narrow, narrow, narrow, narrow, logs, tall_f32, wide, wide, one_row],
        (normed, joined2, bq2, bv2, ctx, w_out, wo2, bo, sc1, g2, s2, tokens, mask, mt, cotangent, sc2),
        10 * rows * width * half + attend_flops,
        12,
        scratch=scratch,
        name="second",
        cuts={1: (1, 3)},
        waves=[[(0, 0), (1, 0), (2, 0)], [(1, 1), (1, 2), (3, 0)]],
    )

    natural = tuple(range(bits))
    by_x, by_y = natural, natural[1:2] + natural[0:1] + natural[2:]
    by_z = natural[2 % bits :] + natural[: 2 % bits]

    part = units // 2
    chunk = min(1024, part)
    hiddens, gps, ups, downs = [], [], [], []

    def feed(weights, first, size, after=()):
        w_up, w_down, b_up, b_start = weights
        count = size // chunk
        hidden, gp, grads, sums, scale_sum = moved_call(
            functools.partial(feed_kernel, chunk),
            [
                shape_of((tall, size)),
                shape_of((tall, size)),
                shape_of((n, width // n, 2 * size)),
                shape_of((1, size), F32),
                one_row,
            ],
            (normed2, View(w_up, 1, first, size), go, View(w_down, 0, first, size),
             View(b_up, 1, b_start + first, size)),
            8 * tall * width * size,
            4 * count + 2,
            name="feed",
            after=after,
            cuts={1: (1, count), 3: (0, count)},
            waves=[[(i, 0) for i in range(5)]],
        )
        hiddens.append(hidden)
        gps.append(gp)
        ups.append(View(w_up, 1, first, size))
        downs.append(View(w_down, 0, first, size))
        scale_sums.append(scale_sum)
        return grads, sums

    def grouped(size, block, *terms, third=None):
        parts = ((0, 3, by_x), (3, 3, by_y), (6, 2, third or by_z))
        return Group([Segment(terms, at * size // 8, w * size // 8, o) for at, w, o in parts], block)

    mine, other = (w_up, w_down, bu, 0), (wu2, wd2, biases2, 2 * half)
    scale_sums = []
    theirs, sums_up2 = feed(other, 0, units)
    theirs = swap(theirs)
    own, sums_up_a = feed(mine, 0, part, [sums_up2])
    a = grouped(2 * part, chunk, (own, 0), (theirs, 0))
    sent = exchange([a], [sums_up_a])
    own, sums_up_b = feed(mine, part, part, sent)
    b = grouped(2 * part, chunk, (own, 0), (theirs, 2 * part))
    sent = exchange([a, b], [sums_up_b])

    back_outs = [narrow, narrow, narrow, shape_of((n, width // n, 4 * half)), shape_of((1, 2 * half), F32)]
    back_flops = 10 * rows * width * half + 3 * attend_flops
    back_scratch = [pltpu.VMEM((tall, half), BF16)]
    gm, gbr, sums_two, dq2, dk2, dv2, gw2, sums_b2 = moved_call(
        functools.partial(middle_back_kernel, rows, len(gps)),
        [tall_f32, wide, shape_of((4, width), F32)] + back_outs,
        (*gps, *ups, middle, tokens, mask, mt, cotangent, g2, sc1, wo2, ctx2, q2, k2, v2, log2, normed),
        8 * tall * width * part + back_flops,
        13,
        scratch=scratch + back_scratch,
        name="middle",
        after=sent,
        cuts={0: (1, 2), 3: (1, 2)},
        waves=[[(0, 0), (3, 0)], [(0, 1), (3, 1)], [(1, 0), (4, 0)], [(2, 0), (5, 0)]],
    )
    sent, gw2 = exchange([a, b], [sums_b2], carry=gw2)
    gw2 = swap(gw2)

    def back(wo, ctx, q, k, v, log, after):
        return moved_call(
            functools.partial(back_kernel, rows),
            back_outs,
            (gbr, wo, ctx, q, k, v, log, normed),
            back_flops,
            8,
            scratch=back_scratch,
            name="back",
            after=after,
            waves=[[(0, 0), (1, 0)], [(2, 0)]],
        )

    dq, dk, dv, gw, sums_b = back(w_out, ctx, q, k, v, log, sent)
    by_z_last = natural[2:3] + natural[:2] + natural[3:]
    c = grouped(4 * half, half, (gw, 0), (gw2, 0), third=by_z_last)
    sent = exchange([c, b, a], [sums_b])

    grad_tokens, sums_one = moved_call(
        functools.partial(input_kernel, rows),
        [shape_of((rows, width), F32), shape_of((3, width), F32)],
        (dq, dk, dv, dq2, dk2, dv2, w_query, w_key, w_value, joined2, tokens, mask, mt, g1, gm),
        12 * rows * width * half,
        2,
        scratch=scratch,
        cuts={9: (1, 3)},
        waves=[[(0, 0), (6, 0)], [(1, 0), (7, 0)], [(2, 0), (8, 0), (3, 0), (9, 0)]],
        name="input",
        after=sent,
    )
    same = [sums_one, sums_two, sum_go, *scale_sums]
    sums = Sums(same, [sums_b, sums_up_a, sums_up_b], [sums_b2, sums_up2], list(natural), [bd, sc2])
    sent = exchange([c, b, a], [sums_one], sums=sums)
    block_out = moved_call(
        functools.partial(output_kernel, rows, len(hiddens)),
        [shape_of((rows, width))],
        (*hiddens, *downs, middle, bd, sc2),
        8 * tall * width * part,
        1,
        scratch=scratch,
        cuts={0: (1, 2), 3: (0, 2)},
        waves=[[(0, 0), (3, 0)], [(0, 1), (3, 1)], [(1, 0), (4, 0)], [(2, 0), (5, 0)]],
        name="output",
        after=sent,
    )[0]
    last = block_out
    while sums.result is None:
        last = exchange([g for g in (c, b, a) if g.result is None], [last], sums=sums)[-1]

    done = [one for group in (a, b) for one in group.result]
    grad_w_down = jnp.concatenate(done[0::2], axis=1).T
    grad_w_up = jnp.concatenate(done[1::2], axis=1)
    grad_w_query, grad_w_key, grad_w_value, grad_w_out = c.result
    (grad_mask_token, grad_gain_one, grad_shift_one, grad_gain_two, grad_shift_two, grad_scale_one, grad_b_out,
     grad_b_down, grad_scale_two, grad_b_query, grad_b_value, grad_b_up) = (
        one.reshape(-1) for one in sums.result
    )
    return (
        block_out,
        grad_tokens,
        grad_mask_token,
        grad_gain_one,
        grad_shift_one,
        grad_w_query,
        grad_w_key,
        grad_w_value,
        grad_b_query,
        grad_b_value,
        grad_w_out.T,
        grad_b_out,
        grad_scale_one,
        grad_gain_two,
        grad_shift_two,
        grad_w_up,
        grad_b_up,
        grad_w_down,
        grad_b_down,
        grad_scale_two,
    )


def solution(mesh):
    placed = (
        P(("dp", "tp"), None),
        P(("dp", "tp")),
        P(("dp", "tp"), None),
        P(),
        P(),
        P(),
        P(None, "tp"),
        P(None, "tp"),
        P(None, "tp"),
        P("tp"),
        P("tp"),
        P("tp", None),
        P(),
        P(),
        P(),
        P(),
        P(None, "tp"),
        P("tp"),
        P("tp", None),
        P(),
        P(),
    )
    fits = mesh.shape["tp"] == 2 and mesh.shape["dp"].bit_count() == 1
    return jax.shard_map(
        local_body if fits else gathered_body,
        mesh=mesh,
        in_specs=placed,
        out_specs=(
            P(("dp", "tp"), None),
            P(("dp", "tp"), None),
            P(),
            P(),
            P(),
            P("dp", "tp"),
            P("dp", "tp"),
            P("dp", "tp"),
            P("tp"),
            P("tp"),
            P("tp", "dp"),
            P(),
            P(),
            P(),
            P(),
            P("dp", "tp"),
            P("tp"),
            P("tp", "dp"),
            P(),
            P(),
        ),
        check_vma=False,
    )
```

```python
import functools
import math

import jax
import jax.numpy as jnp
from jax import lax
from jax.experimental import pallas as pl
from jax.experimental.pallas import tpu as pltpu
from jax.sharding import PartitionSpec as P

SEQ = 197
HD = 64
PAIR = 2 * HD
EPSILON = 1e-06
BF16 = jnp.bfloat16
F32 = jnp.float32
MIB = 2**20
LOWEST = -1e30
KERNEL_VMEM = 64 * MIB
EXCHANGE_VMEM = 64 * MIB

def layer_norm(rows_in, gain_vec, shift_vec):
    center = rows_in - jnp.mean(rows_in, axis=-1, keepdims=True)
    spread = jnp.mean(center * center, axis=-1, keepdims=True)
    return center * lax.rsqrt(spread + EPSILON) * gain_vec + shift_vec


def norm_backward(rows_in, gain_vec, shift_vec, grad_rows):
    unused, pull = jax.vjp(layer_norm, rows_in, gain_vec, shift_vec)
    return pull(grad_rows)


def gelu_exact(values):
    return jax.nn.gelu(values, approximate=False)


def product(left, right):
    return jnp.dot(left, right, preferred_element_type=jnp.float32)


def times_transposed(left, right):
    return lax.dot_general(
        left, right, (((1,), (1,)), ((), ())), preferred_element_type=jnp.float32
    )


def transposed_times(left, right):
    return lax.dot_general(
        left, right, (((0,), (0,)), ((), ())), preferred_element_type=jnp.float32
    )


def attend_forward(queries, key_rows, values, factor):
    scores = (
        jnp.einsum("iqhd,ikhd->ihqk", queries, key_rows, preferred_element_type=jnp.float32)
        * factor
    )
    row_max = jnp.max(scores, axis=-1, keepdims=True)
    raised = jnp.exp(scores - row_max)
    sum_exp = jnp.sum(raised, axis=-1, keepdims=True)
    probs_low = (raised / sum_exp).astype(jnp.bfloat16)
    context = jnp.einsum("ihqk,ikhd->iqhd", probs_low, values, preferred_element_type=jnp.float32)
    return (context, row_max + jnp.log(sum_exp))


def attend_backward(queries, key_rows, values, log_total, grad_context, factor):
    scores = (
        jnp.einsum("iqhd,ikhd->ihqk", queries, key_rows, preferred_element_type=jnp.float32)
        * factor
    )
    probs = jnp.exp(scores - log_total)
    grad_probs = jnp.einsum(
        "iqhd,ikhd->ihqk", grad_context, values, preferred_element_type=jnp.float32
    )
    inner = jnp.sum(grad_probs * probs, axis=-1, keepdims=True)
    grad_scores = (probs * (grad_probs - inner)).astype(jnp.bfloat16)
    grad_queries = (
        jnp.einsum("ihqk,ikhd->iqhd", grad_scores, key_rows, preferred_element_type=jnp.float32)
        * factor
    )
    grad_keys = (
        jnp.einsum("ihqk,iqhd->ikhd", grad_scores, queries, preferred_element_type=jnp.float32)
        * factor
    )
    grad_values = jnp.einsum(
        "ihqk,iqhd->ikhd",
        probs.astype(jnp.bfloat16),
        grad_context,
        preferred_element_type=jnp.float32,
    )
    return (grad_queries, grad_keys, grad_values)


def gathered_body(
    tokens,
    masked,
    cotangent,
    mask_token,
    gain_one,
    shift_one,
    w_query,
    w_key,
    w_value,
    b_query,
    b_value,
    w_out,
    b_out,
    scale_one,
    gain_two,
    shift_two,
    w_up,
    b_up,
    w_down,
    b_down,
    scale_two,
):
    local_cols = w_query.shape[1]
    local_heads = local_cols // HD
    factor = 1.0 / math.sqrt(HD)
    chosen = (masked > 0)[:, None]
    initial = jnp.where(chosen, mask_token[None, :], tokens.astype(jnp.float32))
    normed = layer_norm(initial, gain_one, shift_one).astype(jnp.bfloat16)
    w_joined = jnp.concatenate([w_query, w_key, w_value], axis=1)
    b_joined = jnp.concatenate([b_query, jnp.zeros_like(b_query), b_value])
    gathered = lax.all_gather(normed, "tp", axis=0, tiled=True)
    joined = (product(gathered, w_joined) + b_joined).astype(jnp.bfloat16)
    group_rows = gathered.shape[0]
    head_shape = (group_rows // SEQ, SEQ, local_heads, HD)
    queries = joined[:, :local_cols].reshape(head_shape)
    key_rows = joined[:, local_cols : 2 * local_cols].reshape(head_shape)
    values = joined[:, 2 * local_cols :].reshape(head_shape)
    context, log_total = attend_forward(queries, key_rows, values, factor)
    context = context.reshape(group_rows, local_cols).astype(jnp.bfloat16)
    branch = (
        lax.psum_scatter(
            product(context, w_out).astype(jnp.bfloat16), "tp", scatter_dimension=0, tiled=True
        ).astype(jnp.float32)
        + b_out
    )
    middle = initial + scale_one * branch
    normed_two = layer_norm(middle, gain_two, shift_two).astype(jnp.bfloat16)
    gathered_two = lax.all_gather(normed_two, "tp", axis=0, tiled=True)
    pre_act = product(gathered_two, w_up) + b_up
    hidden = gelu_exact(pre_act).astype(jnp.bfloat16)
    output = (
        lax.psum_scatter(
            product(hidden, w_down).astype(jnp.bfloat16), "tp", scatter_dimension=0, tiled=True
        ).astype(jnp.float32)
        + b_down
    )
    block_out = (middle + scale_two * output).astype(jnp.bfloat16)
    grad_block = cotangent.astype(jnp.float32) * chosen.astype(jnp.float32)
    grad_output = (scale_two * grad_block).astype(jnp.bfloat16)
    grad_scale_two = jnp.sum(grad_block * output, axis=0)
    grad_b_down = jnp.sum(grad_output.astype(jnp.float32), axis=0)
    portion = lax.all_gather(grad_output, "tp", axis=0, tiled=True)
    grad_hidden = times_transposed(portion, w_down)
    grad_w_down = transposed_times(hidden, portion)
    grad_hidden, grad_w_down = (grad_hidden, grad_w_down)
    unused, gelu_pull = jax.vjp(gelu_exact, pre_act)
    grad_pre = gelu_pull(grad_hidden)[0].astype(jnp.bfloat16)
    grad_b_up = jnp.sum(grad_pre.astype(jnp.float32), axis=0)
    grad_normed_two = lax.psum_scatter(
        times_transposed(grad_pre, w_up).astype(jnp.bfloat16), "tp", scatter_dimension=0, tiled=True
    ).astype(jnp.float32)
    grad_w_up = transposed_times(lax.all_gather(normed_two, "tp", axis=0, tiled=True), grad_pre)
    grad_middle_norm, grad_gain_two, grad_shift_two = norm_backward(
        middle, gain_two, shift_two, grad_normed_two
    )
    grad_middle = grad_block + grad_middle_norm
    grad_branch = (scale_one * grad_middle).astype(jnp.bfloat16)
    grad_scale_one = jnp.sum(grad_middle * branch, axis=0)
    grad_b_out = jnp.sum(grad_branch.astype(jnp.float32), axis=0)
    portion = lax.all_gather(grad_branch, "tp", axis=0, tiled=True)
    grad_context = times_transposed(portion, w_out)
    grad_w_out = transposed_times(context, portion)
    grad_context, grad_w_out = (grad_context, grad_w_out)
    grad_context = grad_context.astype(jnp.bfloat16).reshape(head_shape)
    grad_queries, grad_keys, grad_values = attend_backward(
        queries, key_rows, values, log_total, grad_context, factor
    )
    grad_joined = jnp.concatenate(
        [
            grad_queries.reshape(group_rows, local_cols),
            grad_keys.reshape(group_rows, local_cols),
            grad_values.reshape(group_rows, local_cols),
        ],
        axis=1,
    ).astype(jnp.bfloat16)
    grad_b_query = jnp.sum(grad_joined[:, :local_cols].astype(jnp.float32), axis=0)
    grad_b_value = jnp.sum(grad_joined[:, 2 * local_cols :].astype(jnp.float32), axis=0)
    grad_normed = lax.psum_scatter(
        times_transposed(grad_joined, w_joined).astype(jnp.bfloat16),
        "tp",
        scatter_dimension=0,
        tiled=True,
    ).astype(jnp.float32)
    grad_w_joined = transposed_times(lax.all_gather(normed, "tp", axis=0, tiled=True), grad_joined)
    grad_initial_norm, grad_gain_one, grad_shift_one = norm_backward(
        initial, gain_one, shift_one, grad_normed
    )
    grad_initial = grad_middle + grad_initial_norm
    grad_tokens = jnp.where(chosen, 0.0, grad_initial)
    grad_mask_token = jnp.sum(jnp.where(chosen, grad_initial, 0.0), axis=0)
    (
        grad_mask_token,
        grad_gain_one,
        grad_shift_one,
        grad_b_out,
        grad_scale_one,
        grad_gain_two,
        grad_shift_two,
        grad_b_down,
        grad_scale_two,
    ) = lax.psum(
        (
            grad_mask_token,
            grad_gain_one,
            grad_shift_one,
            grad_b_out,
            grad_scale_one,
            grad_gain_two,
            grad_shift_two,
            grad_b_down,
            grad_scale_two,
        ),
        ("dp", "tp"),
    )
    grad_b_query, grad_b_value, grad_b_up = lax.psum((grad_b_query, grad_b_value, grad_b_up), "dp")
    grad_w_joined, grad_w_out, grad_w_up, grad_w_down = (
        lax.psum_scatter(
            grad_w_joined.astype(jnp.bfloat16), "dp", scatter_dimension=0, tiled=True
        ).astype(jnp.float32),
        lax.psum_scatter(
            grad_w_out.astype(jnp.bfloat16), "dp", scatter_dimension=1, tiled=True
        ).astype(jnp.float32),
        lax.psum_scatter(
            grad_w_up.astype(jnp.bfloat16), "dp", scatter_dimension=0, tiled=True
        ).astype(jnp.float32),
        lax.psum_scatter(
            grad_w_down.astype(jnp.bfloat16), "dp", scatter_dimension=1, tiled=True
        ).astype(jnp.float32),
    )
    grad_w_query = grad_w_joined[:, :local_cols]
    grad_w_key = grad_w_joined[:, local_cols : 2 * local_cols]
    grad_w_value = grad_w_joined[:, 2 * local_cols :]
    return (
        block_out,
        grad_tokens,
        grad_mask_token,
        grad_gain_one,
        grad_shift_one,
        grad_w_query,
        grad_w_key,
        grad_w_value,
        grad_b_query,
        grad_b_value,
        grad_w_out,
        grad_b_out,
        grad_scale_one,
        grad_gain_two,
        grad_shift_two,
        grad_w_up,
        grad_b_up,
        grad_w_down,
        grad_b_down,
        grad_scale_two,
    )


def nn(left, right):
    return lax.dot_general(left, right, (((1,), (0,)), ((), ())), preferred_element_type=F32)


def nt(left, right):
    return lax.dot_general(left, right, (((1,), (1,)), ((), ())), preferred_element_type=F32)


def tn(left, right):
    return lax.dot_general(left, right, (((0,), (0,)), ((), ())), preferred_element_type=F32)


def padded(rows):
    return -(-rows // 32) * 32


def windows(rows):
    found = []
    for image in range(rows // SEQ):
        first = image * SEQ
        start = first // 16 * 16
        found.append((start, -(-(first - start + SEQ) // 16) * 16, first - start))
    return found


def row_blocks(total, size=160):
    return [slice(s, min(s + size, total)) for s in range(0, total, size)]


def inside(shape, axis, offset):
    at = lax.broadcasted_iota(jnp.int32, shape, axis)
    return (at >= offset) & (at < offset + SEQ)


def col_sum(values):
    return jnp.sum(values, axis=0, keepdims=True)


def row_mean(values):
    return jnp.mean(values, axis=-1, keepdims=True)


def moments(rows_in):
    center = rows_in - row_mean(rows_in)
    return center, lax.rsqrt(row_mean(center * center) + EPSILON)


def norm_pull(rows_in, gain, grad):
    center, inv = moments(rows_in)
    hat = center * inv
    scaled = grad * gain
    back = (scaled - row_mean(scaled) - hat * row_mean(scaled * hat)) * inv
    return back, col_sum(grad * hat), col_sum(grad)


def gelu_parts(v):
    cdf = 0.5 + 0.5 * lax.erf(v * math.sqrt(0.5))
    return cdf, v * (jnp.exp(-0.5 * (v * v)) * (1.0 / math.sqrt(2.0 * math.pi)))


def rows_outside(values, offset, fill):
    size = values.shape[0]

    def edge(part, base):
        at = lax.broadcasted_iota(jnp.int32, part.shape, 0) + base
        return jnp.where((at >= offset) & (at < offset + SEQ), part, fill)

    head = edge(values[:16], 0) if offset else values[:16]
    return jnp.concatenate([head, values[16:-32], edge(values[-32:], size - 32)], axis=0)


def one_head(shape, head):
    return (lax.broadcasted_iota(jnp.int32, shape, 1) < HD) == (head == 0)


def in_turn(rows, lead, begin, finish):
    units = [(window, head) for window in windows(rows) for head in (0, 1)]
    begun = [begin(*unit) for unit in units[:lead]]
    for i, unit in enumerate(units):
        if i + lead < len(units):
            begun.append(begin(*units[i + lead]))
        finish(i, *unit, begun[i])
        begun[i] = None


def norm_rows(rows, cols):
    return (cols // HD * (rows // SEQ), 256)


def attend(rows, q_ref, k_ref, v_ref, ctx_ref, log_ref):
    ctx_ref[padded(rows) - 32 :, :] = jnp.zeros((32, ctx_ref.shape[1]), BF16)
    count = 2 * (rows // SEQ)

    def one_pair(pair, carry):
        lanes = pl.ds(pl.multiple_of(pair * PAIR, PAIR), PAIR)
        halves = {}

        def begin(window, head):
            start, size, _ = window
            win = slice(start, start + size)
            k = k_ref[win, lanes]
            return nt(jnp.where(one_head(k.shape, head), k, jnp.zeros_like(k)), q_ref[win, lanes])

        def finish(i, window, head, scores):
            start, size, offset = window
            win = slice(start, start + size)
            scores = rows_outside(scores, offset, LOWEST)
            top = jnp.max(scores, axis=0, keepdims=True)
            raised = jnp.exp(scores - top)
            total = jnp.sum(raised, axis=0, keepdims=True)
            out = tn(v_ref[win, lanes], raised.astype(BF16))
            halves[head] = out[head * HD : (head + 1) * HD] * (1.0 / total)
            log_ref[pl.ds(pair * count + i, 1), :size] = top + jnp.log(total)
            if head == 1:
                both = jnp.concatenate([halves[0], halves[1]], axis=0).T.astype(BF16)
                keep = inside((size, PAIR), 0, offset)
                ctx_ref[win, lanes] = jnp.where(keep, both, ctx_ref[win, lanes])

        in_turn(rows, 4, begin, finish)
        return carry

    lax.fori_loop(0, q_ref.shape[1] // PAIR, one_pair, 0, unroll=2)


def attend_back(rows, q_ref, k_ref, v_ref, gc_ref, log_ref, dq_ref, dk_ref, dv_ref):
    for ref in (dq_ref, dk_ref, dv_ref):
        ref[padded(rows) - 32 :, :] = jnp.zeros((32, ref.shape[1]), BF16)
    factor = 1.0 / math.sqrt(HD)
    count = 2 * (rows // SEQ)

    def one_pair(pair, carry):
        lanes = pl.ds(pl.multiple_of(pair * PAIR, PAIR), PAIR)
        halves = {}

        def begin(window, head):
            start, size, offset = window
            win = slice(start, start + size)
            zero = jnp.zeros((size, PAIR), BF16)
            mine = one_head(zero.shape, head)
            k = jnp.where(mine, k_ref[win, lanes], zero)
            v = jnp.where(mine, v_ref[win, lanes], zero)
            gc = jnp.where(inside(zero.shape, 0, offset), gc_ref[win, lanes], zero)
            q = q_ref[win, lanes]
            return nt(k, q), nt(v, gc), k, q, gc

        def finish(i, window, head, begun):
            start, size, offset = window
            win = slice(start, start + size)
            scores, grad_probs, k, q, gc = begun
            scores = rows_outside(scores, offset, LOWEST)
            probs = jnp.exp(scores - log_ref[pl.ds(pair * count + i, 1), :size])
            inner = jnp.sum(grad_probs * probs, axis=0, keepdims=True)
            grad_scores = (probs * (grad_probs - inner)).astype(BF16)
            halves[head] = tn(grad_scores, k), nn(grad_scores, q), nn(probs.astype(BF16), gc)
            if head == 1:
                keep = inside((size, PAIR), 0, offset)
                first = one_head((size, PAIR), 0)
                low, high = halves[0], halves[1]
                for ref, new in (
                    (dq_ref, (low[0] + high[0]) * factor),
                    (dk_ref, jnp.where(first, low[1], high[1])),
                    (dv_ref, jnp.where(first, low[2], high[2])),
                ):
                    ref[win, lanes] = jnp.where(keep, new.astype(BF16), ref[win, lanes])

        in_turn(rows, 2, begin, finish)
        return carry

    lax.fori_loop(0, q_ref.shape[1] // PAIR, one_pair, 0, unroll=2)


class Moved:
    def __init__(self, far, near, line, pieces=(None,)):
        self.far, self.near, self.line, self.pieces = far, near, line, pieces
        self.copies = [line.add(*self.views(p)) for p in pieces]

    def views(self, p):
        return (self.far, self.near) if p is None else (self.far.at[p], self.near.at[p])

    def part(self, i):
        self.line.wait(self.copies[i])
        return self.views(self.pieces[i])[1]

    @property
    def ref(self):
        for copy in self.copies:
            self.line.wait(copy)
        return self.near

    def send(self, p=None):
        far, near = self.views(p)
        self.line.send(near, far)


class Line:
    def __init__(self, sems, count):
        self.sems, self.free = sems, iter(range(count))
        self.queue, self.waves, self.started, self.waited, self.sent = [], [], 0, set(), []

    def copy(self, source, target):
        return pltpu.make_async_copy(source, target, self.sems.at[next(self.free)])

    def add(self, source, target):
        self.queue.append(self.copy(source, target))
        return len(self.queue) - 1

    def begin(self, waves=()):
        first = [i for wave in waves for i in wave]
        rest = [i for i in range(len(self.queue)) if i not in first]
        self.waves = [list(wave) for wave in waves] + [rest]
        self.start_to(1)

    def start_to(self, stop):
        while self.started < min(stop, len(self.waves)):
            for i in self.waves[self.started]:
                self.queue[i].start()
            self.started += 1

    def wait(self, i):
        if i in self.waited:
            return
        wave = next(k for k, some in enumerate(self.waves) if i in some)
        self.start_to(wave + 1)
        self.queue[i].wait()
        self.waited.add(i)
        self.start_to(wave + 2)

    def send(self, source, target):
        copy = self.copy(source, target)
        copy.start()
        self.sent.append(copy)

    def finish(self):
        for i in range(len(self.queue)):
            self.wait(i)
        for copy in self.sent:
            copy.wait()


class View:
    def __init__(self, array, axis=0, start=0, size=None):
        self.array, self.shape, self.index = array, array.shape, None
        if size is not None:
            p = slice(start, start + size)
            self.index = (slice(None),) * axis + (p,)
            self.shape = tuple(size if i == axis else n for i, n in enumerate(array.shape))


def cut_in(size, axis, count):
    step = size // count
    spans = [slice(i * step, (i + 1) * step) for i in range(count)]
    return [(slice(None),) * axis + (p,) for p in spans]


def moved_call(kernel, outs, args, flops, sends, scratch=(), name=None, after=(), cuts=None, waves=()):
    hbm = pl.BlockSpec(memory_space=pl.ANY)
    cuts = cuts or {}
    views = [a if isinstance(a, View) else View(a) for a in args]
    args = [view.array for view in views]
    n_in, n_out = len(args), len(outs)
    pieces = [
        cut_in(v.shape[cuts[i][0]], *cuts[i]) if i in cuts else [None] for i, v in enumerate(views)
    ]
    n_sems = sum(len(p) for p in pieces) + sends
    buffers = [pltpu.VMEM(v.shape, v.array.dtype) for v in views]
    buffers += [pltpu.VMEM(o.shape, o.dtype) for o in outs]

    def inner(*refs):
        refs = refs[len(after) :]
        far_in, far_out, rest = refs[:n_in], refs[n_in : n_in + n_out], list(refs[n_in + n_out :])
        line = Line(rest.pop(), n_sems)
        ins = []
        for far, view, p in zip(far_in, views, pieces):
            far = far if view.index is None else far.at[view.index]
            ins.append(Moved(far, rest.pop(0), line, p))
        line.begin([[ins[i].copies[j] for i, j in wave] for wave in waves])
        results = [Moved(far, rest.pop(0), line, ()) for far in far_out]
        kernel(*ins, *results, *rest)
        line.finish()

    return pl.pallas_call(
        inner,
        in_specs=[hbm] * (len(after) + n_in),
        out_specs=[hbm] * n_out,
        out_shape=outs,
        scratch_shapes=buffers + list(scratch) + [pltpu.SemaphoreType.DMA((n_sems,))],
        compiler_params=pltpu.CompilerParams(vmem_limit_bytes=KERNEL_VMEM),
        cost_estimate=cost(flops, *args, *outs),
        name=name,
    )(*after, *args)


def halves_of(tall):
    middle = tall // 2 // 16 * 16
    return [slice(0, middle), slice(middle, tall)]


def blocks_within(part, rows, size=400):
    stop = min(part.stop, rows)
    return [slice(s, min(s + size, stop)) for s in range(part.start, stop, size)]


def first_kernel(
    rows, tok, mask, mt, gain, shift, wq, wk, wv, bq, bv,
    normed, q, k, v, ctx, log,
):
    normed_ref = normed.near
    tok_ref, mask_ref = tok.ref, mask.ref
    mt_ref, gain_ref, shift_ref = mt.ref, gain.ref, shift.ref
    for block in blocks_within(slice(0, rows), rows):
        initial = jnp.where(mask_ref[block] > 0, mt_ref[...], tok_ref[block].astype(F32))
        center, inv = moments(initial)
        normed_ref[block] = (center * inv * gain_ref[...] + shift_ref[...]).astype(BF16)
    over = padded(rows) - rows
    normed_ref[rows:] = jnp.zeros((over, normed_ref.shape[1]), BF16)
    normed.send()
    project(normed_ref, [wq, wk, wv], bq, bv, q, k, v)
    attend(rows, q.near, k.near, v.near, ctx.near, log.near)
    ctx.send()
    log.send()


def project(normed_ref, weights, bq, bv, q, k, v):
    scale = BF16(1.0 / math.sqrt(HD))
    wq, wk, wv = weights
    q.near[...] = (nn(normed_ref[...], wq.ref[...]) + bq.ref[...]).astype(BF16) * scale
    q.send()
    k.near[...] = nn(normed_ref[...], wk.ref[...]).astype(BF16)
    k.send()
    v.near[...] = (nn(normed_ref[...], wv.ref[...]) + bv.ref[...]).astype(BF16)
    v.send()


class Third:
    def __init__(self, moved, i):
        self.moved, self.i = moved, i

    @property
    def ref(self):
        return self.moved.part(self.i)


def second_kernel(
    rows, normed, joined, bq, bv, ctx, wo, wo2, bo,
    s1, gain, shift, tok, mask, mt, cot, s2,
    q, k, v, ctx2, log, middle, normed2, go, sums, acc_ref,
):
    project(normed.ref, [Third(joined, i) for i in range(3)], bq, bv, q, k, v)
    attend(rows, q.near, k.near, v.near, ctx2.near, log.near)
    ctx2.send()
    log.send()
    over = padded(rows) - rows
    width = acc_ref.shape[1]
    total = jnp.zeros((1, width), F32)
    ctx_ref, wo_ref, wo2_ref = ctx.ref, wo.ref, wo2.ref
    tok_ref, mask_ref, cot_ref = tok.ref, mask.ref, cot.ref
    bo_ref, s1_ref, gain_ref, shift_ref, mt_ref, s2_ref = (v.ref for v in (bo, s1, gain, shift, mt, s2))
    for half in halves_of(padded(rows)):
        acc_ref[half] = nn(ctx_ref[half], wo_ref[...]) + nn(ctx2.near[half], wo2_ref[...])
    for half in halves_of(padded(rows)):
        for block in blocks_within(half, rows):
            masked = mask_ref[block] > 0
            initial = jnp.where(masked, mt_ref[...], tok_ref[block].astype(F32))
            one = initial + s1_ref[...] * (acc_ref[block] + bo_ref[...])
            middle.near[block] = one
            center, inv = moments(one)
            normed2.near[block] = (center * inv * gain_ref[...] + shift_ref[...]).astype(BF16)
            grad_out = jnp.where(masked, cot_ref[block].astype(F32), 0.0) * s2_ref[...]
            grad_out = grad_out.astype(BF16)
            go.near[block] = grad_out
            total += col_sum(grad_out.astype(F32))
        if half.stop == padded(rows):
            middle.near[rows:] = jnp.zeros((over, width), F32)
            normed2.near[rows:] = jnp.zeros((over, width), BF16)
            go.near[rows:] = jnp.zeros((over, width), BF16)
        for one in (normed2, go, middle):
            one.send(half)
    sums.near[...] = total
    sums.send()


def feed_kernel(chunk, n2, wu, go, wd, bu, hidden, gp, grads, sums, scale_sum):
    me = lax.axis_index("dp")
    cols = hidden.near.shape[1]
    width = n2.near.shape[1]
    lanes = None
    for i in range(cols // chunk):
        at = slice(i * chunk, (i + 1) * chunk)
        pre = nn(n2.ref[...], wu.part(i)[...]) + bu.ref[:, at]
        grad_hidden = nt(go.ref[...], wd.part(i)[...])
        cdf, slope = gelu_parts(pre)
        new_hidden = (pre * cdf).astype(BF16)
        grad_pre = (grad_hidden * (cdf + slope)).astype(BF16)
        hidden.near[:, at] = new_hidden
        gp.near[:, at] = grad_pre
        hidden.send((slice(None), at))
        gp.send((slice(None), at))
        sums.near[:, at] = col_sum(grad_pre.astype(F32))
        down = tn(go.ref[...], new_hidden)
        weighed = down * wd.part(i)[...].T.astype(F32)
        for k in range(0, chunk, 128):
            part = weighed[:, k : k + 128]
            lanes = part if lanes is None else lanes + part
        for j, grad in enumerate((down, tn(n2.ref[...], grad_pre))):
            base = (2 * i + j) * chunk
            store_blocks(me, grad, grads.near, base)
            grads.send((slice(None), slice(None), slice(base, base + chunk)))
    sums.send()
    scale_sum.near[...] = col_sum(lanes.T)
    scale_sum.send()


def store_blocks(me, product_rows, out_ref, at):
    parts, size, _ = out_ref.shape
    cols = product_rows.shape[1]
    for b in range(parts):
        out_ref[b ^ me, :, at : at + cols] = product_rows[b * size : (b + 1) * size].astype(BF16)


def in_pieces(*groups):
    for some in zip(*groups):
        for j in range(len(some[0].pieces)):
            yield [functools.partial(one.part, j) for one in some]


def middle_kernel(rows, count, *refs):
    gps, wus = refs[:count], refs[count : 2 * count]
    middle, tok, mask, mt, cot, gain, s1 = refs[2 * count : 2 * count + 7]
    gm, gbr, sums, acc_ref = refs[2 * count + 7 :]
    width = acc_ref.shape[1]
    total = [jnp.zeros((1, width), F32)] * 4
    halves = halves_of(padded(rows))
    for i, (one, w) in enumerate(in_pieces(gps, wus)):
        for half in halves:
            part = nt(one()[half], w()[...])
            acc_ref[half] = part if i == 0 else acc_ref[half] + part
    middle_ref, tok_ref, mask_ref, cot_ref = middle.ref, tok.ref, mask.ref, cot.ref
    mt_ref, gain_ref, s1_ref = mt.ref, gain.ref, s1.ref
    over = padded(rows) - rows
    for half in halves:
        for block in blocks_within(half, rows):
            masked = mask_ref[block] > 0
            one = middle_ref[block]
            back, grad_gain, grad_shift = norm_pull(one, gain_ref[...], acc_ref[block])
            grad_middle = jnp.where(masked, cot_ref[block].astype(F32), 0.0) + back
            gm.near[block] = grad_middle
            grad_branch = (s1_ref[...] * grad_middle).astype(BF16)
            gbr.near[block] = grad_branch
            initial = jnp.where(masked, mt_ref[...], tok_ref[block].astype(F32))
            new = (
                grad_gain,
                grad_shift,
                col_sum(grad_middle * (one - initial)) / s1_ref[...],
                col_sum(grad_branch.astype(F32)),
            )
            total = [a + b for a, b in zip(total, new)]
        if half.stop == padded(rows):
            gm.near[rows:] = jnp.zeros((over, width), F32)
            gbr.near[rows:] = jnp.zeros((over, width), BF16)
        gbr.send(half)
        gm.send(half)
    for i, one in enumerate(total):
        sums.near[i : i + 1] = one
    sums.send()


def back_kernel(
    rows, gbr, wo, ctx, q, k, v, log, n1,
    dq, dk, dv, grads, sums, gc_ref,
):
    me = lax.axis_index("dp")
    cols = dq.near.shape[1]
    gc_ref[...] = nt(gbr.ref[...], wo.ref[...]).astype(BF16)
    store_blocks(me, tn(gbr.ref[...], ctx.ref[...]), grads.near, 3 * cols)
    grads.send((slice(None), slice(None), slice(3 * cols, 4 * cols)))
    attend_back(rows, q.ref, k.ref, v.ref, gc_ref, log.ref, dq.near, dk.near, dv.near)
    for i, one in enumerate((dq, dk, dv)):
        one.send()
        store_blocks(me, tn(n1.ref[...], one.near[...]), grads.near, i * cols)
        grads.send((slice(None), slice(None), slice(i * cols, (i + 1) * cols)))
        if i != 1:
            at = i // 2 * cols
            sums.near[:, at : at + cols] = col_sum(one.near[...].astype(F32))
    sums.send()


def middle_back_kernel(rows, count, *refs):
    first, others = refs[: 2 * count + 7], refs[2 * count + 7 : 2 * count + 14]
    (gm, gbr, sums), outs = refs[2 * count + 14 : 2 * count + 17], refs[2 * count + 17 : 2 * count + 22]
    acc_ref, gc_ref = refs[2 * count + 22 :]
    middle_kernel(rows, count, *first, gm, gbr, sums, acc_ref)
    back_kernel(rows, gbr, *others, *outs, gc_ref)


def input_kernel(rows, *refs):
    grads, weights = refs[:6], list(refs[6:9]) + [Third(refs[9], i) for i in range(3)]
    tok, mask, mt, gain, gm, out, sums, acc_ref = refs[10:]
    width = acc_ref.shape[1]
    halves = halves_of(padded(rows))
    for i, (one, w) in enumerate(zip(grads, weights)):
        for half in halves:
            part = nt(one.ref[half], w.ref[...])
            acc_ref[half] = part if i == 0 else acc_ref[half] + part
    total = [jnp.zeros((1, width), F32)] * 3
    tok_ref, mask_ref, gm_ref, mt_ref, gain_ref = tok.ref, mask.ref, gm.ref, mt.ref, gain.ref
    for half in halves:
        for block in blocks_within(half, rows):
            masked = mask_ref[block] > 0
            initial = jnp.where(masked, mt_ref[...], tok_ref[block].astype(F32))
            back, grad_gain, grad_shift = norm_pull(initial, gain_ref[...], acc_ref[block])
            grad_initial = gm_ref[block] + back
            out.near[block] = jnp.where(masked, 0.0, grad_initial)
            new = (col_sum(jnp.where(masked, grad_initial, 0.0)), grad_gain, grad_shift)
            total = [a + b for a, b in zip(total, new)]
    out.send()
    for i, one in enumerate(total):
        sums.near[i : i + 1] = one
    sums.send()


def output_kernel(rows, count, *refs):
    hiddens, wds = refs[:count], refs[count : 2 * count]
    middle, bd, s2, out, acc_ref = refs[2 * count :]
    halves = halves_of(padded(rows))
    for i, (one, w) in enumerate(in_pieces(hiddens, wds)):
        for half in halves:
            part = nn(one()[half], w()[...])
            acc_ref[half] = part if i == 0 else acc_ref[half] + part
    middle_ref, bd_ref, s2_ref = middle.ref, bd.ref, s2.ref
    for block in blocks_within(slice(0, rows), rows):
        output = acc_ref[block] + bd_ref[...]
        out.near[block] = (middle_ref[block] + s2_ref[...] * output).astype(BF16)
    out.send()


def shape_of(shape, dtype=BF16):
    return jax.ShapeDtypeStruct(shape, dtype)


def cost(flops, *arrays):
    moved = sum(a.size * a.dtype.itemsize for a in arrays)
    return pl.CostEstimate(flops=flops, bytes_accessed=moved, transcendentals=0)


def without(kernel, at, count):
    def inner(*refs):
        kernel(*refs[:at], *refs[at + count :])

    return inner


def pairs(n, bit):
    return [(i, i ^ (1 << bit)) for i in range(n)]


TILE = 256


class Segment:
    def __init__(self, terms, start, width, order):
        self.start, self.width, self.order, self.used, self.got = start, width, list(order), [], []
        self.bits = sorted(order, reverse=True)
        dims = (2,) * len(self.bits)
        self.terms = [(a.reshape(dims + a.shape[1:]), base + start) for a, base in terms]
        self.rows = terms[0][0].shape[1]
        self.across = width // TILE

    @property
    def rest(self):
        return self.order[1:]

    @property
    def tiles(self):
        return self.across << len(self.rest)

    def views(self):
        bit, found = self.order[0] if self.order else None, []
        for array, start in self.terms:
            one = View(array)
            one.index = tuple(0 if b in self.used else 1 if b == bit else slice(None) for b in self.bits)
            one.index += (slice(None), slice(start, start + self.width))
            one.shape = (2,) * len(self.rest) + (self.rows, self.width)
            found.append(one)
        for array, start in self.got:
            found.append(View(array, 0, start + (self.tiles if self.order else 0), self.tiles))
        return found

    def add(self, refs):
        originals, got = refs[: len(self.terms)], refs[len(self.terms) :]
        for at in range(1 << len(self.rest)):
            side = {b: at >> (len(self.rest) - 1 - i) & 1 for i, b in enumerate(self.rest)}
            index = tuple(side[b] for b in self.bits if b in side)
            for c in range(self.across):
                cols, tile = slice(c * TILE, (c + 1) * TILE), at * self.across + c
                parts = [ref[(*index, slice(None), cols)] for ref in originals] + [ref[tile] for ref in got]
                yield tile, self.start + c * TILE, functools.reduce(jnp.add, [p.astype(F32) for p in parts])

    def received(self, array, start):
        self.used.append(self.order.pop(0))
        self.got.append((array, start))


class Group:
    def __init__(self, segments, block):
        self.segments, self.block, self.result = segments, block, None
        self.width = sum(s.width for s in segments)

    @property
    def last(self):
        return not self.segments[0].order


class Sums:
    def __init__(self, same, own, other, bits, last):
        self.parts, self.own, self.n_own, self.last_terms = same + other, same + own, len(own), last
        self.rounds = [bits[i : i + 2] for i in range(0, len(bits), 2)]
        self.stage, self.terms, self.result = 0, [], None

    def job(self):
        width = self.parts[0].shape[1]
        height = -(-sum(p.size for p in self.parts) // (8 * width)) * 8
        packed = {0: self.parts, 1: self.own}.get(self.stage, [])
        places, row, col = [], 0, 0
        for p in packed:
            steps = []
            for at in range(0, p.shape[1], width):
                size = min(width, p.shape[1] - at)
                steps.append(((slice(row, row + p.shape[0]), slice(col, col + size)), slice(at, at + size)))
                col += size
                if col == width:
                    row, col = row + p.shape[0], 0
            places.append(steps)
        return packed, places, self.terms, shape_of((height, width), F32)

    def final_shapes(self):
        own = self.own[len(self.own) - self.n_own :]
        width = own[0].shape[1]
        return [shape_of((1, width), F32)] * 9 + [shape_of((1, width // 2), F32)] * 2 + [
            shape_of((1, sum(p.size for p in own[1:])), F32)
        ]

    def final(self, total, ins, outs):
        bias, scale = (one.ref[...] for one in ins)
        start = sum(p.shape[0] for p in self.own[: len(self.own) - self.n_own])
        rows = [total[i : i + 1] for i in range(total.shape[0])]
        for out, value in zip(outs, rows[:8]):
            out.near[...] = value
        outs[8].near[...] = (functools.reduce(jnp.add, rows[8:start]) + bias * rows[7]) / scale
        half = outs[9].near.shape[1]
        outs[9].near[...] = rows[start][:, :half]
        outs[10].near[...] = rows[start][:, half:]
        count = outs[11].near.shape[1] // (2 * half)
        for i, value in enumerate(rows[start + 1 : start + 1 + count]):
            outs[11].near[:, i * 2 * half : (i + 1) * 2 * half] = value

    @property
    def last(self):
        return self.stage == len(self.rounds) + 1

    def take(self, sent):
        n = lax.axis_size("dp")
        if self.last:
            self.result = sent
        elif self.stage == 0:
            self.terms = [swap(sent[0])]
        else:
            bits = self.rounds[self.stage - 1]
            self.terms = list(sent)
            for some in range(1, 1 << len(bits)):
                flip = sum(1 << b for i, b in enumerate(bits) if some >> i & 1)
                self.terms.append(lax.ppermute(sent[0], "dp", [(d, d ^ flip) for d in range(n)]))
        self.stage += 1


def exchange(groups, after, sums=None, carry=None):
    buffers, shapes, plan = {}, [], []
    for segment in [s for g in groups if not g.last for s in g.segments]:
        buffers.setdefault(segment.order[0], []).append(segment)
    for some in buffers.values():
        starts = [sum(s.tiles for s in some[:i]) for i in range(len(some))]
        plan.append(list(zip(some, starts)))
        shapes.append(shape_of((sum(s.tiles for s in some), some[0].rows, TILE)))
    ending = [g for g in groups if g.last]
    for g in ending:
        shapes += [shape_of((g.segments[0].rows, g.block), F32)] * (g.width // g.block)
    views = [s.views() for one in plan for s, _ in one] + [s.views() for g in ending for s in g.segments]
    counts = [len(v) for v in views]
    views = [v for some in views for v in some]
    n_summed = len(shapes)
    packed, places, terms = [], [], []
    sums_last = sums is not None and sums.last
    if sums is not None:
        packed, places, terms, shape = sums.job()
        views += [View(a) for a in packed + terms + (sums.last_terms if sums_last else [])]
        shapes += sums.final_shapes() if sums_last else [shape]
    passed = [] if carry is None else [carry]
    hbm = pl.BlockSpec(memory_space=pl.ANY)
    skipped, n_in, n_out = len(after) + len(passed), len(views), len(shapes)

    def kernel(*refs):
        far_in, far_out = refs[skipped : skipped + n_in], refs[skipped + n_in :][:n_out]
        nears = list(refs[skipped + n_in + n_out + len(passed) :])
        line = Line(nears.pop(), n_in + n_out)
        ins = []
        for far, view in zip(far_in, views):
            far = far if view.index is None else far.at[view.index]
            ins.append(Moved(far, nears.pop(0), line))
        line.begin()
        outs = [Moved(far, nears.pop(0), line, ()) for far in far_out]
        sizes = list(counts)

        def taken():
            return [ins.pop(0).ref for _ in range(sizes.pop(0))]

        for one in plan:
            out = outs.pop(0)
            for segment, start in one:
                for tile, _, total in segment.add(taken()):
                    out.near[start + tile] = total.astype(BF16)
            out.send()
        for g in ending:
            mine = [outs.pop(0) for _ in range(g.width // g.block)]
            for segment in g.segments:
                for _, col, total in segment.add(taken()):
                    mine[col // g.block].near[:, col % g.block : col % g.block + TILE] = total
            for out in mine:
                out.send()
        if sums is not None:
            if packed:
                new = outs[0]
                new.near[...] = ins[-1].ref[...] if terms else jnp.zeros(shape.shape, F32)
                for one, steps in zip(ins, places):
                    for place, cols in steps:
                        new.near[place] += one.ref[:, cols]
            else:
                total = functools.reduce(jnp.add, [one.ref[...] for one in ins[: len(terms)]])
                if sums_last:
                    sums.final(total, ins[len(terms) :], outs)
                else:
                    outs[0].near[...] = total
            for out in outs:
                out.send()
        line.finish()

    outs = pl.pallas_call(
        kernel,
        in_specs=[hbm] * (skipped + n_in),
        out_specs=[hbm] * (n_out + len(passed)),
        out_shape=shapes + [shape_of(p.shape, p.dtype) for p in passed],
        input_output_aliases={len(after): n_out} if passed else {},
        scratch_shapes=[pltpu.VMEM(v.shape, v.array.dtype) for v in views]
        + [pltpu.VMEM(o.shape, o.dtype) for o in shapes]
        + [pltpu.SemaphoreType.DMA((n_in + n_out,))],
        compiler_params=pltpu.CompilerParams(vmem_limit_bytes=EXCHANGE_VMEM),
        cost_estimate=cost(0, *shapes),
        name="exchange",
    )(*after, *passed, *[v.array for v in views])
    n, left = lax.axis_size("dp"), list(outs[:n_summed])
    for bit, one in zip(buffers, plan):
        got = lax.ppermute(left.pop(0), "dp", pairs(n, bit))
        for segment, start in one:
            segment.received(got, start)
    for g in ending:
        g.result = [left.pop(0) for _ in range(g.width // g.block)]
    if sums is not None:
        sums.take(list(outs[n_summed:n_out]))
    sent = list(outs[:n_out])
    return sent if carry is None else (sent, outs[-1])


def swap(array):
    return lax.ppermute(array, "tp", [(0, 1), (1, 0)])


def local_body(
    tokens, masked, cotangent, mask_token, gain_one, shift_one, w_query, w_key, w_value, b_query,
    b_value, w_out, b_out, scale_one, gain_two, shift_two, w_up, b_up, w_down, b_down, scale_two,
):
    rows, width = tokens.shape
    tall = padded(rows)
    half = w_query.shape[1]
    units = w_up.shape[1]
    n = lax.axis_size("dp")
    bits = n.bit_length() - 1
    me = lax.axis_index("dp").astype(jnp.int32).reshape(1)
    biases = jnp.concatenate([b_query, b_value, b_up]).reshape(1, -1)

    joined2 = swap(jnp.concatenate([w_query, w_key, w_value], axis=1))
    biases2 = swap(biases)
    wo2 = swap(w_out)
    wu2, wd2 = swap(w_up), swap(w_down)
    row = lambda v: v.reshape(1, -1)
    bq2, bv2 = View(biases2, 1, 0, half), View(biases2, 1, half, half)
    bq, bv, bu = row(b_query), row(b_value), row(b_up)
    mt, g1, s1, bo, sc1 = row(mask_token), row(gain_one), row(shift_one), row(b_out), row(scale_one)
    g2, s2, bd, sc2 = row(gain_two), row(shift_two), row(b_down), row(scale_two)
    mask = masked.reshape(rows, 1)

    narrow = shape_of((tall, half))
    wide = shape_of((tall, width))
    attend_flops = 2 * 2 * 256 * SEQ * rows * half // HD
    logs = shape_of(norm_rows(rows, half), F32)
    normed, q, k, v, ctx, log = moved_call(
        functools.partial(first_kernel, rows),
        [wide, narrow, narrow, narrow, narrow, logs],
        (tokens, mask, mt, g1, s1, w_query, w_key, w_value, bq, bv),
        6 * rows * width * half + attend_flops,
        6,
        name="first",
        waves=[[(i, 0) for i in range(5)]],
    )
    tall_f32 = shape_of((tall, width), F32)
    scratch = [pltpu.VMEM((tall, width), F32)]
    one_row = shape_of((1, width), F32)
    q2, k2, v2, ctx2, log2, middle, normed2, go, sum_go = moved_call(
        functools.partial(second_kernel, rows),
        [narrow, narrow, narrow, narrow, logs, tall_f32, wide, wide, one_row],
        (normed, joined2, bq2, bv2, ctx, w_out, wo2, bo, sc1, g2, s2, tokens, mask, mt, cotangent, sc2),
        10 * rows * width * half + attend_flops,
        12,
        scratch=scratch,
        name="second",
        cuts={1: (1, 3)},
        waves=[[(0, 0), (1, 0), (2, 0)], [(1, 1), (1, 2), (3, 0)]],
    )

    natural = tuple(range(bits))
    by_x, by_y = natural, natural[1:2] + natural[0:1] + natural[2:]
    by_yzzx, by_zxyz = natural[1:] + natural[:1], natural[2:3] + natural[:2] + natural[3:]

    part = units // 2
    chunk = min(1024, part)
    hiddens, gps, ups, downs = [], [], [], []

    def feed(weights, first, size, after=()):
        w_up, w_down, b_up, b_start = weights
        count = size // chunk
        hidden, gp, grads, sums, scale_sum = moved_call(
            functools.partial(feed_kernel, chunk),
            [
                shape_of((tall, size)),
                shape_of((tall, size)),
                shape_of((n, width // n, 2 * size)),
                shape_of((1, size), F32),
                one_row,
            ],
            (normed2, View(w_up, 1, first, size), go, View(w_down, 0, first, size),
             View(b_up, 1, b_start + first, size)),
            8 * tall * width * size,
            4 * count + 2,
            name="feed",
            after=after,
            cuts={1: (1, count), 3: (0, count)},
            waves=[[(i, 0) for i in range(5)]],
        )
        hiddens.append(hidden)
        gps.append(gp)
        ups.append(View(w_up, 1, first, size))
        downs.append(View(w_down, 0, first, size))
        scale_sums.append(scale_sum)
        return grads, sums

    def grouped(size, block, parts, *terms):
        whole, at, segments = sum(w for w, _ in parts), 0, []
        for w, order in parts:
            segments.append(Segment(terms, at, w * size // whole, order))
            at += w * size // whole
        return Group(segments, block)

    mine, other = (w_up, w_down, bu, 0), (wu2, wd2, biases2, 2 * half)
    scale_sums = []
    theirs, sums_up2 = feed(other, 0, units)
    theirs = swap(theirs)
    own, sums_up = feed(mine, 0, units, [sums_up2])
    parts = ((6, by_x), (5, by_yzzx), (5, by_zxyz))
    b = grouped(2 * units, chunk, parts, (own, 0), (theirs, 0))
    sent = exchange([b], [sums_up])

    back_outs = [narrow, narrow, narrow, shape_of((n, width // n, 4 * half)), shape_of((1, 2 * half), F32)]
    back_flops = 10 * rows * width * half + 3 * attend_flops
    back_scratch = [pltpu.VMEM((tall, half), BF16)]
    gm, gbr, sums_two, dq2, dk2, dv2, gw2, sums_b2 = moved_call(
        functools.partial(middle_back_kernel, rows, len(gps)),
        [tall_f32, wide, shape_of((4, width), F32)] + back_outs,
        (*gps, *ups, middle, tokens, mask, mt, cotangent, g2, sc1, wo2, ctx2, q2, k2, v2, log2, normed),
        8 * tall * width * part + back_flops,
        13,
        scratch=scratch + back_scratch,
        name="middle",
        after=sent,
        cuts={i: (1, 2) for i in range(4)},
        waves=[[(i, j), (2 + i, j)] for i in range(2) for j in range(2)],
    )
    sent, gw2 = exchange([b], [sums_b2], carry=gw2)
    gw2 = swap(gw2)

    def back(wo, ctx, q, k, v, log, after):
        return moved_call(
            functools.partial(back_kernel, rows),
            back_outs,
            (gbr, wo, ctx, q, k, v, log, normed),
            back_flops,
            8,
            scratch=back_scratch,
            name="back",
            after=after,
            waves=[[(0, 0), (1, 0)], [(2, 0)]],
        )

    dq, dk, dv, gw, sums_b = back(w_out, ctx, q, k, v, log, sent)
    c = grouped(4 * half, half, ((4, by_x), (3, by_y), (1, by_zxyz)), (gw, 0), (gw2, 0))
    sent = exchange([c, b], [sums_b])

    grad_tokens, sums_one = moved_call(
        functools.partial(input_kernel, rows),
        [shape_of((rows, width), F32), shape_of((3, width), F32)],
        (dq, dk, dv, dq2, dk2, dv2, w_query, w_key, w_value, joined2, tokens, mask, mt, g1, gm),
        12 * rows * width * half,
        2,
        scratch=scratch,
        cuts={9: (1, 3)},
        waves=[[(0, 0), (6, 0)], [(1, 0), (7, 0)], [(2, 0), (8, 0), (3, 0), (9, 0)]],
        name="input",
        after=sent,
    )
    same = [sums_one, sums_two, sum_go, *scale_sums]
    sums = Sums(same, [sums_b, sums_up], [sums_b2, sums_up2], list(natural), [bd, sc2])
    sent = exchange([c, b], [sums_one], sums=sums)
    block_out = moved_call(
        functools.partial(output_kernel, rows, len(hiddens)),
        [shape_of((rows, width))],
        (*hiddens, *downs, middle, bd, sc2),
        8 * tall * width * part,
        1,
        scratch=scratch,
        cuts={0: (1, 2), 1: (1, 2), 2: (0, 2), 3: (0, 2)},
        waves=[[(i, j), (2 + i, j)] for i in range(2) for j in range(2)],
        name="output",
        after=sent,
    )[0]
    last = block_out
    while sums.result is None:
        last = exchange([g for g in (c, b) if g.result is None], [last], sums=sums)[-1]

    done = b.result
    grad_w_down = jnp.concatenate(done[0::2], axis=1).T
    grad_w_up = jnp.concatenate(done[1::2], axis=1)
    grad_w_query, grad_w_key, grad_w_value, grad_w_out = c.result
    (grad_mask_token, grad_gain_one, grad_shift_one, grad_gain_two, grad_shift_two, grad_scale_one, grad_b_out,
     grad_b_down, grad_scale_two, grad_b_query, grad_b_value, grad_b_up) = (
        one.reshape(-1) for one in sums.result
    )
    return (
        block_out,
        grad_tokens,
        grad_mask_token,
        grad_gain_one,
        grad_shift_one,
        grad_w_query,
        grad_w_key,
        grad_w_value,
        grad_b_query,
        grad_b_value,
        grad_w_out.T,
        grad_b_out,
        grad_scale_one,
        grad_gain_two,
        grad_shift_two,
        grad_w_up,
        grad_b_up,
        grad_w_down,
        grad_b_down,
        grad_scale_two,
    )


def solution(mesh):
    placed = (
        P(("dp", "tp"), None),
        P(("dp", "tp")),
        P(("dp", "tp"), None),
        P(),
        P(),
        P(),
        P(None, "tp"),
        P(None, "tp"),
        P(None, "tp"),
        P("tp"),
        P("tp"),
        P("tp", None),
        P(),
        P(),
        P(),
        P(),
        P(None, "tp"),
        P("tp"),
        P("tp", None),
        P(),
        P(),
    )
    fits = mesh.shape["tp"] == 2 and mesh.shape["dp"].bit_count() == 1
    return jax.shard_map(
        local_body if fits else gathered_body,
        mesh=mesh,
        in_specs=placed,
        out_specs=(
            P(("dp", "tp"), None),
            P(("dp", "tp"), None),
            P(),
            P(),
            P(),
            P("dp", "tp"),
            P("dp", "tp"),
            P("dp", "tp"),
            P("tp"),
            P("tp"),
            P("tp", "dp"),
            P(),
            P(),
            P(),
            P(),
            P("dp", "tp"),
            P("tp"),
            P("tp", "dp"),
            P(),
            P(),
        ),
        check_vma=False,
    )
```

```python
import functools
import math

import jax
import jax.numpy as jnp
from jax import lax
from jax.experimental import pallas as pl
from jax.experimental.pallas import tpu as pltpu
from jax.sharding import PartitionSpec as P

SEQ = 197
HD = 64
PAIR = 2 * HD
EPSILON = 1e-06
BF16 = jnp.bfloat16
F32 = jnp.float32
MIB = 2**20
LOWEST = -1e30
KERNEL_VMEM = 64 * MIB
EXCHANGE_VMEM = 64 * MIB

def layer_norm(rows_in, gain_vec, shift_vec):
    center = rows_in - jnp.mean(rows_in, axis=-1, keepdims=True)
    spread = jnp.mean(center * center, axis=-1, keepdims=True)
    return center * lax.rsqrt(spread + EPSILON) * gain_vec + shift_vec


def norm_backward(rows_in, gain_vec, shift_vec, grad_rows):
    unused, pull = jax.vjp(layer_norm, rows_in, gain_vec, shift_vec)
    return pull(grad_rows)


def gelu_exact(values):
    return jax.nn.gelu(values, approximate=False)


def product(left, right):
    return jnp.dot(left, right, preferred_element_type=jnp.float32)


def times_transposed(left, right):
    return lax.dot_general(
        left, right, (((1,), (1,)), ((), ())), preferred_element_type=jnp.float32
    )


def transposed_times(left, right):
    return lax.dot_general(
        left, right, (((0,), (0,)), ((), ())), preferred_element_type=jnp.float32
    )


def attend_forward(queries, key_rows, values, factor):
    scores = (
        jnp.einsum("iqhd,ikhd->ihqk", queries, key_rows, preferred_element_type=jnp.float32)
        * factor
    )
    row_max = jnp.max(scores, axis=-1, keepdims=True)
    raised = jnp.exp(scores - row_max)
    sum_exp = jnp.sum(raised, axis=-1, keepdims=True)
    probs_low = (raised / sum_exp).astype(jnp.bfloat16)
    context = jnp.einsum("ihqk,ikhd->iqhd", probs_low, values, preferred_element_type=jnp.float32)
    return (context, row_max + jnp.log(sum_exp))


def attend_backward(queries, key_rows, values, log_total, grad_context, factor):
    scores = (
        jnp.einsum("iqhd,ikhd->ihqk", queries, key_rows, preferred_element_type=jnp.float32)
        * factor
    )
    probs = jnp.exp(scores - log_total)
    grad_probs = jnp.einsum(
        "iqhd,ikhd->ihqk", grad_context, values, preferred_element_type=jnp.float32
    )
    inner = jnp.sum(grad_probs * probs, axis=-1, keepdims=True)
    grad_scores = (probs * (grad_probs - inner)).astype(jnp.bfloat16)
    grad_queries = (
        jnp.einsum("ihqk,ikhd->iqhd", grad_scores, key_rows, preferred_element_type=jnp.float32)
        * factor
    )
    grad_keys = (
        jnp.einsum("ihqk,iqhd->ikhd", grad_scores, queries, preferred_element_type=jnp.float32)
        * factor
    )
    grad_values = jnp.einsum(
        "ihqk,iqhd->ikhd",
        probs.astype(jnp.bfloat16),
        grad_context,
        preferred_element_type=jnp.float32,
    )
    return (grad_queries, grad_keys, grad_values)


def gathered_body(
    tokens,
    masked,
    cotangent,
    mask_token,
    gain_one,
    shift_one,
    w_query,
    w_key,
    w_value,
    b_query,
    b_value,
    w_out,
    b_out,
    scale_one,
    gain_two,
    shift_two,
    w_up,
    b_up,
    w_down,
    b_down,
    scale_two,
):
    local_cols = w_query.shape[1]
    local_heads = local_cols // HD
    factor = 1.0 / math.sqrt(HD)
    chosen = (masked > 0)[:, None]
    initial = jnp.where(chosen, mask_token[None, :], tokens.astype(jnp.float32))
    normed = layer_norm(initial, gain_one, shift_one).astype(jnp.bfloat16)
    w_joined = jnp.concatenate([w_query, w_key, w_value], axis=1)
    b_joined = jnp.concatenate([b_query, jnp.zeros_like(b_query), b_value])
    gathered = lax.all_gather(normed, "tp", axis=0, tiled=True)
    joined = (product(gathered, w_joined) + b_joined).astype(jnp.bfloat16)
    group_rows = gathered.shape[0]
    head_shape = (group_rows // SEQ, SEQ, local_heads, HD)
    queries = joined[:, :local_cols].reshape(head_shape)
    key_rows = joined[:, local_cols : 2 * local_cols].reshape(head_shape)
    values = joined[:, 2 * local_cols :].reshape(head_shape)
    context, log_total = attend_forward(queries, key_rows, values, factor)
    context = context.reshape(group_rows, local_cols).astype(jnp.bfloat16)
    branch = (
        lax.psum_scatter(
            product(context, w_out).astype(jnp.bfloat16), "tp", scatter_dimension=0, tiled=True
        ).astype(jnp.float32)
        + b_out
    )
    middle = initial + scale_one * branch
    normed_two = layer_norm(middle, gain_two, shift_two).astype(jnp.bfloat16)
    gathered_two = lax.all_gather(normed_two, "tp", axis=0, tiled=True)
    pre_act = product(gathered_two, w_up) + b_up
    hidden = gelu_exact(pre_act).astype(jnp.bfloat16)
    output = (
        lax.psum_scatter(
            product(hidden, w_down).astype(jnp.bfloat16), "tp", scatter_dimension=0, tiled=True
        ).astype(jnp.float32)
        + b_down
    )
    block_out = (middle + scale_two * output).astype(jnp.bfloat16)
    grad_block = cotangent.astype(jnp.float32) * chosen.astype(jnp.float32)
    grad_output = (scale_two * grad_block).astype(jnp.bfloat16)
    grad_scale_two = jnp.sum(grad_block * output, axis=0)
    grad_b_down = jnp.sum(grad_output.astype(jnp.float32), axis=0)
    portion = lax.all_gather(grad_output, "tp", axis=0, tiled=True)
    grad_hidden = times_transposed(portion, w_down)
    grad_w_down = transposed_times(hidden, portion)
    grad_hidden, grad_w_down = (grad_hidden, grad_w_down)
    unused, gelu_pull = jax.vjp(gelu_exact, pre_act)
    grad_pre = gelu_pull(grad_hidden)[0].astype(jnp.bfloat16)
    grad_b_up = jnp.sum(grad_pre.astype(jnp.float32), axis=0)
    grad_normed_two = lax.psum_scatter(
        times_transposed(grad_pre, w_up).astype(jnp.bfloat16), "tp", scatter_dimension=0, tiled=True
    ).astype(jnp.float32)
    grad_w_up = transposed_times(lax.all_gather(normed_two, "tp", axis=0, tiled=True), grad_pre)
    grad_middle_norm, grad_gain_two, grad_shift_two = norm_backward(
        middle, gain_two, shift_two, grad_normed_two
    )
    grad_middle = grad_block + grad_middle_norm
    grad_branch = (scale_one * grad_middle).astype(jnp.bfloat16)
    grad_scale_one = jnp.sum(grad_middle * branch, axis=0)
    grad_b_out = jnp.sum(grad_branch.astype(jnp.float32), axis=0)
    portion = lax.all_gather(grad_branch, "tp", axis=0, tiled=True)
    grad_context = times_transposed(portion, w_out)
    grad_w_out = transposed_times(context, portion)
    grad_context, grad_w_out = (grad_context, grad_w_out)
    grad_context = grad_context.astype(jnp.bfloat16).reshape(head_shape)
    grad_queries, grad_keys, grad_values = attend_backward(
        queries, key_rows, values, log_total, grad_context, factor
    )
    grad_joined = jnp.concatenate(
        [
            grad_queries.reshape(group_rows, local_cols),
            grad_keys.reshape(group_rows, local_cols),
            grad_values.reshape(group_rows, local_cols),
        ],
        axis=1,
    ).astype(jnp.bfloat16)
    grad_b_query = jnp.sum(grad_joined[:, :local_cols].astype(jnp.float32), axis=0)
    grad_b_value = jnp.sum(grad_joined[:, 2 * local_cols :].astype(jnp.float32), axis=0)
    grad_normed = lax.psum_scatter(
        times_transposed(grad_joined, w_joined).astype(jnp.bfloat16),
        "tp",
        scatter_dimension=0,
        tiled=True,
    ).astype(jnp.float32)
    grad_w_joined = transposed_times(lax.all_gather(normed, "tp", axis=0, tiled=True), grad_joined)
    grad_initial_norm, grad_gain_one, grad_shift_one = norm_backward(
        initial, gain_one, shift_one, grad_normed
    )
    grad_initial = grad_middle + grad_initial_norm
    grad_tokens = jnp.where(chosen, 0.0, grad_initial)
    grad_mask_token = jnp.sum(jnp.where(chosen, grad_initial, 0.0), axis=0)
    (
        grad_mask_token,
        grad_gain_one,
        grad_shift_one,
        grad_b_out,
        grad_scale_one,
        grad_gain_two,
        grad_shift_two,
        grad_b_down,
        grad_scale_two,
    ) = lax.psum(
        (
            grad_mask_token,
            grad_gain_one,
            grad_shift_one,
            grad_b_out,
            grad_scale_one,
            grad_gain_two,
            grad_shift_two,
            grad_b_down,
            grad_scale_two,
        ),
        ("dp", "tp"),
    )
    grad_b_query, grad_b_value, grad_b_up = lax.psum((grad_b_query, grad_b_value, grad_b_up), "dp")
    grad_w_joined, grad_w_out, grad_w_up, grad_w_down = (
        lax.psum_scatter(
            grad_w_joined.astype(jnp.bfloat16), "dp", scatter_dimension=0, tiled=True
        ).astype(jnp.float32),
        lax.psum_scatter(
            grad_w_out.astype(jnp.bfloat16), "dp", scatter_dimension=1, tiled=True
        ).astype(jnp.float32),
        lax.psum_scatter(
            grad_w_up.astype(jnp.bfloat16), "dp", scatter_dimension=0, tiled=True
        ).astype(jnp.float32),
        lax.psum_scatter(
            grad_w_down.astype(jnp.bfloat16), "dp", scatter_dimension=1, tiled=True
        ).astype(jnp.float32),
    )
    grad_w_query = grad_w_joined[:, :local_cols]
    grad_w_key = grad_w_joined[:, local_cols : 2 * local_cols]
    grad_w_value = grad_w_joined[:, 2 * local_cols :]
    return (
        block_out,
        grad_tokens,
        grad_mask_token,
        grad_gain_one,
        grad_shift_one,
        grad_w_query,
        grad_w_key,
        grad_w_value,
        grad_b_query,
        grad_b_value,
        grad_w_out,
        grad_b_out,
        grad_scale_one,
        grad_gain_two,
        grad_shift_two,
        grad_w_up,
        grad_b_up,
        grad_w_down,
        grad_b_down,
        grad_scale_two,
    )


def nn(left, right):
    return lax.dot_general(left, right, (((1,), (0,)), ((), ())), preferred_element_type=F32)


def nt(left, right):
    return lax.dot_general(left, right, (((1,), (1,)), ((), ())), preferred_element_type=F32)


def tn(left, right):
    return lax.dot_general(left, right, (((0,), (0,)), ((), ())), preferred_element_type=F32)


def padded(rows):
    return -(-rows // 32) * 32


def windows(rows):
    found = []
    for image in range(rows // SEQ):
        first = image * SEQ
        start = first // 16 * 16
        found.append((start, -(-(first - start + SEQ) // 16) * 16, first - start))
    return found


def row_blocks(total, size=160):
    return [slice(s, min(s + size, total)) for s in range(0, total, size)]


def inside(shape, axis, offset):
    at = lax.broadcasted_iota(jnp.int32, shape, axis)
    return (at >= offset) & (at < offset + SEQ)


def col_sum(values):
    return jnp.sum(values, axis=0, keepdims=True)


def row_mean(values):
    return jnp.mean(values, axis=-1, keepdims=True)


def moments(rows_in):
    center = rows_in - row_mean(rows_in)
    return center, lax.rsqrt(row_mean(center * center) + EPSILON)


def norm_pull(rows_in, gain, grad):
    center, inv = moments(rows_in)
    hat = center * inv
    scaled = grad * gain
    back = (scaled - row_mean(scaled) - hat * row_mean(scaled * hat)) * inv
    return back, col_sum(grad * hat), col_sum(grad)


def gelu_parts(v):
    cdf = 0.5 + 0.5 * lax.erf(v * math.sqrt(0.5))
    return cdf, v * (jnp.exp(-0.5 * (v * v)) * (1.0 / math.sqrt(2.0 * math.pi)))


def rows_outside(values, offset, fill):
    size = values.shape[0]

    def edge(part, base):
        at = lax.broadcasted_iota(jnp.int32, part.shape, 0) + base
        return jnp.where((at >= offset) & (at < offset + SEQ), part, fill)

    head = edge(values[:16], 0) if offset else values[:16]
    return jnp.concatenate([head, values[16:-32], edge(values[-32:], size - 32)], axis=0)


def one_head(shape, head):
    return (lax.broadcasted_iota(jnp.int32, shape, 1) < HD) == (head == 0)


def in_turn(rows, lead, begin, finish):
    units = [(window, head) for window in windows(rows) for head in (0, 1)]
    begun = [begin(*unit) for unit in units[:lead]]
    for i, unit in enumerate(units):
        if i + lead < len(units):
            begun.append(begin(*units[i + lead]))
        finish(i, *unit, begun[i])
        begun[i] = None


def norm_rows(rows, cols):
    return (cols // HD * (rows // SEQ), 256)


def attend(rows, q_ref, k_ref, v_ref, ctx_ref, log_ref):
    ctx_ref[padded(rows) - 32 :, :] = jnp.zeros((32, ctx_ref.shape[1]), BF16)
    count = 2 * (rows // SEQ)

    def one_pair(pair, carry):
        lanes = pl.ds(pl.multiple_of(pair * PAIR, PAIR), PAIR)
        halves = {}

        def begin(window, head):
            start, size, _ = window
            win = slice(start, start + size)
            k = k_ref[win, lanes]
            return nt(jnp.where(one_head(k.shape, head), k, jnp.zeros_like(k)), q_ref[win, lanes])

        def finish(i, window, head, scores):
            start, size, offset = window
            win = slice(start, start + size)
            scores = rows_outside(scores, offset, LOWEST)
            top = jnp.max(scores, axis=0, keepdims=True)
            raised = jnp.exp(scores - top)
            total = jnp.sum(raised, axis=0, keepdims=True)
            out = tn(v_ref[win, lanes], raised.astype(BF16))
            halves[head] = out[head * HD : (head + 1) * HD] * (1.0 / total)
            log_ref[pl.ds(pair * count + i, 1), :size] = top + jnp.log(total)
            if head == 1:
                both = jnp.concatenate([halves[0], halves[1]], axis=0).T.astype(BF16)
                keep = inside((size, PAIR), 0, offset)
                ctx_ref[win, lanes] = jnp.where(keep, both, ctx_ref[win, lanes])

        in_turn(rows, 4, begin, finish)
        return carry

    lax.fori_loop(0, q_ref.shape[1] // PAIR, one_pair, 0, unroll=4)


def attend_back(rows, q_ref, k_ref, v_ref, gc_ref, log_ref, dq_ref, dk_ref, dv_ref):
    for ref in (dq_ref, dk_ref, dv_ref):
        ref[padded(rows) - 32 :, :] = jnp.zeros((32, ref.shape[1]), BF16)
    factor = 1.0 / math.sqrt(HD)
    count = 2 * (rows // SEQ)

    def one_pair(pair, carry):
        lanes = pl.ds(pl.multiple_of(pair * PAIR, PAIR), PAIR)
        halves = {}

        def begin(window, head):
            start, size, offset = window
            win = slice(start, start + size)
            zero = jnp.zeros((size, PAIR), BF16)
            mine = one_head(zero.shape, head)
            k = jnp.where(mine, k_ref[win, lanes], zero)
            v = jnp.where(mine, v_ref[win, lanes], zero)
            gc = jnp.where(inside(zero.shape, 0, offset), gc_ref[win, lanes], zero)
            q = q_ref[win, lanes]
            return nt(k, q), nt(v, gc), k, q, gc

        def finish(i, window, head, begun):
            start, size, offset = window
            win = slice(start, start + size)
            scores, grad_probs, k, q, gc = begun
            scores = rows_outside(scores, offset, LOWEST)
            probs = jnp.exp(scores - log_ref[pl.ds(pair * count + i, 1), :size])
            inner = jnp.sum(grad_probs * probs, axis=0, keepdims=True)
            grad_scores = (probs * (grad_probs - inner)).astype(BF16)
            halves[head] = tn(grad_scores, k), nn(grad_scores, q), nn(probs.astype(BF16), gc)
            if head == 1:
                keep = inside((size, PAIR), 0, offset)
                first = one_head((size, PAIR), 0)
                low, high = halves[0], halves[1]
                for ref, new in (
                    (dq_ref, (low[0] + high[0]) * factor),
                    (dk_ref, jnp.where(first, low[1], high[1])),
                    (dv_ref, jnp.where(first, low[2], high[2])),
                ):
                    ref[win, lanes] = jnp.where(keep, new.astype(BF16), ref[win, lanes])

        in_turn(rows, 2, begin, finish)
        return carry

    lax.fori_loop(0, q_ref.shape[1] // PAIR, one_pair, 0, unroll=2)


class Moved:
    def __init__(self, far, near, line, pieces=(None,)):
        self.far, self.near, self.line, self.pieces = far, near, line, pieces
        self.copies = [line.add(*self.views(p)) for p in pieces]

    def views(self, p):
        return (self.far, self.near) if p is None else (self.far.at[p], self.near.at[p])

    def part(self, i):
        self.line.wait(self.copies[i])
        return self.views(self.pieces[i])[1]

    @property
    def ref(self):
        for copy in self.copies:
            self.line.wait(copy)
        return self.near

    def send(self, p=None):
        far, near = self.views(p)
        self.line.send(near, far)


class Line:
    def __init__(self, sems, count):
        self.sems, self.free = sems, iter(range(count))
        self.queue, self.waves, self.started, self.waited, self.sent = [], [], 0, set(), []

    def copy(self, source, target):
        return pltpu.make_async_copy(source, target, self.sems.at[next(self.free)])

    def add(self, source, target):
        self.queue.append(self.copy(source, target))
        return len(self.queue) - 1

    def begin(self, waves=()):
        first = [i for wave in waves for i in wave]
        rest = [i for i in range(len(self.queue)) if i not in first]
        self.waves = [list(wave) for wave in waves] + [rest]
        self.start_to(1)

    def start_to(self, stop):
        while self.started < min(stop, len(self.waves)):
            for i in self.waves[self.started]:
                self.queue[i].start()
            self.started += 1

    def wait(self, i):
        if i in self.waited:
            return
        wave = next(k for k, some in enumerate(self.waves) if i in some)
        self.start_to(wave + 1)
        self.queue[i].wait()
        self.waited.add(i)
        self.start_to(wave + 2)

    def send(self, source, target):
        copy = self.copy(source, target)
        copy.start()
        self.sent.append(copy)

    def finish(self):
        for i in range(len(self.queue)):
            self.wait(i)
        for copy in self.sent:
            copy.wait()


class View:
    def __init__(self, array, axis=0, start=0, size=None):
        self.array, self.shape, self.index = array, array.shape, None
        if size is not None:
            p = slice(start, start + size)
            self.index = (slice(None),) * axis + (p,)
            self.shape = tuple(size if i == axis else n for i, n in enumerate(array.shape))


def cut_in(size, axis, count):
    step = size // count
    spans = [slice(i * step, (i + 1) * step) for i in range(count)]
    return [(slice(None),) * axis + (p,) for p in spans]


def moved_call(kernel, outs, args, flops, sends, scratch=(), name=None, after=(), cuts=None, waves=()):
    hbm = pl.BlockSpec(memory_space=pl.ANY)
    cuts = cuts or {}
    views = [a if isinstance(a, View) else View(a) for a in args]
    args = [view.array for view in views]
    n_in, n_out = len(args), len(outs)
    pieces = [
        cut_in(v.shape[cuts[i][0]], *cuts[i]) if i in cuts else [None] for i, v in enumerate(views)
    ]
    n_sems = sum(len(p) for p in pieces) + sends
    buffers = [pltpu.VMEM(v.shape, v.array.dtype) for v in views]
    buffers += [pltpu.VMEM(o.shape, o.dtype) for o in outs]

    def inner(*refs):
        refs = refs[len(after) :]
        far_in, far_out, rest = refs[:n_in], refs[n_in : n_in + n_out], list(refs[n_in + n_out :])
        line = Line(rest.pop(), n_sems)
        ins = []
        for far, view, p in zip(far_in, views, pieces):
            far = far if view.index is None else far.at[view.index]
            ins.append(Moved(far, rest.pop(0), line, p))
        line.begin([[ins[i].copies[j] for i, j in wave] for wave in waves])
        results = [Moved(far, rest.pop(0), line, ()) for far in far_out]
        kernel(*ins, *results, *rest)
        line.finish()

    return pl.pallas_call(
        inner,
        in_specs=[hbm] * (len(after) + n_in),
        out_specs=[hbm] * n_out,
        out_shape=outs,
        scratch_shapes=buffers + list(scratch) + [pltpu.SemaphoreType.DMA((n_sems,))],
        compiler_params=pltpu.CompilerParams(vmem_limit_bytes=KERNEL_VMEM),
        cost_estimate=cost(flops, *args, *outs),
        name=name,
    )(*after, *args)


def halves_of(tall):
    middle = tall // 2 // 16 * 16
    return [slice(0, middle), slice(middle, tall)]


def blocks_within(part, rows, size=400):
    stop = min(part.stop, rows)
    return [slice(s, min(s + size, stop)) for s in range(part.start, stop, size)]


def first_kernel(
    rows, tok, mask, mt, gain, shift, wq, wk, wv, bq, bv,
    normed, q, k, v, ctx, log,
):
    normed_ref = normed.near
    tok_ref, mask_ref = tok.ref, mask.ref
    mt_ref, gain_ref, shift_ref = mt.ref, gain.ref, shift.ref
    for block in blocks_within(slice(0, rows), rows):
        initial = jnp.where(mask_ref[block] > 0, mt_ref[...], tok_ref[block].astype(F32))
        center, inv = moments(initial)
        normed_ref[block] = (center * inv * gain_ref[...] + shift_ref[...]).astype(BF16)
    over = padded(rows) - rows
    normed_ref[rows:] = jnp.zeros((over, normed_ref.shape[1]), BF16)
    normed.send()
    project(normed_ref, [wq, wk, wv], bq, bv, q, k, v)
    attend(rows, q.near, k.near, v.near, ctx.near, log.near)
    ctx.send()
    log.send()


def project(normed_ref, weights, bq, bv, q, k, v):
    scale = BF16(1.0 / math.sqrt(HD))
    wq, wk, wv = weights
    q.near[...] = (nn(normed_ref[...], wq.ref[...]) + bq.ref[...]).astype(BF16) * scale
    q.send()
    k.near[...] = nn(normed_ref[...], wk.ref[...]).astype(BF16)
    k.send()
    v.near[...] = (nn(normed_ref[...], wv.ref[...]) + bv.ref[...]).astype(BF16)
    v.send()


class Third:
    def __init__(self, moved, i):
        self.moved, self.i = moved, i

    @property
    def ref(self):
        return self.moved.part(self.i)


def second_kernel(
    rows, normed, joined, bq, bv, ctx, wo, wo2, bo,
    s1, gain, shift, tok, mask, mt, cot, s2,
    q, k, v, ctx2, log, middle, normed2, go, sums, acc_ref,
):
    project(normed.ref, [Third(joined, i) for i in range(3)], bq, bv, q, k, v)
    attend(rows, q.near, k.near, v.near, ctx2.near, log.near)
    ctx2.send()
    log.send()
    over = padded(rows) - rows
    width = acc_ref.shape[1]
    total = jnp.zeros((1, width), F32)
    ctx_ref, wo_ref, wo2_ref = ctx.ref, wo.ref, wo2.ref
    tok_ref, mask_ref, cot_ref = tok.ref, mask.ref, cot.ref
    bo_ref, s1_ref, gain_ref, shift_ref, mt_ref, s2_ref = (v.ref for v in (bo, s1, gain, shift, mt, s2))
    for half in halves_of(padded(rows)):
        acc_ref[half] = nn(ctx_ref[half], wo_ref[...]) + nn(ctx2.near[half], wo2_ref[...])
    for half in halves_of(padded(rows)):
        for block in blocks_within(half, rows):
            masked = mask_ref[block] > 0
            initial = jnp.where(masked, mt_ref[...], tok_ref[block].astype(F32))
            one = initial + s1_ref[...] * (acc_ref[block] + bo_ref[...])
            middle.near[block] = one
            center, inv = moments(one)
            normed2.near[block] = (center * inv * gain_ref[...] + shift_ref[...]).astype(BF16)
            grad_out = jnp.where(masked, cot_ref[block].astype(F32), 0.0) * s2_ref[...]
            grad_out = grad_out.astype(BF16)
            go.near[block] = grad_out
            total += col_sum(grad_out.astype(F32))
        if half.stop == padded(rows):
            middle.near[rows:] = jnp.zeros((over, width), F32)
            normed2.near[rows:] = jnp.zeros((over, width), BF16)
            go.near[rows:] = jnp.zeros((over, width), BF16)
        for one in (normed2, go, middle):
            one.send(half)
    sums.near[...] = total
    sums.send()


def feed_kernel(chunk, n2, wu, go, wd, bu, hidden, gp, grads, sums, scale_sum):
    me = lax.axis_index("dp")
    cols = hidden.near.shape[1]
    width = n2.near.shape[1]
    lanes = None
    for i in range(cols // chunk):
        at = slice(i * chunk, (i + 1) * chunk)
        pre = nn(n2.ref[...], wu.part(i)[...]) + bu.ref[:, at]
        grad_hidden = nt(go.ref[...], wd.part(i)[...])
        cdf, slope = gelu_parts(pre)
        new_hidden = (pre * cdf).astype(BF16)
        grad_pre = (grad_hidden * (cdf + slope)).astype(BF16)
        hidden.near[:, at] = new_hidden
        gp.near[:, at] = grad_pre
        hidden.send((slice(None), at))
        gp.send((slice(None), at))
        sums.near[:, at] = col_sum(grad_pre.astype(F32))
        down = tn(go.ref[...], new_hidden)
        weighed = down * wd.part(i)[...].T.astype(F32)
        for k in range(0, chunk, 128):
            part = weighed[:, k : k + 128]
            lanes = part if lanes is None else lanes + part
        for j, grad in enumerate((down, tn(n2.ref[...], grad_pre))):
            base = (2 * i + j) * chunk
            store_blocks(me, grad, grads.near, base)
            grads.send((slice(None), slice(None), slice(base, base + chunk)))
    sums.send()
    scale_sum.near[...] = col_sum(lanes.T)
    scale_sum.send()


def store_blocks(me, product_rows, out_ref, at):
    parts, size, _ = out_ref.shape
    cols = product_rows.shape[1]
    for b in range(parts):
        out_ref[b ^ me, :, at : at + cols] = product_rows[b * size : (b + 1) * size].astype(BF16)


def in_pieces(*groups):
    for some in zip(*groups):
        for j in range(len(some[0].pieces)):
            yield [functools.partial(one.part, j) for one in some]


def middle_kernel(rows, count, *refs):
    gps, wus = refs[:count], refs[count : 2 * count]
    middle, tok, mask, mt, cot, gain, s1 = refs[2 * count : 2 * count + 7]
    gm, gbr, sums, acc_ref = refs[2 * count + 7 :]
    width = acc_ref.shape[1]
    total = [jnp.zeros((1, width), F32)] * 4
    halves = halves_of(padded(rows))
    for i, (one, w) in enumerate(in_pieces(gps, wus)):
        for half in halves:
            part = nt(one()[half], w()[...])
            acc_ref[half] = part if i == 0 else acc_ref[half] + part
    middle_ref, tok_ref, mask_ref, cot_ref = middle.ref, tok.ref, mask.ref, cot.ref
    mt_ref, gain_ref, s1_ref = mt.ref, gain.ref, s1.ref
    over = padded(rows) - rows
    for half in halves:
        for block in blocks_within(half, rows):
            masked = mask_ref[block] > 0
            one = middle_ref[block]
            back, grad_gain, grad_shift = norm_pull(one, gain_ref[...], acc_ref[block])
            grad_middle = jnp.where(masked, cot_ref[block].astype(F32), 0.0) + back
            gm.near[block] = grad_middle
            grad_branch = (s1_ref[...] * grad_middle).astype(BF16)
            gbr.near[block] = grad_branch
            initial = jnp.where(masked, mt_ref[...], tok_ref[block].astype(F32))
            new = (
                grad_gain,
                grad_shift,
                col_sum(grad_middle * (one - initial)) / s1_ref[...],
                col_sum(grad_branch.astype(F32)),
            )
            total = [a + b for a, b in zip(total, new)]
        if half.stop == padded(rows):
            gm.near[rows:] = jnp.zeros((over, width), F32)
            gbr.near[rows:] = jnp.zeros((over, width), BF16)
        gbr.send(half)
        gm.send(half)
    for i, one in enumerate(total):
        sums.near[i : i + 1] = one
    sums.send()


def back_kernel(
    rows, gbr, wo, ctx, q, k, v, log, n1,
    dq, dk, dv, grads, sums, gc_ref,
):
    me = lax.axis_index("dp")
    cols = dq.near.shape[1]
    gc_ref[...] = nt(gbr.ref[...], wo.ref[...]).astype(BF16)
    store_blocks(me, tn(gbr.ref[...], ctx.ref[...]), grads.near, 3 * cols)
    grads.send((slice(None), slice(None), slice(3 * cols, 4 * cols)))
    attend_back(rows, q.ref, k.ref, v.ref, gc_ref, log.ref, dq.near, dk.near, dv.near)
    for i, one in enumerate((dq, dk, dv)):
        one.send()
        store_blocks(me, tn(n1.ref[...], one.near[...]), grads.near, i * cols)
        grads.send((slice(None), slice(None), slice(i * cols, (i + 1) * cols)))
        if i != 1:
            at = i // 2 * cols
            sums.near[:, at : at + cols] = col_sum(one.near[...].astype(F32))
    sums.send()


def middle_back_kernel(rows, count, *refs):
    first, others = refs[: 2 * count + 7], refs[2 * count + 7 : 2 * count + 14]
    (gm, gbr, sums), outs = refs[2 * count + 14 : 2 * count + 17], refs[2 * count + 17 : 2 * count + 22]
    acc_ref, gc_ref = refs[2 * count + 22 :]
    middle_kernel(rows, count, *first, gm, gbr, sums, acc_ref)
    back_kernel(rows, gbr, *others, *outs, gc_ref)


def input_kernel(rows, *refs):
    grads, weights = refs[:6], list(refs[6:9]) + [Third(refs[9], i) for i in range(3)]
    tok, mask, mt, gain, gm, out, sums, acc_ref = refs[10:]
    width = acc_ref.shape[1]
    halves = halves_of(padded(rows))
    for i, (one, w) in enumerate(zip(grads, weights)):
        for half in halves:
            part = nt(one.ref[half], w.ref[...])
            acc_ref[half] = part if i == 0 else acc_ref[half] + part
    total = [jnp.zeros((1, width), F32)] * 3
    tok_ref, mask_ref, gm_ref, mt_ref, gain_ref = tok.ref, mask.ref, gm.ref, mt.ref, gain.ref
    for half in halves:
        for block in blocks_within(half, rows):
            masked = mask_ref[block] > 0
            initial = jnp.where(masked, mt_ref[...], tok_ref[block].astype(F32))
            back, grad_gain, grad_shift = norm_pull(initial, gain_ref[...], acc_ref[block])
            grad_initial = gm_ref[block] + back
            out.near[block] = jnp.where(masked, 0.0, grad_initial)
            new = (col_sum(jnp.where(masked, grad_initial, 0.0)), grad_gain, grad_shift)
            total = [a + b for a, b in zip(total, new)]
    out.send()
    for i, one in enumerate(total):
        sums.near[i : i + 1] = one
    sums.send()


def output_kernel(rows, count, *refs):
    hiddens, wds = refs[:count], refs[count : 2 * count]
    middle, bd, s2, out, acc_ref = refs[2 * count :]
    halves = halves_of(padded(rows))
    for i, (one, w) in enumerate(in_pieces(hiddens, wds)):
        for half in halves:
            part = nn(one()[half], w()[...])
            acc_ref[half] = part if i == 0 else acc_ref[half] + part
    middle_ref, bd_ref, s2_ref = middle.ref, bd.ref, s2.ref
    for block in blocks_within(slice(0, rows), rows):
        output = acc_ref[block] + bd_ref[...]
        out.near[block] = (middle_ref[block] + s2_ref[...] * output).astype(BF16)
    out.send()


def shape_of(shape, dtype=BF16):
    return jax.ShapeDtypeStruct(shape, dtype)


def cost(flops, *arrays):
    moved = sum(a.size * a.dtype.itemsize for a in arrays)
    return pl.CostEstimate(flops=flops, bytes_accessed=moved, transcendentals=0)


def without(kernel, at, count):
    def inner(*refs):
        kernel(*refs[:at], *refs[at + count :])

    return inner


def pairs(n, bit):
    return [(i, i ^ (1 << bit)) for i in range(n)]


TILE = 256


class Segment:
    def __init__(self, terms, start, width, order):
        self.start, self.width, self.order, self.used, self.got = start, width, list(order), [], []
        self.bits = sorted(order, reverse=True)
        dims = (2,) * len(self.bits)
        self.terms = [(a.reshape(dims + a.shape[1:]), base + start) for a, base in terms]
        self.rows = terms[0][0].shape[1]
        self.across = width // TILE

    @property
    def rest(self):
        return self.order[1:]

    @property
    def tiles(self):
        return self.across << len(self.rest)

    def views(self):
        bit, found = self.order[0] if self.order else None, []
        for array, start in self.terms:
            one = View(array)
            one.index = tuple(0 if b in self.used else 1 if b == bit else slice(None) for b in self.bits)
            one.index += (slice(None), slice(start, start + self.width))
            one.shape = (2,) * len(self.rest) + (self.rows, self.width)
            found.append(one)
        for array, start in self.got:
            found.append(View(array, 0, start + (self.tiles if self.order else 0), self.tiles))
        return found

    def add(self, refs):
        originals, got = refs[: len(self.terms)], refs[len(self.terms) :]
        for at in range(1 << len(self.rest)):
            side = {b: at >> (len(self.rest) - 1 - i) & 1 for i, b in enumerate(self.rest)}
            index = tuple(side[b] for b in self.bits if b in side)
            for c in range(self.across):
                cols, tile = slice(c * TILE, (c + 1) * TILE), at * self.across + c
                parts = [ref[(*index, slice(None), cols)] for ref in originals] + [ref[tile] for ref in got]
                yield tile, self.start + c * TILE, functools.reduce(jnp.add, [p.astype(F32) for p in parts])

    def received(self, array, start):
        self.used.append(self.order.pop(0))
        self.got.append((array, start))


class Group:
    def __init__(self, segments, block):
        self.segments, self.block, self.result = segments, block, None
        self.width = sum(s.width for s in segments)

    @property
    def last(self):
        return not self.segments[0].order


class Sums:
    def __init__(self, same, own, other, bits, last):
        self.parts, self.own, self.n_own, self.last_terms = same + other, same + own, len(own), last
        self.rounds = [bits[i : i + 2] for i in range(0, len(bits), 2)]
        self.stage, self.terms, self.result = 0, [], None

    def job(self):
        width = self.parts[0].shape[1]
        height = -(-sum(p.size for p in self.parts) // (8 * width)) * 8
        packed = {0: self.parts, 1: self.own}.get(self.stage, [])
        places, row, col = [], 0, 0
        for p in packed:
            steps = []
            for at in range(0, p.shape[1], width):
                size = min(width, p.shape[1] - at)
                steps.append(((slice(row, row + p.shape[0]), slice(col, col + size)), slice(at, at + size)))
                col += size
                if col == width:
                    row, col = row + p.shape[0], 0
            places.append(steps)
        return packed, places, self.terms, shape_of((height, width), F32)

    def final_shapes(self):
        own = self.own[len(self.own) - self.n_own :]
        width = own[0].shape[1]
        return [shape_of((1, width), F32)] * 9 + [shape_of((1, width // 2), F32)] * 2 + [
            shape_of((1, sum(p.size for p in own[1:])), F32)
        ]

    def final(self, total, ins, outs):
        bias, scale = (one.ref[...] for one in ins)
        start = sum(p.shape[0] for p in self.own[: len(self.own) - self.n_own])
        rows = [total[i : i + 1] for i in range(total.shape[0])]
        for out, value in zip(outs, rows[:8]):
            out.near[...] = value
        outs[8].near[...] = (functools.reduce(jnp.add, rows[8:start]) + bias * rows[7]) / scale
        half = outs[9].near.shape[1]
        outs[9].near[...] = rows[start][:, :half]
        outs[10].near[...] = rows[start][:, half:]
        count = outs[11].near.shape[1] // (2 * half)
        for i, value in enumerate(rows[start + 1 : start + 1 + count]):
            outs[11].near[:, i * 2 * half : (i + 1) * 2 * half] = value

    @property
    def last(self):
        return self.stage == len(self.rounds) + 1

    def take(self, sent):
        n = lax.axis_size("dp")
        if self.last:
            self.result = sent
        elif self.stage == 0:
            self.terms = [swap(sent[0])]
        else:
            bits = self.rounds[self.stage - 1]
            self.terms = list(sent)
            for some in range(1, 1 << len(bits)):
                flip = sum(1 << b for i, b in enumerate(bits) if some >> i & 1)
                self.terms.append(lax.ppermute(sent[0], "dp", [(d, d ^ flip) for d in range(n)]))
        self.stage += 1


def exchange(groups, after, sums=None, carry=None):
    buffers, shapes, plan = {}, [], []
    for segment in [s for g in groups if not g.last for s in g.segments]:
        buffers.setdefault(segment.order[0], []).append(segment)
    for some in buffers.values():
        starts = [sum(s.tiles for s in some[:i]) for i in range(len(some))]
        plan.append(list(zip(some, starts)))
        shapes.append(shape_of((sum(s.tiles for s in some), some[0].rows, TILE)))
    ending = [g for g in groups if g.last]
    for g in ending:
        shapes += [shape_of((g.segments[0].rows, g.block), F32)] * (g.width // g.block)
    views = [s.views() for one in plan for s, _ in one] + [s.views() for g in ending for s in g.segments]
    counts = [len(v) for v in views]
    views = [v for some in views for v in some]
    n_summed = len(shapes)
    packed, places, terms = [], [], []
    sums_last = sums is not None and sums.last
    if sums is not None:
        packed, places, terms, shape = sums.job()
        views += [View(a) for a in packed + terms + (sums.last_terms if sums_last else [])]
        shapes += sums.final_shapes() if sums_last else [shape]
    passed = [] if carry is None else [carry]
    hbm = pl.BlockSpec(memory_space=pl.ANY)
    skipped, n_in, n_out = len(after) + len(passed), len(views), len(shapes)

    def kernel(*refs):
        far_in, far_out = refs[skipped : skipped + n_in], refs[skipped + n_in :][:n_out]
        nears = list(refs[skipped + n_in + n_out + len(passed) :])
        line = Line(nears.pop(), n_in + n_out)
        ins = []
        for far, view in zip(far_in, views):
            far = far if view.index is None else far.at[view.index]
            ins.append(Moved(far, nears.pop(0), line))
        line.begin()
        outs = [Moved(far, nears.pop(0), line, ()) for far in far_out]
        sizes = list(counts)

        def taken():
            return [ins.pop(0).ref for _ in range(sizes.pop(0))]

        for one in plan:
            out = outs.pop(0)
            for segment, start in one:
                for tile, _, total in segment.add(taken()):
                    out.near[start + tile] = total.astype(BF16)
            out.send()
        for g in ending:
            mine = [outs.pop(0) for _ in range(g.width // g.block)]
            for segment in g.segments:
                for _, col, total in segment.add(taken()):
                    mine[col // g.block].near[:, col % g.block : col % g.block + TILE] = total
            for out in mine:
                out.send()
        if sums is not None:
            if packed:
                new = outs[0]
                new.near[...] = ins[-1].ref[...] if terms else jnp.zeros(shape.shape, F32)
                for one, steps in zip(ins, places):
                    for place, cols in steps:
                        new.near[place] += one.ref[:, cols]
            else:
                total = functools.reduce(jnp.add, [one.ref[...] for one in ins[: len(terms)]])
                if sums_last:
                    sums.final(total, ins[len(terms) :], outs)
                else:
                    outs[0].near[...] = total
            for out in outs:
                out.send()
        line.finish()

    outs = pl.pallas_call(
        kernel,
        in_specs=[hbm] * (skipped + n_in),
        out_specs=[hbm] * (n_out + len(passed)),
        out_shape=shapes + [shape_of(p.shape, p.dtype) for p in passed],
        input_output_aliases={len(after): n_out} if passed else {},
        scratch_shapes=[pltpu.VMEM(v.shape, v.array.dtype) for v in views]
        + [pltpu.VMEM(o.shape, o.dtype) for o in shapes]
        + [pltpu.SemaphoreType.DMA((n_in + n_out,))],
        compiler_params=pltpu.CompilerParams(vmem_limit_bytes=EXCHANGE_VMEM),
        cost_estimate=cost(0, *shapes),
        name="exchange",
    )(*after, *passed, *[v.array for v in views])
    n, left = lax.axis_size("dp"), list(outs[:n_summed])
    for bit, one in zip(buffers, plan):
        got = lax.ppermute(left.pop(0), "dp", pairs(n, bit))
        for segment, start in one:
            segment.received(got, start)
    for g in ending:
        g.result = [left.pop(0) for _ in range(g.width // g.block)]
    if sums is not None:
        sums.take(list(outs[n_summed:n_out]))
    sent = list(outs[:n_out])
    return sent if carry is None else (sent, outs[-1])


def swap(array):
    return lax.ppermute(array, "tp", [(0, 1), (1, 0)])


def local_body(
    tokens, masked, cotangent, mask_token, gain_one, shift_one, w_query, w_key, w_value, b_query,
    b_value, w_out, b_out, scale_one, gain_two, shift_two, w_up, b_up, w_down, b_down, scale_two,
):
    rows, width = tokens.shape
    tall = padded(rows)
    half = w_query.shape[1]
    units = w_up.shape[1]
    n = lax.axis_size("dp")
    bits = n.bit_length() - 1
    me = lax.axis_index("dp").astype(jnp.int32).reshape(1)
    biases = jnp.concatenate([b_query, b_value, b_up]).reshape(1, -1)

    joined2 = swap(jnp.concatenate([w_query, w_key, w_value], axis=1))
    biases2 = swap(biases)
    wo2 = swap(w_out)
    wu2, wd2 = swap(w_up), swap(w_down)
    row = lambda v: v.reshape(1, -1)
    bq2, bv2 = View(biases2, 1, 0, half), View(biases2, 1, half, half)
    bq, bv, bu = row(b_query), row(b_value), row(b_up)
    mt, g1, s1, bo, sc1 = row(mask_token), row(gain_one), row(shift_one), row(b_out), row(scale_one)
    g2, s2, bd, sc2 = row(gain_two), row(shift_two), row(b_down), row(scale_two)
    mask = masked.reshape(rows, 1)

    narrow = shape_of((tall, half))
    wide = shape_of((tall, width))
    attend_flops = 2 * 2 * 256 * SEQ * rows * half // HD
    logs = shape_of(norm_rows(rows, half), F32)
    normed, q, k, v, ctx, log = moved_call(
        functools.partial(first_kernel, rows),
        [wide, narrow, narrow, narrow, narrow, logs],
        (tokens, mask, mt, g1, s1, w_query, w_key, w_value, bq, bv),
        6 * rows * width * half + attend_flops,
        6,
        name="first",
        waves=[[(i, 0) for i in range(5)]],
    )
    tall_f32 = shape_of((tall, width), F32)
    scratch = [pltpu.VMEM((tall, width), F32)]
    one_row = shape_of((1, width), F32)
    q2, k2, v2, ctx2, log2, middle, normed2, go, sum_go = moved_call(
        functools.partial(second_kernel, rows),
        [narrow, narrow, narrow, narrow, logs, tall_f32, wide, wide, one_row],
        (normed, joined2, bq2, bv2, ctx, w_out, wo2, bo, sc1, g2, s2, tokens, mask, mt, cotangent, sc2),
        10 * rows * width * half + attend_flops,
        12,
        scratch=scratch,
        name="second",
        cuts={1: (1, 3)},
        waves=[[(0, 0), (1, 0), (2, 0)], [(1, 1), (1, 2), (3, 0)]],
    )

    natural = tuple(range(bits))
    by_x, by_y = natural, natural[1:2] + natural[0:1] + natural[2:]
    by_zyzx = natural[2:3] + natural[1:2] + natural[3:] + natural[:1]
    by_yzzx, by_zxyz = natural[1:] + natural[:1], natural[2:3] + natural[:2] + natural[3:]

    part = units // 2
    chunk = min(1024, part)
    hiddens, gps, ups, downs = [], [], [], []

    def feed(weights, first, size, after=()):
        w_up, w_down, b_up, b_start = weights
        count = size // chunk
        hidden, gp, grads, sums, scale_sum = moved_call(
            functools.partial(feed_kernel, chunk),
            [
                shape_of((tall, size)),
                shape_of((tall, size)),
                shape_of((n, width // n, 2 * size)),
                shape_of((1, size), F32),
                one_row,
            ],
            (normed2, View(w_up, 1, first, size), go, View(w_down, 0, first, size),
             View(b_up, 1, b_start + first, size)),
            8 * tall * width * size,
            4 * count + 2,
            name="feed",
            after=after,
            cuts={1: (1, count), 3: (0, count)},
            waves=[[(i, 0) for i in range(5)]],
        )
        hiddens.append(hidden)
        gps.append(gp)
        ups.append(View(w_up, 1, first, size))
        downs.append(View(w_down, 0, first, size))
        scale_sums.append(scale_sum)
        return grads, sums

    def grouped(size, block, parts, *terms):
        whole, at, segments = sum(w for w, _ in parts), 0, []
        for w, order in parts:
            segments.append(Segment(terms, at, w * size // whole, order))
            at += w * size // whole
        return Group(segments, block)

    mine, other = (w_up, w_down, bu, 0), (wu2, wd2, biases2, 2 * half)
    scale_sums = []
    theirs, sums_up2 = feed(other, 0, units)
    theirs = swap(theirs)
    own, sums_up = feed(mine, 0, units, [sums_up2])
    parts = ((6, by_x), (5, by_yzzx), (5, by_zxyz))
    b = grouped(2 * units, chunk, parts, (own, 0), (theirs, 0))
    sent = exchange([b], [sums_up])

    back_outs = [narrow, narrow, narrow, shape_of((n, width // n, 4 * half)), shape_of((1, 2 * half), F32)]
    back_flops = 10 * rows * width * half + 3 * attend_flops
    back_scratch = [pltpu.VMEM((tall, half), BF16)]
    gm, gbr, sums_two, dq2, dk2, dv2, gw2, sums_b2 = moved_call(
        functools.partial(middle_back_kernel, rows, len(gps)),
        [tall_f32, wide, shape_of((4, width), F32)] + back_outs,
        (*gps, *ups, middle, tokens, mask, mt, cotangent, g2, sc1, wo2, ctx2, q2, k2, v2, log2, normed),
        8 * tall * width * part + back_flops,
        13,
        scratch=scratch + back_scratch,
        name="middle",
        after=sent,
        cuts={i: (1, 2) for i in range(4)},
        waves=[[(i, j), (2 + i, j)] for i in range(2) for j in range(2)],
    )
    sent, gw2 = exchange([b], [sums_b2], carry=gw2)
    gw2 = swap(gw2)

    def back(wo, ctx, q, k, v, log, after):
        return moved_call(
            functools.partial(back_kernel, rows),
            back_outs,
            (gbr, wo, ctx, q, k, v, log, normed),
            back_flops,
            8,
            scratch=back_scratch,
            name="back",
            after=after,
            waves=[[(0, 0), (1, 0)], [(2, 0)]],
        )

    dq, dk, dv, gw, sums_b = back(w_out, ctx, q, k, v, log, sent)
    c = grouped(4 * half, half, ((4, by_x), (3, by_yzzx), (1, by_zyzx)), (gw, 0), (gw2, 0))
    sent = exchange([c, b], [sums_b])

    grad_tokens, sums_one = moved_call(
        functools.partial(input_kernel, rows),
        [shape_of((rows, width), F32), shape_of((3, width), F32)],
        (dq, dk, dv, dq2, dk2, dv2, w_query, w_key, w_value, joined2, tokens, mask, mt, g1, gm),
        12 * rows * width * half,
        2,
        scratch=scratch,
        cuts={9: (1, 3)},
        waves=[[(0, 0), (6, 0)], [(1, 0), (7, 0)], [(2, 0), (8, 0), (3, 0), (9, 0)]],
        name="input",
        after=sent,
    )
    same = [sums_one, sums_two, sum_go, *scale_sums]
    sums = Sums(same, [sums_b, sums_up], [sums_b2, sums_up2], list(natural), [bd, sc2])
    sent = exchange([c, b], [sums_one], sums=sums)
    block_out = moved_call(
        functools.partial(output_kernel, rows, len(hiddens)),
        [shape_of((rows, width))],
        (*hiddens, *downs, middle, bd, sc2),
        8 * tall * width * part,
        1,
        scratch=scratch,
        cuts={0: (1, 2), 1: (1, 2), 2: (0, 2), 3: (0, 2)},
        waves=[[(i, j), (2 + i, j)] for i in range(2) for j in range(2)],
        name="output",
        after=sent,
    )[0]
    last = block_out
    while sums.result is None:
        last = exchange([g for g in (c, b) if g.result is None], [last], sums=sums)[-1]

    done = b.result
    grad_w_down = jnp.concatenate(done[0::2], axis=1).T
    grad_w_up = jnp.concatenate(done[1::2], axis=1)
    grad_w_query, grad_w_key, grad_w_value, grad_w_out = c.result
    (grad_mask_token, grad_gain_one, grad_shift_one, grad_gain_two, grad_shift_two, grad_scale_one, grad_b_out,
     grad_b_down, grad_scale_two, grad_b_query, grad_b_value, grad_b_up) = (
        one.reshape(-1) for one in sums.result
    )
    return (
        block_out,
        grad_tokens,
        grad_mask_token,
        grad_gain_one,
        grad_shift_one,
        grad_w_query,
        grad_w_key,
        grad_w_value,
        grad_b_query,
        grad_b_value,
        grad_w_out.T,
        grad_b_out,
        grad_scale_one,
        grad_gain_two,
        grad_shift_two,
        grad_w_up,
        grad_b_up,
        grad_w_down,
        grad_b_down,
        grad_scale_two,
    )


def solution(mesh):
    placed = (
        P(("dp", "tp"), None),
        P(("dp", "tp")),
        P(("dp", "tp"), None),
        P(),
        P(),
        P(),
        P(None, "tp"),
        P(None, "tp"),
        P(None, "tp"),
        P("tp"),
        P("tp"),
        P("tp", None),
        P(),
        P(),
        P(),
        P(),
        P(None, "tp"),
        P("tp"),
        P("tp", None),
        P(),
        P(),
    )
    fits = mesh.shape["tp"] == 2 and mesh.shape["dp"].bit_count() == 1
    return jax.shard_map(
        local_body if fits else gathered_body,
        mesh=mesh,
        in_specs=placed,
        out_specs=(
            P(("dp", "tp"), None),
            P(("dp", "tp"), None),
            P(),
            P(),
            P(),
            P("dp", "tp"),
            P("dp", "tp"),
            P("dp", "tp"),
            P("tp"),
            P("tp"),
            P("tp", "dp"),
            P(),
            P(),
            P(),
            P(),
            P("dp", "tp"),
            P("tp"),
            P("tp", "dp"),
            P(),
            P(),
        ),
        check_vma=False,
    )
```
